32 devices in a mesh: section: 8 (over z, y), dp: 4 (over x, core).
Axes of the slice: x: 2, y: 2, z: 4, core: 2. Of those that a mesh axis runs over, the one named last changes fastest.
Arguments:
- tokens: bfloat16 [4, 4, 128, 768], P(None, 'dp', 'section'), may hold values from -6 to 6
- lengths: int32 [4, 4, 4], P(None, 'dp'), may hold values from 1 to 96, 128 in all within a row
- cotangent: bfloat16 [4, 4, 128, 768], P(None, 'dp', 'section'), may hold values from -6 to 6
- first_gain: float32 [768], replicated, may hold values from 0.5 to 1.5
- first_shift: float32 [768], replicated, may hold values from -3 to 3
- qkv_weight: bfloat16 [768, 2304], replicated, may hold values from -0.21875 to 0.21875
- qv_bias: float32 [1536], replicated, may hold values from -3 to 3
- out_weight: bfloat16 [768, 768], replicated, may hold values from -0.625 to 0.625
- out_bias: float32 [768], replicated, may hold values from -3 to 3
- second_gain: float32 [768], replicated, may hold values from 0.5 to 1.5
- second_shift: float32 [768], replicated, may hold values from -3 to 3
- expand_weight: bfloat16 [768, 3072], replicated, may hold values from -0.21875 to 0.21875
- expand_bias: float32 [3072], replicated, may hold values from -3 to 3
- contract_weight: bfloat16 [3072, 768], replicated, may hold values from -0.15625 to 0.15625
- contract_bias: float32 [768], replicated, may hold values from -3 to 3
Outputs:
- result_tokens: bfloat16 [4, 4, 128, 768], P(None, 'dp', 'section')
- grad_tokens: float32 [4, 4, 128, 768], P(None, 'dp', 'section')
- grad_first_gain: float32 [768], P('dp')
- grad_first_shift: float32 [768], P('dp')
- grad_qkv_weight: float32 [768, 2304], P('dp')
- grad_qv_bias: float32 [1536], P('dp')
- grad_out_weight: float32 [768, 768], P('dp')
- grad_out_bias: float32 [768], P('dp')
- grad_second_gain: float32 [768], P('dp')
- grad_second_shift: float32 [768], P('dp')
- grad_expand_weight: float32 [768, 3072], P('dp')
- grad_expand_bias: float32 [3072], P('dp')
- grad_contract_weight: float32 [3072, 768], P('dp')
- grad_contract_bias: float32 [768], P('dp')
The draws below stay inside these ranges and needn't reach their ends.
Inputs may be any that keep to these rules, and one draw needn't show every extreme that they name: Each row of 4 lengths sums to 128, and its largest is exactly 96.
All inputs are finite; a program needn't handle non-finite values.
Results may differ from the reference program's by a relative error of at most 0.017.
Values may be sent and summed in bfloat16 or wider, within the bound.
No kernel may reach another device: no remote copies, remote signals or barrier semaphores. Data moves between devices by JAX's collectives and lax.ppermute only.
A program may use at most 384 MiB of HBM per device.

```python
import math
import jax
import jax.numpy as jnp
import numpy as np
from jax import lax

D = 768
HEADS = 12
HEAD_DIM = 64
FF = 3072
TOK_SH = 128
SLOTS = 4
MOST = 96
MB = 4
LAYERS = 8
N_DP = 4


def shard_levels(rng, shape, split, low, top_value):
    def one(axis_at, blocks):
        heights = jax.random.uniform(jax.random.fold_in(jax.random.fold_in(rng, 6), axis_at), (blocks,), jnp.float32, low / len(split), top_value / len(split))
        return jnp.repeat(jnp.exp(heights), shape[axis_at] // blocks).reshape((-1,) + (1,) * (len(shape) - axis_at - 1))

    loudness = one(*split[0])
    for cut in split[1:]:
        loudness = loudness * one(*cut)
    return loudness


def profile(number_of, total, limit, slope):
    weights = [(1 << 20) // math.isqrt(grade ** slope) + 1 for grade in range(2, number_of + 1)]
    surplus, counts = total - limit - (number_of - 1), [1] * (number_of - 1)
    while surplus > 0:
        candidates = [i for i in range(number_of - 1) if counts[i] < limit]
        mass, remaining = sum([weights[i] for i in candidates]), surplus
        for i in candidates:
            extra = min(limit - counts[i], max(1, remaining * weights[i] // mass), surplus)
            counts[i] = counts[i] + extra
            surplus = surplus - extra
    return np.array([limit] + counts)


def uneven_parts(stream_key, amount, total, most, skew):
    if amount == 2:
        one = jax.random.randint(stream_key, (), max(1, total - most), min(most, total - 1) + 1)
        return jnp.stack([one, total - one])
    sizes = jnp.asarray(profile(amount, total, most, skew), jnp.int32)
    pairs = (amount - 1) // 2
    source_of, taker = sizes[1:1 + 2 * pairs:2], sizes[2:2 + 2 * pairs:2]
    slack = jnp.minimum(source_of - 1, most - taker)
    passed = jax.random.randint(jax.random.fold_in(stream_key, 1), (pairs,), 0, 1 << 20) % (slack + 1)
    sizes = sizes.at[1:1 + 2 * pairs:2].set(source_of - passed).at[2:2 + 2 * pairs:2].set(taker + passed)
    return sizes[jax.random.permutation(jax.random.fold_in(stream_key, 2), amount)]


def bell_draw(rng, dims, scale, bound, cuts=(), kind=jnp.bfloat16):
    result = jax.random.normal(rng, dims, jnp.float32) * scale
    if len(cuts) > 0:
        result = shard_levels(rng, dims, cuts, -0.22, 0.18) * result
    return jnp.clip(result, min=-bound, max=bound).astype(kind)


def setup_inputs(seed: int = 0) -> dict:
    keys = jax.random.split(jax.random.key(seed), 16)
    tokens = bell_draw(keys[0], (MB, N_DP, TOK_SH, D), 1.0, 6.0, ((1, 4), (2, 8)))
    lengths = jax.vmap(lambda own: uneven_parts(own, SLOTS, TOK_SH, MOST, 2))(jax.random.split(keys[1], MB * N_DP)).reshape((MB, N_DP, SLOTS)).astype(jnp.int32)
    cotangent = bell_draw(keys[2], (MB, N_DP, TOK_SH, D), 1.0, 6.0, ((1, 4), (2, 8)))
    first_gain = jnp.clip(1.0 + 0.1 * jax.random.normal(keys[3], (D,), jnp.float32), 0.5, 1.5)
    first_shift = bell_draw(keys[4], (D,), 0.3, 3.0, (), jnp.float32)
    qkv_weight = bell_draw(keys[5], (D, 3 * D), D ** -0.5, 0.21875)
    qv_bias = bell_draw(keys[6], (2 * D,), 0.3, 3.0, (), jnp.float32)
    out_weight = bell_draw(keys[7], (D, D), (D // 8) ** -0.5, 0.625)
    out_bias = bell_draw(keys[8], (D,), 0.3, 3.0, (), jnp.float32)
    second_gain = jnp.clip(1.0 + 0.1 * jax.random.normal(keys[9], (D,), jnp.float32), 0.5, 1.5)
    second_shift = bell_draw(keys[10], (D,), 0.3, 3.0, (), jnp.float32)
    expand_weight = bell_draw(keys[11], (D, FF), D ** -0.5, 0.21875)
    expand_bias = bell_draw(keys[12], (FF,), 0.3, 3.0, (), jnp.float32)
    contract_weight = bell_draw(keys[13], (FF, D), (FF // 2) ** -0.5, 0.15625)
    contract_bias = bell_draw(keys[14], (D,), 0.3, 3.0, (), jnp.float32)
    return {"tokens": tokens, "lengths": lengths, "cotangent": cotangent, "first_gain": first_gain, "first_shift": first_shift, "qkv_weight": qkv_weight, "qv_bias": qv_bias, "out_weight": out_weight, "out_bias": out_bias, "second_gain": second_gain, "second_shift": second_shift, "expand_weight": expand_weight, "expand_bias": expand_bias, "contract_weight": contract_weight, "contract_bias": contract_bias}


@jax.custom_vjp
def low(v):
    return lax.optimization_barrier(v.astype(jnp.bfloat16)).astype(jnp.float32)

@jax.custom_vjp
def low_back(v):
    return v

def low_keep(v):
    return (low(v), None)

def low_pass(kept, grad):
    return (grad,)

def back_keep(v):
    return (v, None)

def back_low(kept, grad):
    return (low(grad),)
low.defvjp(low_keep, low_pass)
low_back.defvjp(back_keep, back_low)
EPSILON = 1e-05
SCORE_SCALE = 0.125
MASKED = -1e+30
HIGHEST = lax.Precision.HIGHEST

def layer_norm(values, gain_row, shift_row):
    center = values - lax.optimization_barrier(jnp.mean(values, axis=-1, keepdims=True))
    inverse = lax.rsqrt(lax.optimization_barrier(jnp.mean(center * center, axis=-1, keepdims=True)) + EPSILON)
    return center * inverse * gain_row + shift_row

def product(left_side, right_side):
    return jnp.einsum('rtd,de->rte', left_side, right_side, precision=HIGHEST)

def layer(hidden, allowed, weights):
    first_gain, first_shift, qkv_weight, qv_bias, out_weight, out_bias, second_gain, second_shift, expand_weight, expand_bias, contract_weight, contract_bias = weights
    shard_count, row_count, model_width = hidden.shape
    first_low = low(layer_norm(hidden, first_gain, first_shift))
    full_bias = jnp.concatenate([qv_bias[:model_width], jnp.zeros((model_width,), jnp.float32), qv_bias[model_width:]])
    projected = low_back(low(product(first_low, qkv_weight) + full_bias))
    heads_shape = (shard_count, row_count, HEADS, HEAD_DIM)
    queries = projected[:, :, :model_width].reshape(heads_shape)
    key_rows = projected[:, :, model_width:2 * model_width].reshape(heads_shape)
    value_rows = projected[:, :, 2 * model_width:].reshape(heads_shape)
    raw_scores = jnp.einsum('rqhd,rkhd->rhqk', queries, key_rows, precision=HIGHEST) * SCORE_SCALE
    scores = jnp.where(allowed[:, None], low_back(raw_scores), MASKED)
    highest = lax.optimization_barrier(jnp.max(scores, axis=-1, keepdims=True))
    log_total = highest + jnp.log(lax.optimization_barrier(jnp.sum(jnp.exp(scores - highest), axis=-1, keepdims=True)))
    probs_low = low(jnp.exp(scores - log_total))
    mixed_heads = jnp.einsum('rhqk,rkhd->rqhd', probs_low, value_rows, precision=HIGHEST)
    attended = low_back(low(mixed_heads.reshape(shard_count, row_count, model_width)))
    middle = hidden + low_back(product(attended, out_weight) + out_bias)
    second_low = low(layer_norm(middle, second_gain, second_shift))
    pre_act = low_back(product(second_low, expand_weight) + expand_bias)
    activated = low(jax.nn.gelu(pre_act, approximate=True))
    return middle + low_back(product(activated, contract_weight) + contract_bias)

def reference(tokens, lengths, cotangent, first_gain, first_shift, qkv_weight, qv_bias, out_weight, out_bias, second_gain, second_shift, expand_weight, expand_bias, contract_weight, contract_bias):
    shard_count = MB * N_DP
    inputs = tokens.astype(jnp.float32).reshape(shard_count, TOK_SH, D)
    seq_ends = jnp.cumsum(lengths.reshape(shard_count, SLOTS), axis=-1)
    places = jnp.arange(TOK_SH, dtype=jnp.int32)
    owners = lax.optimization_barrier(jnp.sum((places[None, :, None] >= seq_ends[:, None, :]).astype(jnp.int32), axis=-1))
    allowed = (owners[:, :, None] == owners[:, None, :]) & (places[None, None, :] <= places[None, :, None])
    weights = tuple((member.astype(jnp.float32) for member in (first_gain, first_shift, qkv_weight, qv_bias, out_weight, out_bias, second_gain, second_shift, expand_weight, expand_bias, contract_weight, contract_bias)))

    def forward(layer_inputs, layer_weights):
        hidden = layer_inputs
        for layer_step in range(LAYERS):
            if layer_step > 0:
                hidden = low_back(low(hidden))
            hidden = layer(hidden, allowed, layer_weights)
        return hidden
    outputs, pullback = jax.vjp(forward, inputs, weights)
    grad_inputs, grad_weights = pullback(cotangent.astype(jnp.float32).reshape(shard_count, TOK_SH, D))
    return (outputs.reshape(MB, N_DP, TOK_SH, D).astype(jnp.bfloat16), grad_inputs.reshape(MB, N_DP, TOK_SH, D), grad_weights[0], grad_weights[1], grad_weights[2], grad_weights[3], grad_weights[4], grad_weights[5], grad_weights[6], grad_weights[7], grad_weights[8], grad_weights[9], grad_weights[10], grad_weights[11])
```

```python
from functools import partial

import jax
import jax.numpy as jnp
from jax import lax
from jax.experimental import pallas as pl
from jax.experimental.pallas import tpu as pltpu
from jax.sharding import PartitionSpec as P

HEAD_DIM = 64
EPSILON = 1e-05
SCORE_SCALE = 0.125
MASKED = -1e30
GELU_A = 0.7978845608028654
GELU_B = 0.044715
BF = jnp.bfloat16
F32 = jnp.float32
AXES = ("section", "dp")
VMEM_LIMIT = 60 * 2**20


def nn(left, right):
    return jnp.dot(left, right, preferred_element_type=F32)


def nt(left, right):
    return lax.dot_general(left, right, (((1,), (1,)), ((), ())), preferred_element_type=F32)


def tn(left, right):
    return lax.dot_general(left, right, (((0,), (0,)), ((), ())), preferred_element_type=F32)


def normed_of(values):
    center = values - jnp.mean(values, axis=-1, keepdims=True)
    inverse = lax.rsqrt(jnp.mean(center * center, axis=-1, keepdims=True) + EPSILON)
    return center * inverse, inverse


def norm_back(upstream, normed, inverse, gain_row):
    scaled = upstream * gain_row
    return inverse * (
        scaled
        - jnp.mean(scaled, axis=-1, keepdims=True)
        - normed * jnp.mean(scaled * normed, axis=-1, keepdims=True)
    )


def lane_split(pair):
    lane = lax.broadcasted_iota(jnp.int32, pair.shape, 1)
    zero = jnp.zeros_like(pair)
    return jnp.where(lane < HEAD_DIM, pair, zero), jnp.where(lane < HEAD_DIM, zero, pair)


def forward_kernel(
    ends_ref, x_ref, vec_ref, ebias_ref, qkvb_ref, wq_ref, wo_ref, we_ref, wc_ref,
    first_ref, n1_ref, proj_ref, probs_ref, att_ref, n2_ref, second_ref, slope_ref, act_ref,
    inv_ref, last_ref, h_scr, mask_scr,
):
    step = pl.program_id(0)
    rows, width = h_scr.shape
    pairs = width // 128
    ff = we_ref.shape[1]

    @pl.when(step == 0)
    def _():
        h_scr[...] = x_ref[...].astype(F32)
        query = lax.broadcasted_iota(jnp.int32, (rows, rows), 0)
        key = lax.broadcasted_iota(jnp.int32, (rows, rows), 1)
        own_q = jnp.zeros((rows, rows), jnp.int32)
        own_k = jnp.zeros((rows, rows), jnp.int32)
        for slot in range(ends_ref.shape[0]):
            end = ends_ref[slot]
            own_q += (query >= end).astype(jnp.int32)
            own_k += (key >= end).astype(jnp.int32)
        mask_scr[...] = ((own_q == own_k) & (key <= query)).astype(F32)

    h = h_scr[...]
    n1, inv1 = normed_of(h)
    first_low = (n1 * vec_ref[0:1, :] + vec_ref[1:2, :]).astype(BF)
    first_ref[0] = first_low
    n1_ref[0] = n1.astype(BF)
    proj = (nn(first_low, wq_ref[...]) + qkvb_ref[...]).astype(BF)
    proj_ref[0] = proj
    allowed = jnp.concatenate([mask_scr[...], mask_scr[...]], axis=0) > 0.5
    outs = []
    for p in range(pairs):
        q = proj[:, 128 * p : 128 * (p + 1)]
        k = proj[:, width + 128 * p : width + 128 * (p + 1)]
        v = proj[:, 2 * width + 128 * p : 2 * width + 128 * (p + 1)]
        scores = nt(jnp.concatenate(lane_split(q), axis=0), k) * SCORE_SCALE
        scores = jnp.where(allowed, scores, MASKED)
        highest = jnp.max(scores, axis=-1, keepdims=True)
        weight = jnp.exp(scores - highest)
        low = (weight / jnp.sum(weight, axis=-1, keepdims=True)).astype(BF)
        probs_ref[0, 2 * rows * p : 2 * rows * (p + 1), :] = low
        both = jnp.concatenate([low[:rows], low[rows:]], axis=1)
        outs.append(nn(both, jnp.concatenate(lane_split(v), axis=0)).astype(BF))
    attended = jnp.concatenate(outs, axis=1)
    att_ref[0] = attended
    middle = h + (nn(attended, wo_ref[...]) + vec_ref[2:3, :])
    n2, inv2 = normed_of(middle)
    second_low = (n2 * vec_ref[3:4, :] + vec_ref[4:5, :]).astype(BF)
    second_ref[0] = second_low
    n2_ref[0] = n2.astype(BF)
    inv_ref[0] = jnp.concatenate(
        [jnp.broadcast_to(inv1, (rows, 128)), jnp.broadcast_to(inv2, (rows, 128))], axis=1
    )
    total = middle + vec_ref[5:6, :]
    chunk = 1024
    for j in range(ff // chunk):
        cols = slice(chunk * j, chunk * (j + 1))
        pre = nn(second_low, we_ref[:, cols]) + ebias_ref[:, cols]
        square = pre * pre
        t = jnp.tanh(GELU_A * pre * (1.0 + GELU_B * square))
        half = 0.5 * (1.0 + t)
        act = (pre * half).astype(BF)
        slope = half + 0.5 * GELU_A * pre * (1.0 - t * t) * (1.0 + 3.0 * GELU_B * square)
        slope_ref[0, :, cols] = slope.astype(BF)
        act_ref[0, :, cols] = act
        total = total + nn(act, wc_ref[cols, :])
    low_out = total.astype(BF)
    h_scr[...] = low_out.astype(F32)

    @pl.when(step == pl.num_programs(0) - 1)
    def _():
        last_ref[...] = low_out


def fold(values):
    return jnp.sum(values.reshape(-1, 8, values.shape[-1]), axis=0)


def backward_kernel(
    cot_ref, vec_ref, wqt_ref, wot_ref, wet_ref, wct_ref,
    n1_ref, proj_ref, probs_ref, n2_ref, slope_ref, inv_ref,
    gproj_ref, gattn_ref, gpre_ref, gmlp_ref, gtok_ref, sums_ref,
    g_scr, s768_scr, s2304_scr, s3072_scr,
):
    step = pl.program_id(0)
    rows, width = g_scr.shape
    pairs = width // 128
    ff = wct_ref.shape[1]

    @pl.when(step == 0)
    def _():
        g_scr[...] = cot_ref[...].astype(F32)
        s768_scr[...] = jnp.zeros_like(s768_scr)
        s2304_scr[...] = jnp.zeros_like(s2304_scr)
        s3072_scr[...] = jnp.zeros_like(s3072_scr)

    g = g_scr[...]
    gmlp = g.astype(BF)
    gmlp_ref[0] = gmlp
    gsec = jnp.zeros((rows, width), F32)
    chunk = 1024
    for j in range(ff // chunk):
        cols = slice(chunk * j, chunk * (j + 1))
        gpre = (nn(gmlp, wct_ref[:, cols]) * slope_ref[0, :, cols].astype(F32)).astype(BF)
        gpre_ref[0, :, cols] = gpre
        s3072_scr[:, cols] += fold(gpre.astype(F32))
        gsec = gsec + nn(gpre, wet_ref[cols, :])
    n2 = n2_ref[0].astype(F32)
    gmid = g + norm_back(gsec, n2, inv_ref[0, :, 128:129], vec_ref[3:4, :])
    gattn = gmid.astype(BF)
    gattn_ref[0] = gattn
    gatt = nn(gattn, wot_ref[...]).astype(BF)
    dqs, dks, dvs = [], [], []
    for p in range(pairs):
        q = proj_ref[0, :, 128 * p : 128 * (p + 1)]
        k = proj_ref[0, :, width + 128 * p : width + 128 * (p + 1)]
        v = proj_ref[0, :, 2 * width + 128 * p : 2 * width + 128 * (p + 1)]
        out2 = jnp.concatenate(lane_split(gatt[:, 128 * p : 128 * (p + 1)]), axis=0)
        low = probs_ref[0, 2 * rows * p : 2 * rows * (p + 1), :]
        prob = low.astype(F32)
        gprob = nt(out2, v)
        gscore = prob * (gprob - jnp.sum(prob * gprob, axis=-1, keepdims=True))
        gscore = gscore.astype(BF)
        both = jnp.concatenate([gscore[:rows], gscore[rows:]], axis=1)
        k2 = jnp.concatenate(lane_split(k), axis=0)
        q2 = jnp.concatenate(lane_split(q), axis=0)
        dqs.append((nn(both, k2) * SCORE_SCALE).astype(BF))
        dks.append((tn(gscore, q2) * SCORE_SCALE).astype(BF))
        dvs.append(tn(low, out2).astype(BF))
    gproj = jnp.concatenate(dqs + dks + dvs, axis=1)
    gproj_ref[0] = gproj
    gfirst = nn(gproj, wqt_ref[...])
    n1 = n1_ref[0].astype(F32)
    gin = gmid + norm_back(gfirst, n1, inv_ref[0, :, 0:1], vec_ref[0:1, :])
    s768_scr[0] += fold(gfirst * n1)
    s768_scr[1] += fold(gfirst)
    s768_scr[2] += fold(gattn.astype(F32))
    s768_scr[3] += fold(gsec * n2)
    s768_scr[4] += fold(gsec)
    s768_scr[5] += fold(gmlp.astype(F32))
    s2304_scr[...] += fold(gproj.astype(F32))
    low_out = gin.astype(BF)
    g_scr[...] = low_out.astype(F32)

    @pl.when(step == pl.num_programs(0) - 1)
    def _():
        gtok_ref[...] = low_out
        row = lambda v: jnp.sum(v, axis=0, keepdims=True)
        sums_ref[0:1, 0:width] = row(s768_scr[0])
        sums_ref[1:2, 0:width] = row(s768_scr[1])
        sums_ref[2:3, 0:width] = row(s2304_scr[:, 0:width])
        sums_ref[2:3, width : 2 * width] = row(s2304_scr[:, 2 * width : 3 * width])
        sums_ref[3:4, 0:width] = row(s768_scr[2])
        sums_ref[4:5, 0:width] = row(s768_scr[3])
        sums_ref[5:6, 0:width] = row(s768_scr[4])
        sums_ref[6:7, :] = row(s3072_scr[...])
        sums_ref[7:8, 0:width] = row(s768_scr[5])


def whole_spec(shape):
    zeros = (0,) * len(shape)
    return pl.BlockSpec(shape, lambda i, *_: zeros, pipeline_mode=pl.Buffered(1))


def forward_all(ends, x, vec, ebias, qkvb, wq, wo, we, wc, layers):
    rows, width = x.shape
    ff = we.shape[1]
    pairs = width // 128
    stack = lambda cols, r=rows, t=BF: jax.ShapeDtypeStruct((layers, r, cols), t)
    outs = [
        stack(width), stack(width), stack(3 * width), stack(rows, 2 * rows * pairs), stack(width),
        stack(width), stack(width), stack(ff), stack(ff), stack(256, rows, F32),
    ]
    per_layer = lambda s: pl.BlockSpec((1,) + s.shape[1:], lambda i, *_: (i, 0, 0))
    last = jax.ShapeDtypeStruct((rows, width), BF)
    return pl.pallas_call(
        forward_kernel,
        grid_spec=pltpu.PrefetchScalarGridSpec(
            num_scalar_prefetch=1,
            grid=(layers,),
            in_specs=[whole_spec(a.shape) for a in (x, vec, ebias, qkvb, wq, wo, we, wc)],
            out_specs=[per_layer(s) for s in outs] + [whole_spec(last.shape)],
            scratch_shapes=[pltpu.VMEM((rows, width), F32), pltpu.VMEM((rows, rows), F32)],
        ),
        out_shape=outs + [last],
        compiler_params=pltpu.CompilerParams(vmem_limit_bytes=VMEM_LIMIT),
    )(ends, x, vec, ebias, qkvb, wq, wo, we, wc)


def backward_all(cot, vec, wqt, wot, wet, wct, n1, proj, probs, n2, slope, inv):
    layers, rows, width = n1.shape
    ff = wct.shape[1]
    stack = lambda cols: jax.ShapeDtypeStruct((layers, rows, cols), BF)
    outs = [stack(3 * width), stack(width), stack(ff), stack(width)]
    per_layer = lambda s: pl.BlockSpec((1,) + s.shape[1:], lambda i: (layers - 1 - i, 0, 0))
    last = [jax.ShapeDtypeStruct((rows, width), BF), jax.ShapeDtypeStruct((8, ff), F32)]
    return pl.pallas_call(
        backward_kernel,
        grid=(layers,),
        in_specs=[whole_spec(a.shape) for a in (cot, vec, wqt, wot, wet, wct)]
        + [per_layer(a) for a in (n1, proj, probs, n2, slope, inv)],
        out_specs=[per_layer(s) for s in outs] + [whole_spec(s.shape) for s in last],
        out_shape=outs + last,
        scratch_shapes=[
            pltpu.VMEM((rows, width), F32),
            pltpu.VMEM((6, 8, width), F32),
            pltpu.VMEM((8, 3 * width), F32),
            pltpu.VMEM((8, ff), F32),
        ],
        compiler_params=pltpu.CompilerParams(vmem_limit_bytes=VMEM_LIMIT),
    )(cot, vec, wqt, wot, wet, wct, n1, proj, probs, n2, slope, inv)


def outer_kernel(start_ref, left_ref, right_ref, out_ref):
    out_ref[...] = tn(left_ref[...], right_ref[...]).astype(BF)


def outer(left, right, start, count, tile_m=384, tile_n=768):
    depth, cols = right.shape
    return pl.pallas_call(
        outer_kernel,
        grid_spec=pltpu.PrefetchScalarGridSpec(
            num_scalar_prefetch=1,
            grid=(count, cols // tile_n),
            in_specs=[
                pl.BlockSpec((depth, tile_m), lambda i, j, s: (0, s[0] + i)),
                pl.BlockSpec((depth, tile_n), lambda i, j, s: (0, j)),
            ],
            out_specs=pl.BlockSpec((tile_m, tile_n), lambda i, j, s: (i, j)),
        ),
        out_shape=jax.ShapeDtypeStruct((count * tile_m, cols), BF),
        compiler_params=pltpu.CompilerParams(vmem_limit_bytes=VMEM_LIMIT),
    )(start, left, right)


def xor_order(stacked, flips):
    count = stacked.shape[0]
    rest = stacked.shape[1:]
    bit = 1
    while bit < count:
        split = stacked.reshape((count // (2 * bit), 2, bit) + rest)
        split = jnp.where((flips & bit) != 0, split[:, ::-1], split)
        stacked = split.reshape((count,) + rest)
        bit *= 2
    return stacked


class Places:
    def __init__(self, sections, dps):
        self.sections, self.dps = sections, dps

    def spread(self, k):
        pairs = []
        for i in range(self.sections):
            for d in range(self.dps):
                own_x = (d >> 1) & 1
                label = i ^ k
                target = (label & ~1) | own_x
                to = (d & ~2) | ((label & 1) << 1)
                pairs.append((i * self.dps + d, target * self.dps + to))
        return pairs

    def collect(self, k):
        return [(b, a) for a, b in self.spread(k)]

    def other_core(self):
        return [(d, d ^ 1) for d in range(self.dps)]


def body(
    tokens, lengths, cotangent, first_gain, first_shift, qkv_weight, qv_bias, out_weight, out_bias,
    second_gain, second_shift, expand_weight, expand_bias, contract_weight, contract_bias,
):
    sections, dps = lax.axis_size("section"), lax.axis_size("dp")
    section, dp = lax.axis_index("section"), lax.axis_index("dp")
    micro, _, piece_rows, width = tokens.shape
    rows = piece_rows * sections
    ff = expand_weight.shape[1]
    places = Places(sections, dps)
    core, own_x, high = dp & 1, (dp >> 1) & 1, dp >> 2
    highs = dps // 4

    ends = jnp.cumsum(lengths[:, 0], axis=-1).astype(BF)
    slots = ends.shape[-1]
    ends = jnp.pad(ends, ((0, 0), (0, 128 - slots)))
    ends = jnp.broadcast_to(ends[:, None], (micro, piece_rows, 128))
    sent = jnp.concatenate([tokens[:, 0], cotangent[:, 0], ends], axis=-1)
    got = []
    for k in range(sections):
        block = lax.dynamic_index_in_dim(sent, (section ^ k) >> 1, 0, keepdims=False)
        got.append(lax.ppermute(block, AXES, places.spread(k)))
    label = (section & ~1) | own_x
    shard = xor_order(jnp.stack(got), label).reshape(rows, -1)
    x, cot = shard[:, :width], shard[:, width : 2 * width]
    ends_here = shard[0, 2 * width : 2 * width + slots].astype(jnp.int32)

    vec = jnp.stack(
        [first_gain, first_shift, out_bias, second_gain, second_shift, contract_bias, out_bias, out_bias]
    )
    qkvb = jnp.concatenate([qv_bias[:width], jnp.zeros((width,), F32), qv_bias[width:]])[None]
    first, n1, proj, probs, att, n2, second, slope, act, inv, last = forward_all(
        ends_here, x, vec, expand_bias[None], qkvb,
        qkv_weight, out_weight, expand_weight, contract_weight, sections,
    )
    gproj, gattn, gpre, gmlp, gtok, sums = backward_all(
        cot, vec, qkv_weight.T, out_weight.T, expand_weight.T, contract_weight.T,
        n1, proj, probs, n2, slope, inv,
    )

    flat = lambda a: a.reshape(-1, a.shape[-1])

    def own_half(left, right):
        left, right = flat(left), flat(right)
        cols = left.shape[1]
        if highs == 1:
            count = cols // 768
            start = (own_x * count)[None].astype(jnp.int32)
        else:
            left = left.reshape(-1, highs, 2, 2, cols // dps)
            left = lax.dynamic_index_in_dim(left, own_x, 2, keepdims=False).reshape(-1, cols // 2)
            count, start = cols // 768, jnp.zeros((1,), jnp.int32)
        out = outer(left, right, start, count)
        return out.reshape(highs, 2, cols // dps, right.shape[1])

    def vector_half(row):
        parts = row.reshape(highs, 2, 2, -1)
        return lax.dynamic_index_in_dim(parts, own_x, 1, keepdims=False)

    small_sizes = [width, width, 2 * width, width, width, width, ff, width]
    small = jnp.concatenate(
        [vector_half(sums[i, :n]) for i, n in enumerate(small_sizes)], axis=-1
    ).astype(BF)[:, :, None]
    pieces = [own_half(first, gproj), own_half(att, gattn), own_half(second, gpre), own_half(act, gmlp), small]
    totals = []
    for part in pieces:
        give = lax.dynamic_index_in_dim(part, 1 - core, 1, keepdims=False)
        keep = lax.dynamic_index_in_dim(part, core, 1, keepdims=False)
        part = keep + lax.ppermute(give, "dp", places.other_core())
        if highs > 1:
            groups = [[4 * h + low for h in range(highs)] for low in range(4)]
            part = lax.psum_scatter(part, "dp", scatter_dimension=0, tiled=False, axis_index_groups=groups)
        else:
            part = part[0]
        totals.append(lax.psum(part, "section").astype(F32))
    g_qkv, g_out, g_exp, g_con, g_small = totals
    g_small = g_small[0]
    vectors, at = [], 0
    for n in small_sizes:
        vectors.append(g_small[at : at + n // dps])
        at += n // dps

    both = jnp.concatenate([last, gtok], axis=1).reshape(sections, piece_rows, 2 * width)
    back = []
    for k in range(0, sections, 2):
        block = lax.dynamic_index_in_dim(both, label ^ k, 0, keepdims=False)
        pairs = [p for p in places.collect(k)]
        back.append(lax.ppermute(block, AXES, pairs))
    back = xor_order(jnp.stack(back), section >> 1)
    result = back[:, None, :, :width]
    grad_tokens = back[:, None, :, width:].astype(F32)
    return (
        result, grad_tokens, vectors[0], vectors[1], g_qkv, vectors[2], g_out, vectors[3],
        vectors[4], vectors[5], g_exp, vectors[6], g_con, vectors[7],
    )


def solution(mesh):
    tok = P(None, "dp", "section", None)
    return jax.shard_map(
        body,
        mesh=mesh,
        in_specs=(tok, P(None, "dp", None), tok) + (P(),) * 12,
        out_specs=(
            tok, tok, P("dp"), P("dp"), P("dp", None), P("dp"), P("dp", None), P("dp"),
            P("dp"), P("dp"), P("dp", None), P("dp"), P("dp", None), P("dp"),
        ),
        check_vma=False,
    )
```

```python
from functools import partial

import jax
import jax.numpy as jnp
from jax import lax
from jax.experimental import pallas as pl
from jax.experimental.pallas import tpu as pltpu
from jax.sharding import PartitionSpec as P

HEAD_DIM = 64
EPSILON = 1e-05
SCORE_SCALE = 0.125
MASKED = -1e30
GELU_A = 0.7978845608028654
GELU_B = 0.044715
BF = jnp.bfloat16
F32 = jnp.float32
AXES = ("section", "dp")
VMEM_LIMIT = 60 * 2**20


def nn(left, right):
    return jnp.dot(left, right, preferred_element_type=F32)


def nt(left, right):
    return lax.dot_general(left, right, (((1,), (1,)), ((), ())), preferred_element_type=F32)


def tn(left, right):
    return lax.dot_general(left, right, (((0,), (0,)), ((), ())), preferred_element_type=F32)


def normed_of(values):
    center = values - jnp.mean(values, axis=-1, keepdims=True)
    inverse = lax.rsqrt(jnp.mean(center * center, axis=-1, keepdims=True) + EPSILON)
    return center * inverse, inverse


def norm_back(upstream, normed, inverse, gain_row):
    scaled = upstream * gain_row
    return inverse * (
        scaled
        - jnp.mean(scaled, axis=-1, keepdims=True)
        - normed * jnp.mean(scaled * normed, axis=-1, keepdims=True)
    )


def lane_split(pair):
    lane = lax.broadcasted_iota(jnp.int32, pair.shape, 1)
    zero = jnp.zeros_like(pair)
    return jnp.where(lane < HEAD_DIM, pair, zero), jnp.where(lane < HEAD_DIM, zero, pair)


def forward_kernel(
    ends_ref, x_ref, vec_ref, ebias_ref, qkvb_ref, wq_ref, wo_ref, we_ref, wc_ref,
    first_ref, n1_ref, proj_ref, probs_ref, att_ref, n2_ref, second_ref, slope_ref, act_ref,
    inv_ref, last_ref, h_scr, mask_scr,
):
    step = pl.program_id(0)
    rows, width = h_scr.shape
    pairs = width // 128
    ff = we_ref.shape[1]

    @pl.when(step == 0)
    def _():
        h_scr[...] = x_ref[...].astype(F32)
        query = lax.broadcasted_iota(jnp.int32, (rows, rows), 0)
        key = lax.broadcasted_iota(jnp.int32, (rows, rows), 1)
        own_q = jnp.zeros((rows, rows), jnp.int32)
        own_k = jnp.zeros((rows, rows), jnp.int32)
        for slot in range(ends_ref.shape[0]):
            end = ends_ref[slot]
            own_q += (query >= end).astype(jnp.int32)
            own_k += (key >= end).astype(jnp.int32)
        mask_scr[...] = ((own_q == own_k) & (key <= query)).astype(F32)

    h = h_scr[...]
    n1, inv1 = normed_of(h)
    first_low = (n1 * vec_ref[0:1, :] + vec_ref[1:2, :]).astype(BF)
    first_ref[0] = first_low
    n1_ref[0] = n1.astype(BF)
    proj = (nn(first_low, wq_ref[...]) + qkvb_ref[...]).astype(BF)
    proj_ref[0] = proj
    allowed = jnp.concatenate([mask_scr[...], mask_scr[...]], axis=0) > 0.5
    outs = []
    for p in range(pairs):
        q = proj[:, 128 * p : 128 * (p + 1)]
        k = proj[:, width + 128 * p : width + 128 * (p + 1)]
        v = proj[:, 2 * width + 128 * p : 2 * width + 128 * (p + 1)]
        scores = nt(jnp.concatenate(lane_split(q), axis=0), k) * SCORE_SCALE
        scores = jnp.where(allowed, scores, MASKED)
        highest = jnp.max(scores, axis=-1, keepdims=True)
        weight = jnp.exp(scores - highest)
        low = (weight / jnp.sum(weight, axis=-1, keepdims=True)).astype(BF)
        probs_ref[0, 2 * rows * p : 2 * rows * (p + 1), :] = low
        both = jnp.concatenate([low[:rows], low[rows:]], axis=1)
        outs.append(nn(both, jnp.concatenate(lane_split(v), axis=0)).astype(BF))
    attended = jnp.concatenate(outs, axis=1)
    att_ref[0] = attended
    middle = h + (nn(attended, wo_ref[...]) + vec_ref[2:3, :])
    n2, inv2 = normed_of(middle)
    second_low = (n2 * vec_ref[3:4, :] + vec_ref[4:5, :]).astype(BF)
    second_ref[0] = second_low
    n2_ref[0] = n2.astype(BF)
    inv_ref[0] = jnp.concatenate(
        [jnp.broadcast_to(inv1, (rows, 128)), jnp.broadcast_to(inv2, (rows, 128))], axis=1
    )
    total = middle + vec_ref[5:6, :]
    chunk = 1024
    for j in range(ff // chunk):
        cols = slice(chunk * j, chunk * (j + 1))
        pre = nn(second_low, we_ref[:, cols]) + ebias_ref[:, cols]
        square = pre * pre
        t = jnp.tanh(GELU_A * pre * (1.0 + GELU_B * square))
        half = 0.5 * (1.0 + t)
        act = (pre * half).astype(BF)
        slope = half + 0.5 * GELU_A * pre * (1.0 - t * t) * (1.0 + 3.0 * GELU_B * square)
        slope_ref[0, :, cols] = slope.astype(BF)
        act_ref[0, :, cols] = act
        total = total + nn(act, wc_ref[cols, :])
    low_out = total.astype(BF)
    h_scr[...] = low_out.astype(F32)

    @pl.when(step == pl.num_programs(0) - 1)
    def _():
        last_ref[...] = low_out


def fold(values):
    return jnp.sum(values.reshape(-1, 8, values.shape[-1]), axis=0)


def backward_kernel(
    cot_ref, vec_ref, wqt_ref, wot_ref, wet_ref, wct_ref,
    n1_ref, proj_ref, probs_ref, n2_ref, slope_ref, inv_ref,
    gproj_ref, gattn_ref, gpre_ref, gmlp_ref, gtok_ref, sums_ref,
    g_scr, s768_scr, s2304_scr, s3072_scr,
):
    step = pl.program_id(0)
    rows, width = g_scr.shape
    pairs = width // 128
    ff = wct_ref.shape[1]

    @pl.when(step == 0)
    def _():
        g_scr[...] = cot_ref[...].astype(F32)
        s768_scr[...] = jnp.zeros_like(s768_scr)
        s2304_scr[...] = jnp.zeros_like(s2304_scr)
        s3072_scr[...] = jnp.zeros_like(s3072_scr)

    g = g_scr[...]
    gmlp = g.astype(BF)
    gmlp_ref[0] = gmlp
    gsec = jnp.zeros((rows, width), F32)
    chunk = 1024
    for j in range(ff // chunk):
        cols = slice(chunk * j, chunk * (j + 1))
        gpre = (nn(gmlp, wct_ref[:, cols]) * slope_ref[0, :, cols].astype(F32)).astype(BF)
        gpre_ref[0, :, cols] = gpre
        s3072_scr[:, cols] += fold(gpre.astype(F32))
        gsec = gsec + nn(gpre, wet_ref[cols, :])
    n2 = n2_ref[0].astype(F32)
    gmid = g + norm_back(gsec, n2, inv_ref[0, :, 128:129], vec_ref[3:4, :])
    gattn = gmid.astype(BF)
    gattn_ref[0] = gattn
    gatt = nn(gattn, wot_ref[...]).astype(BF)
    dqs, dks, dvs = [], [], []
    for p in range(pairs):
        q = proj_ref[0, :, 128 * p : 128 * (p + 1)]
        k = proj_ref[0, :, width + 128 * p : width + 128 * (p + 1)]
        v = proj_ref[0, :, 2 * width + 128 * p : 2 * width + 128 * (p + 1)]
        out2 = jnp.concatenate(lane_split(gatt[:, 128 * p : 128 * (p + 1)]), axis=0)
        low = probs_ref[0, 2 * rows * p : 2 * rows * (p + 1), :]
        prob = low.astype(F32)
        gprob = nt(out2, v)
        gscore = prob * (gprob - jnp.sum(prob * gprob, axis=-1, keepdims=True))
        gscore = gscore.astype(BF)
        both = jnp.concatenate([gscore[:rows], gscore[rows:]], axis=1)
        k2 = jnp.concatenate(lane_split(k), axis=0)
        q2 = jnp.concatenate(lane_split(q), axis=0)
        dqs.append((nn(both, k2) * SCORE_SCALE).astype(BF))
        dks.append((tn(gscore, q2) * SCORE_SCALE).astype(BF))
        dvs.append(tn(low, out2).astype(BF))
    gproj = jnp.concatenate(dqs + dks + dvs, axis=1)
    gproj_ref[0] = gproj
    gfirst = nn(gproj, wqt_ref[...])
    n1 = n1_ref[0].astype(F32)
    gin = gmid + norm_back(gfirst, n1, inv_ref[0, :, 0:1], vec_ref[0:1, :])
    s768_scr[0] += fold(gfirst * n1)
    s768_scr[1] += fold(gfirst)
    s768_scr[2] += fold(gattn.astype(F32))
    s768_scr[3] += fold(gsec * n2)
    s768_scr[4] += fold(gsec)
    s768_scr[5] += fold(gmlp.astype(F32))
    s2304_scr[...] += fold(gproj.astype(F32))
    low_out = gin.astype(BF)
    g_scr[...] = low_out.astype(F32)

    @pl.when(step == pl.num_programs(0) - 1)
    def _():
        gtok_ref[...] = low_out
        row = lambda v: jnp.sum(v, axis=0, keepdims=True)
        for i in range(6):
            sums_ref[i : i + 1, 0:width] = row(s768_scr[i])
        sums_ref[6:7, 0:width] = row(s2304_scr[:, 0:width])
        sums_ref[6:7, width : 2 * width] = row(s2304_scr[:, 2 * width : 3 * width])
        sums_ref[7:8, :] = row(s3072_scr[...])


def whole_spec(shape):
    zeros = (0,) * len(shape)
    return pl.BlockSpec(shape, lambda i, *_: zeros, pipeline_mode=pl.Buffered(1))


def forward_all(ends, x, vec, ebias, qkvb, wq, wo, we, wc, layers):
    rows, width = x.shape
    ff = we.shape[1]
    pairs = width // 128
    stack = lambda cols, r=rows, t=BF: jax.ShapeDtypeStruct((layers, r, cols), t)
    outs = [
        stack(width), stack(width), stack(3 * width), stack(rows, 2 * rows * pairs), stack(width),
        stack(width), stack(width), stack(ff), stack(ff), stack(256, rows, F32),
    ]
    per_layer = lambda s: pl.BlockSpec((1,) + s.shape[1:], lambda i, *_: (i, 0, 0))
    last = jax.ShapeDtypeStruct((rows, width), BF)
    return pl.pallas_call(
        forward_kernel,
        grid_spec=pltpu.PrefetchScalarGridSpec(
            num_scalar_prefetch=1,
            grid=(layers,),
            in_specs=[whole_spec(a.shape) for a in (x, vec, ebias, qkvb, wq, wo, we, wc)],
            out_specs=[per_layer(s) for s in outs] + [whole_spec(last.shape)],
            scratch_shapes=[pltpu.VMEM((rows, width), F32), pltpu.VMEM((rows, rows), F32)],
        ),
        out_shape=outs + [last],
        compiler_params=pltpu.CompilerParams(vmem_limit_bytes=VMEM_LIMIT),
    )(ends, x, vec, ebias, qkvb, wq, wo, we, wc)


def backward_all(cot, vec, wqt, wot, wet, wct, n1, proj, probs, n2, slope, inv):
    layers, rows, width = n1.shape
    ff = wct.shape[1]
    stack = lambda cols: jax.ShapeDtypeStruct((layers, rows, cols), BF)
    outs = [stack(3 * width), stack(width), stack(ff), stack(width)]
    per_layer = lambda s: pl.BlockSpec((1,) + s.shape[1:], lambda i: (layers - 1 - i, 0, 0))
    last = [jax.ShapeDtypeStruct((rows, width), BF), jax.ShapeDtypeStruct((8, ff), F32)]
    return pl.pallas_call(
        backward_kernel,
        grid=(layers,),
        in_specs=[whole_spec(a.shape) for a in (cot, vec, wqt, wot, wet, wct)]
        + [per_layer(a) for a in (n1, proj, probs, n2, slope, inv)],
        out_specs=[per_layer(s) for s in outs] + [whole_spec(s.shape) for s in last],
        out_shape=outs + last,
        scratch_shapes=[
            pltpu.VMEM((rows, width), F32),
            pltpu.VMEM((6, 8, width), F32),
            pltpu.VMEM((8, 3 * width), F32),
            pltpu.VMEM((8, ff), F32),
        ],
        compiler_params=pltpu.CompilerParams(vmem_limit_bytes=VMEM_LIMIT),
    )(cot, vec, wqt, wot, wet, wct, n1, proj, probs, n2, slope, inv)


def outer_kernel(spot_ref, left_ref, right_ref, give_ref, keep_ref, scr, *, tall):
    scr[...] = tn(left_ref[...], right_ref[...]).astype(BF)
    split_out(spot_ref, scr, give_ref, keep_ref, 0, scr.shape[1], tall)


def split_out(spot_ref, scr, give_ref, keep_ref, at, cols, tall):
    x, c, y = spot_ref[0], spot_ref[1], spot_ref[2]
    for crel in (1, 0):
        out = give_ref if crel else keep_ref
        for xrel in (0, 1):
            for yrel in (0, 1):
                part = ((x ^ xrel) * 2 + (c ^ crel)) * 2 + (y ^ yrel)
                start = pl.multiple_of(part * tall, tall)
                out[xrel, yrel, 0:tall, at : at + cols] = scr[pl.ds(start, tall), :]


def parts_of(rows, cols):
    return jax.ShapeDtypeStruct((2, 2, rows, cols), BF)


def expand_grads(spot, left, right, tile=768):
    depth, width = left.shape
    half = right.shape[1] // 2
    steps = half // tile
    out = parts_of(width // 8, half)
    out_spec = pl.BlockSpec((2, 2, width // 8, tile), lambda j, s: (0, 0, 0, j))
    return pl.pallas_call(
        partial(outer_kernel, tall=width // 8),
        grid_spec=pltpu.PrefetchScalarGridSpec(
            num_scalar_prefetch=1,
            grid=(steps,),
            in_specs=[
                pl.BlockSpec((depth, width), lambda j, s: (0, 0)),
                pl.BlockSpec((depth, tile), lambda j, s: (0, s[3] * steps + j)),
            ],
            out_specs=[out_spec, out_spec],
            scratch_shapes=[pltpu.VMEM((width, tile), BF)],
        ),
        out_shape=[out, out],
        cost_estimate=cost_of(depth, width, half),
        compiler_params=pltpu.CompilerParams(vmem_limit_bytes=VMEM_LIMIT),
    )(spot, left, right)


def cost_of(depth, rows, cols):
    return pl.CostEstimate(
        flops=2 * depth * rows * cols, transcendentals=0, bytes_accessed=2 * depth * (rows + cols) + 2 * rows * cols
    )


def contract_kernel(spot_ref, left_ref, right_ref, give_ref, keep_ref, scr):
    step = pl.program_id(0)
    y = spot_ref[2]
    tall = scr.shape[0] // 2
    scr[...] = tn(left_ref[...], right_ref[...]).astype(BF)
    for yrel in (0, 1):
        start = pl.multiple_of((y ^ yrel) * tall, tall)

        @pl.when(step < 2)
        def _():
            give_ref[0, yrel] = scr[pl.ds(start, tall), :]

        @pl.when(step >= 2)
        def _():
            keep_ref[0, yrel] = scr[pl.ds(start, tall), :]


def contract_grads(spot, left, right):
    depth, ff = left.shape
    width = right.shape[1]
    tall = ff // 8

    def column(i, s):
        return (0, (((i & 1) ^ s[0]) * 2 + ((1 - (i >> 1)) ^ s[1])) * 2 + s[3])

    out = parts_of(tall // 2, width)
    return pl.pallas_call(
        contract_kernel,
        grid_spec=pltpu.PrefetchScalarGridSpec(
            num_scalar_prefetch=1,
            grid=(4,),
            in_specs=[
                pl.BlockSpec((depth, tall), column),
                pl.BlockSpec((depth, width), lambda i, s: (0, 0)),
            ],
            out_specs=[
                pl.BlockSpec((1, 2, tall // 2, width), lambda i, s: (jnp.minimum(i, 1), 0, 0, 0)),
                pl.BlockSpec((1, 2, tall // 2, width), lambda i, s: (jnp.maximum(i - 2, 0), 0, 0, 0)),
            ],
            scratch_shapes=[pltpu.VMEM((tall, width), BF)],
        ),
        out_shape=[out, out],
        cost_estimate=cost_of(depth, ff // 2, width),
        compiler_params=pltpu.CompilerParams(vmem_limit_bytes=VMEM_LIMIT),
    )(spot, left, right)


def attention_kernel(
    spot_ref, first_ref, gproj_ref, att_ref, gattn_ref, sums_ref, give_ref, keep_ref, qkv_scr, out_scr,
):
    tall = qkv_scr.shape[0] // 8
    wide = qkv_scr.shape[1]
    qkv_scr[...] = tn(first_ref[...], gproj_ref[...]).astype(BF)
    split_out(spot_ref, qkv_scr, give_ref, keep_ref, 0, wide, tall)
    out_scr[...] = tn(att_ref[...], gattn_ref[...]).astype(BF)
    split_out(spot_ref, out_scr, give_ref, keep_ref, wide, out_scr.shape[1], tall)
    x, c = spot_ref[0], spot_ref[1]
    width, cols = qkv_scr.shape[0], give_ref.shape[3]
    for crel, out in ((1, give_ref), (0, keep_ref)):
        for xrel in (0, 1):
            place = (x ^ xrel) * 2 + (c ^ crel)
            window = lambda i, start, size: sums_ref[i : i + 1, pl.ds(pl.multiple_of(start, 128), size)]
            low = ((place * 3) >> 1) * 128
            singles = [window(i, low, 256) for i in range(6)]
            doubles = [window(6, place * (width // 2), width // 2), window(7, place * width, width)]
            used = (width // 2) * 3
            doubles.append(jnp.zeros((1, cols - used), F32))
            block = jnp.concatenate(
                [
                    jnp.concatenate(singles, axis=1),
                    jnp.concatenate(doubles, axis=1),
                    jnp.zeros((14, cols), F32),
                ],
                axis=0,
            ).astype(BF)
            for yrel in (0, 1):
                out[xrel, yrel, tall : tall + 16, :] = block


def attention_grads(spot, first, gproj, att, gattn, sums):
    depth, width = first.shape
    wide, thin = gproj.shape[1] // 2, gattn.shape[1] // 2
    out = parts_of(width // 8 + 16, wide + thin)
    whole = lambda shape: pl.BlockSpec(shape, lambda i, s: (0,) * len(shape))
    half = lambda cols: pl.BlockSpec((depth, cols), lambda i, s: (0, s[3]))
    return pl.pallas_call(
        attention_kernel,
        grid_spec=pltpu.PrefetchScalarGridSpec(
            num_scalar_prefetch=1,
            grid=(1,),
            in_specs=[
                whole(first.shape), half(wide), whole(att.shape), half(thin), whole(sums.shape),
            ],
            out_specs=[whole(out.shape), whole(out.shape)],
            scratch_shapes=[pltpu.VMEM((width, wide), BF), pltpu.VMEM((width, thin), BF)],
        ),
        out_shape=[out, out],
        cost_estimate=cost_of(depth, width, wide + thin),
        compiler_params=pltpu.CompilerParams(vmem_limit_bytes=VMEM_LIMIT),
    )(spot, first, gproj, att, gattn, sums)


def xor_order(stacked, flips):
    count = stacked.shape[0]
    rest = stacked.shape[1:]
    bit = 1
    while bit < count:
        split = stacked.reshape((count // (2 * bit), 2, bit) + rest)
        split = jnp.where((flips & bit) != 0, split[:, ::-1], split)
        stacked = split.reshape((count,) + rest)
        bit *= 2
    return stacked


def label_of(section):
    return (section & ~3) | ((section & 1) << 1) | ((section >> 1) & 1)


def by_label(k, sections):
    return [(s, label_of(label_of(s) ^ k)) for s in range(sections)]


def move(array, flip_x, flip_y, flip_z, sections, dps):
    flip = flip_z * 2 + flip_y
    pairs = [
        (s * dps + d, (s ^ flip) * dps + (d ^ (flip_x * 2))) for s in range(sections) for d in range(dps)
    ]
    return lax.ppermute(array, AXES, pairs)


def over_core(give, keep, dps):
    return keep + lax.ppermute(give, "dp", [(d, d ^ 1) for d in range(dps)])


def plane_parts(both, hop):
    return hop(both[1, 0], 1, 0, 0), hop(both[0, 1], 0, 1, 0), hop(both[1, 1], 1, 1, 0)


def plane_sum(both, parts):
    return (both[0, 0].astype(F32) + parts[0] + parts[1] + parts[2]).astype(BF)


def all_parts(total, hop):
    return total, hop(total, 0, 1, 0), hop(total, 0, 0, 1), hop(total, 0, 1, 1)


def in_order(pieces, y, r):
    own, other_y, other_r, other_both = (p.astype(F32) for p in pieces)
    low = jnp.where(y == 0, own, other_y), jnp.where(y == 0, other_y, own)
    high = jnp.where(y == 0, other_r, other_both), jnp.where(y == 0, other_both, other_r)
    pick = lambda a, b: jnp.where(r == 0, a, b)
    return (
        (pick(low[0], high[0]), pick(low[1], high[1])),
        (pick(high[0], low[0]), pick(high[1], low[1])),
    )


def body(
    tokens, lengths, cotangent, first_gain, first_shift, qkv_weight, qv_bias, out_weight, out_bias,
    second_gain, second_shift, expand_weight, expand_bias, contract_weight, contract_bias,
):
    sections, dps = lax.axis_size("section"), lax.axis_size("dp")
    section, dp = lax.axis_index("section"), lax.axis_index("dp")
    micro, _, piece_rows, width = tokens.shape
    rows = piece_rows * sections
    ff = expand_weight.shape[1]
    label = label_of(section)

    sent = jnp.concatenate([tokens[:, 0], cotangent[:, 0]], axis=-1)
    got = []
    for k in range(sections):
        block = lax.dynamic_index_in_dim(sent, (label ^ k) >> 1, 0, keepdims=False)
        got.append(block if k == 0 else lax.ppermute(block, "section", by_label(k, sections)))
    shard = xor_order(jnp.stack(got), label)
    shard = shard.reshape(sections // 4, 2, 2, piece_rows, 2 * width).swapaxes(1, 2).reshape(rows, 2 * width)
    x, cot = shard[:, :width], shard[:, width:]
    ends = jnp.cumsum(lax.dynamic_index_in_dim(lengths, label >> 1, 0, keepdims=False)[0])

    vec = jnp.stack(
        [first_gain, first_shift, out_bias, second_gain, second_shift, contract_bias, out_bias, out_bias]
    )
    qkvb = jnp.concatenate([qv_bias[:width], jnp.zeros((width,), F32), qv_bias[width:]])[None]
    first, n1, proj, probs, att, n2, second, slope, act, inv, last = forward_all(
        ends, x, vec, expand_bias[None], qkvb,
        qkv_weight, out_weight, expand_weight, contract_weight, sections,
    )
    gproj, gattn, gpre, gmlp, gtok, sums = backward_all(
        cot, vec, qkv_weight.T, out_weight.T, expand_weight.T, contract_weight.T,
        n1, proj, probs, n2, slope, inv,
    )

    flat = lambda a: a.reshape(-1, a.shape[-1])
    first, att, second, act = flat(first), flat(att), flat(second), flat(act)
    gproj, gattn, gpre, gmlp = flat(gproj), flat(gattn), flat(gpre), flat(gmlp)
    both = jnp.concatenate([last, gtok], axis=1).reshape(sections, piece_rows, 2 * width)
    blocks = [
        lax.dynamic_index_in_dim(both, label_of(label ^ k), 0, keepdims=False) for k in range(0, sections, 2)
    ]
    if (sections, dps) == (8, 4):
        g_qkv, g_out, g_exp, g_con, v, back = grads_small_slice(
            section, dp, first, att, second, act, gproj, gattn, gpre, gmlp, sums, blocks
        )
    else:
        half = (label & 1) == 0

        def everywhere(whole):
            whole = jnp.where(half, whole, 0.0).astype(BF)
            own = lax.psum_scatter(whole, "dp", scatter_dimension=0, tiled=True)
            return lax.psum(own, "section").astype(F32)

        g_qkv, g_out = everywhere(tn(first, gproj)), everywhere(tn(att, gattn))
        g_exp, g_con = everywhere(tn(second, gpre)), everywhere(tn(act, gmlp))
        v = [everywhere(sums[i, :n]) for i, n in enumerate([width] * 6 + [2 * width, ff])]
        back = blocks[:1] + [
            lax.ppermute(block, "section", by_label(2 * i + 2, sections)) for i, block in enumerate(blocks[1:])
        ]

    back = xor_order(jnp.stack(back), label >> 1)
    result = back[:, None, :, :width]
    grad_tokens = back[:, None, :, width:].astype(F32)
    return (
        result, grad_tokens, v[0], v[1], g_qkv, v[6], g_out, v[2], v[3], v[4], g_exp, v[7], g_con, v[5],
    )


def grads_small_slice(section, dp, first, att, second, act, gproj, gattn, gpre, gmlp, sums, blocks):
    sections, dps = 8, 4
    y, r, x, core = section & 1, (section >> 1) & 1, dp >> 1, dp & 1
    spot = jnp.stack([x, core, y, r]).astype(jnp.int32)
    width, ff = first.shape[1], act.shape[1]
    hop = partial(move, sections=sections, dps=dps)
    cols = 2 * width
    tall = width // 8
    tie = lax.optimization_barrier
    add_a = over_core(*contract_grads(spot, act, gmlp), dps)
    second, gpre, add_a = tie((second, gpre, add_a))
    from_a, out_b = plane_parts(add_a, hop), expand_grads(spot, second, gpre)
    from_a, out_b = tie((from_a, out_b))
    plane_a = plane_sum(add_a, from_a)
    z_a, add_b = hop(plane_a, 0, 0, 2), over_core(*out_b, dps)
    first, gproj, att, gattn, add_b = tie((first, gproj, att, gattn, add_b))
    from_b, out_c = plane_parts(add_b, hop), attention_grads(spot, first, gproj, att, gattn, sums)
    from_b, out_c, z_a = tie((from_b, out_c, z_a))
    plane_b, total_a = plane_sum(add_b, from_b), plane_a + z_a
    z_b = hop(jnp.concatenate([plane_b, blocks[2], blocks[3]], axis=0), 0, 0, 2)
    y_a, add_c = hop(total_a, 0, 1, 0), over_core(*out_c, dps)
    from_c = plane_parts(add_c, hop)
    from_c, z_b, y_a = tie((from_c, z_b, y_a))
    pieces = z_b.shape[0] - tall
    z_b, from_z, through_z = z_b[:tall], z_b[tall : tall + pieces // 2], z_b[tall + pieces // 2 :]
    plane_c, total_b = plane_sum(add_c, from_c), plane_b + z_b
    z_c = hop(plane_c, 0, 0, 2)
    y_b = hop(jnp.concatenate([total_b, blocks[1], through_z], axis=0), 0, 1, 0)
    far_a = hop(jnp.stack([total_a, y_a]), 0, 0, 1)
    z_c, y_b, far_a = tie((z_c, y_b, far_a))
    y_b, from_y, from_both = y_b[:tall], y_b[tall : tall + pieces // 2], y_b[tall + pieces // 2 :]
    back = [blocks[0], from_y, from_z, from_both]
    total_c = plane_c + z_c
    rest = all_parts(total_c, hop)
    far_b = hop(jnp.stack([total_b, y_b]), 0, 0, 1)
    con, exp = (total_a, y_a, far_a[0], far_a[1]), (total_b, y_b, far_b[0], far_b[1])
    con, exp, att_part = in_order(con, y, r), in_order(exp, y, r), in_order([p[:tall] for p in rest], y, r)
    g_con = jnp.concatenate([con[0][0], con[0][1], con[1][0], con[1][1]], axis=0)
    g_exp = jnp.concatenate([jnp.concatenate([exp[0][j], exp[1][j]], axis=1) for j in (0, 1)], axis=0)
    wide = gproj.shape[1] // 2
    side = lambda a, b: jnp.concatenate(
        [jnp.concatenate([att_part[0][j][:, a:b], att_part[1][j][:, a:b]], axis=1) for j in (0, 1)], axis=0
    )
    vectors = rest[0][tall:].astype(F32)
    windows = vectors[0].reshape(6, -1)
    quarter = width // 4
    windows = jnp.where(core == 0, windows[:, :quarter], windows[:, 64 : 64 + quarter])
    v = [windows[i] for i in range(6)] + [vectors[1, : 2 * quarter], vectors[1, 2 * quarter : 2 * quarter + ff // 4]]
    return side(0, wide), side(wide, cols), g_exp, g_con, v, back


def solution(mesh):
    tok = P(None, "dp", "section", None)
    return jax.shard_map(
        body,
        mesh=mesh,
        in_specs=(tok, P(None, "dp", None), tok) + (P(),) * 12,
        out_specs=(
            tok, tok, P("dp"), P("dp"), P("dp", None), P("dp"), P("dp", None), P("dp"),
            P("dp"), P("dp"), P("dp", None), P("dp"), P("dp", None), P("dp"),
        ),
        check_vma=False,
    )
```

```python
from functools import partial

import jax
import jax.numpy as jnp
from jax import lax
from jax.experimental import pallas as pl
from jax.experimental.pallas import tpu as pltpu
from jax.sharding import PartitionSpec as P

HEAD_DIM = 64
EPSILON = 1e-05
SCORE_SCALE = 0.125
MASKED = -1e30
GELU_A = 0.7978845608028654
GELU_B = 0.044715
BF = jnp.bfloat16
F32 = jnp.float32
AXES = ("section", "dp")
VMEM_LIMIT = 60 * 2**20


def nn(left, right):
    return jnp.dot(left, right, preferred_element_type=F32)


def nt(left, right):
    return lax.dot_general(left, right, (((1,), (1,)), ((), ())), preferred_element_type=F32)


def tn(left, right):
    return lax.dot_general(left, right, (((0,), (0,)), ((), ())), preferred_element_type=F32)


def normed_of(values):
    center = values - jnp.mean(values, axis=-1, keepdims=True)
    inverse = lax.rsqrt(jnp.mean(center * center, axis=-1, keepdims=True) + EPSILON)
    return center * inverse, inverse


def norm_back(upstream, normed, inverse, gain_row):
    scaled = upstream * gain_row
    return inverse * (
        scaled
        - jnp.mean(scaled, axis=-1, keepdims=True)
        - normed * jnp.mean(scaled * normed, axis=-1, keepdims=True)
    )


def row_of(ref):
    return ref[...].reshape(1, -1)


def lane_split(pair):
    lane = lax.broadcasted_iota(jnp.int32, pair.shape, 1)
    zero = jnp.zeros_like(pair)
    return jnp.where(lane < HEAD_DIM, pair, zero), jnp.where(lane < HEAD_DIM, zero, pair)


def forward_kernel(
    lens_ref, spot_ref, x_ref, g1_ref, b1_ref, qvb_ref, obias_ref, g2_ref, b2_ref, ebias_ref, cbias_ref,
    wq_hbm, wo_hbm, we_hbm, wc_hbm,
    first_ref, n1_ref, proj_ref, probs_ref, att_ref, n2_ref, second_ref, slope_ref, act_ref,
    inv_ref, wqot_ref, wet_ref, wct_ref, last_ref, h_scr, mask_scr, wqo_scr, we_ref, wc_ref, sems,
):
    step = pl.program_id(0)
    rows, width = h_scr.shape
    pairs = width // 128
    ff = we_ref.shape[1]
    loads = [
        pltpu.make_async_copy(wq_hbm, wqo_scr.at[:, 0 : 3 * width], sems.at[0]),
        pltpu.make_async_copy(wo_hbm, wqo_scr.at[:, 3 * width : 4 * width], sems.at[1]),
        pltpu.make_async_copy(we_hbm, we_ref, sems.at[2]),
        pltpu.make_async_copy(wc_hbm, wc_ref, sems.at[3]),
    ]

    @pl.when(step == 0)
    def _():
        for load in loads:
            load.start()
        h_scr[...] = x_ref[...].astype(F32)
        query = lax.broadcasted_iota(jnp.int32, (rows, rows), 0)
        key = lax.broadcasted_iota(jnp.int32, (rows, rows), 1)
        own_q = jnp.zeros((rows, rows), jnp.int32)
        own_k = jnp.zeros((rows, rows), jnp.int32)
        slots = lens_ref.shape[1]
        end = jnp.int32(0)
        for slot in range(slots):
            end = end + lens_ref[spot_ref[4], slot]
            own_q += (query >= end).astype(jnp.int32)
            own_k += (key >= end).astype(jnp.int32)
        mask_scr[...] = jnp.where((own_q == own_k) & (key <= query), 0.0, MASKED)
        loads[0].wait()
        loads[1].wait()

    strip = wqot_ref.shape[0]
    at = pl.multiple_of(jnp.minimum(step, 4 * width // strip - 1) * strip, 128)
    wqot_ref[...] = wqo_scr[:, pl.ds(at, strip)].T
    h = h_scr[...]
    n1, inv1 = normed_of(h)
    first_low = (n1 * row_of(g1_ref) + row_of(b1_ref)).astype(BF)
    first_ref[0] = first_low
    n1_ref[0] = n1.astype(BF)
    raw = nn(first_low, wqo_scr[:, 0 : 3 * width])
    queries = ((raw[:, :width] + row_of(qvb_ref)[:, :width]) * SCORE_SCALE).astype(BF)
    keys = raw[:, width : 2 * width].astype(BF)
    values = (raw[:, 2 * width :] + row_of(qvb_ref)[:, width:]).astype(BF)
    proj_ref[0, :, 0:width] = queries
    proj_ref[0, :, width : 2 * width] = keys
    proj_ref[0, :, 2 * width : 3 * width] = values
    mask = mask_scr[...]
    mask = jnp.concatenate([mask, mask], axis=0)
    outs = []
    for p in range(pairs):
        cut = slice(128 * p, 128 * (p + 1))
        scores = nt(jnp.concatenate(lane_split(queries[:, cut]), axis=0), keys[:, cut]) + mask
        highest = jnp.max(scores, axis=-1, keepdims=True)
        weight = jnp.exp(scores - highest)
        low = (weight * (1.0 / jnp.sum(weight, axis=-1, keepdims=True))).astype(BF)
        probs_ref[0, 2 * rows * p : 2 * rows * (p + 1), :] = low
        both = jnp.concatenate([low[:rows], low[rows:]], axis=1)
        outs.append(nn(both, jnp.concatenate(lane_split(values[:, cut]), axis=0)).astype(BF))
    attended = jnp.concatenate(outs, axis=1)
    att_ref[0] = attended
    middle = h + (nn(attended, wqo_scr[:, 3 * width : 4 * width]) + row_of(obias_ref))
    n2, inv2 = normed_of(middle)
    second_low = (n2 * row_of(g2_ref) + row_of(b2_ref)).astype(BF)
    second_ref[0] = second_low
    n2_ref[0] = n2.astype(BF)
    inv_ref[0] = jnp.concatenate(
        [jnp.broadcast_to(inv1, (rows, 128)), jnp.broadcast_to(inv2, (rows, 128))], axis=1
    )
    total = middle + row_of(cbias_ref)

    @pl.when(step == 0)
    def _():
        loads[2].wait()
        loads[3].wait()

    wet_ref[...] = we_ref[:, pl.ds(at, strip)].T
    wct_ref[...] = wc_ref[pl.ds(at, strip), :].T
    ebias = row_of(ebias_ref)
    chunk = 1024
    for j in range(ff // chunk):
        cols = slice(chunk * j, chunk * (j + 1))
        pre = nn(second_low, we_ref[:, cols]) + ebias[:, cols]
        square = pre * pre
        half = 0.5 + 0.5 * jnp.tanh(pre * (GELU_A + GELU_A * GELU_B * square))
        act = pre * half
        slope = half + act * (1.0 - half) * (2.0 * GELU_A + 6.0 * GELU_A * GELU_B * square)
        act = act.astype(BF)
        slope_ref[0, :, cols] = slope.astype(BF)
        act_ref[0, :, cols] = act
        total = total + nn(act, wc_ref[cols, :])
    low_out = total.astype(BF)
    h_scr[...] = low_out.astype(F32)

    @pl.when(step == pl.num_programs(0) - 1)
    def _():
        last_ref[...] = low_out


def fold(values):
    return jnp.sum(values.reshape(-1, 8, values.shape[-1]), axis=0)


def backward_kernel(
    cot_ref, g1_ref, g2_ref, wqot_hbm, wet_hbm, wct_hbm,
    n1_ref, proj_ref, probs_ref, n2_ref, slope_ref, inv_ref,
    gproj_ref, gattn_ref, gpre_ref, gmlp_ref, gtok_ref, sums_ref,
    g_scr, s768_scr, s2304_scr, s3072_scr, wqot_ref, wet_ref, wct_ref, sems,
):
    step = pl.program_id(0)
    rows, width = g_scr.shape
    pairs = width // 128
    ff = wct_ref.shape[1]

    loads = [
        pltpu.make_async_copy(wct_hbm, wct_ref, sems.at[0]),
        pltpu.make_async_copy(wet_hbm, wet_ref, sems.at[1]),
        pltpu.make_async_copy(wqot_hbm, wqot_ref, sems.at[2]),
    ]

    @pl.when(step == 0)
    def _():
        for load in loads:
            load.start()
        g_scr[...] = cot_ref[...].astype(F32)
        s768_scr[...] = jnp.zeros_like(s768_scr)
        s2304_scr[...] = jnp.zeros_like(s2304_scr)
        s3072_scr[...] = jnp.zeros_like(s3072_scr)
        loads[0].wait()
        loads[1].wait()

    g = g_scr[...]
    gmlp = g.astype(BF)
    gmlp_ref[0] = gmlp
    gsec = jnp.zeros((rows, width), F32)
    chunk = 1024
    for j in range(ff // chunk):
        cols = slice(chunk * j, chunk * (j + 1))
        gpre = (nn(gmlp, wct_ref[:, cols]) * slope_ref[0, :, cols].astype(F32)).astype(BF)
        gpre_ref[0, :, cols] = gpre
        s3072_scr[:, cols] += fold(gpre.astype(F32))
        gsec = gsec + nn(gpre, wet_ref[cols, :])
    n2 = n2_ref[0].astype(F32)
    gmid = g + norm_back(gsec, n2, inv_ref[0, :, 128:129], row_of(g2_ref))
    gattn = gmid.astype(BF)
    gattn_ref[0] = gattn

    @pl.when(step == 0)
    def _():
        loads[2].wait()

    gatt = nn(gattn, wqot_ref[3 * width : 4 * width, :]).astype(BF)
    dqs, dks, dvs = [], [], []
    for p in range(pairs):
        q = proj_ref[0, :, 128 * p : 128 * (p + 1)]
        k = proj_ref[0, :, width + 128 * p : width + 128 * (p + 1)]
        v = proj_ref[0, :, 2 * width + 128 * p : 2 * width + 128 * (p + 1)]
        out2 = jnp.concatenate(lane_split(gatt[:, 128 * p : 128 * (p + 1)]), axis=0)
        low = probs_ref[0, 2 * rows * p : 2 * rows * (p + 1), :]
        prob = low.astype(F32)
        gprob = nt(out2, v)
        gscore = prob * (gprob - jnp.sum(prob * gprob, axis=-1, keepdims=True))
        gscore = gscore.astype(BF)
        both = jnp.concatenate([gscore[:rows], gscore[rows:]], axis=1)
        k2 = jnp.concatenate(lane_split(k), axis=0)
        q2 = jnp.concatenate(lane_split(q), axis=0)
        dqs.append((nn(both, k2) * SCORE_SCALE).astype(BF))
        dks.append(tn(gscore, q2).astype(BF))
        dvs.append(tn(low, out2).astype(BF))
    gproj = jnp.concatenate(dqs + dks + dvs, axis=1)
    gproj_ref[0] = gproj
    gfirst = nn(gproj, wqot_ref[0 : 3 * width, :])
    n1 = n1_ref[0].astype(F32)
    gin = gmid + norm_back(gfirst, n1, inv_ref[0, :, 0:1], row_of(g1_ref))
    s768_scr[0] += fold(gfirst * n1)
    s768_scr[1] += fold(gfirst)
    s768_scr[2] += fold(gattn.astype(F32))
    s768_scr[3] += fold(gsec * n2)
    s768_scr[4] += fold(gsec)
    s768_scr[5] += fold(gmlp.astype(F32))
    s2304_scr[...] += fold(gproj.astype(F32))
    low_out = gin.astype(BF)
    g_scr[...] = low_out.astype(F32)

    @pl.when(step == pl.num_programs(0) - 1)
    def _():
        gtok_ref[...] = low_out
        row = lambda v: jnp.sum(v, axis=0, keepdims=True)
        for i in range(6):
            sums_ref[i : i + 1, 0:width] = row(s768_scr[i])
        sums_ref[6:7, 0:width] = row(s2304_scr[:, 0:width])
        sums_ref[6:7, width : 2 * width] = row(s2304_scr[:, 2 * width : 3 * width])
        sums_ref[7:8, :] = row(s3072_scr[...])


def whole_spec(shape):
    zeros = (0,) * len(shape)
    return pl.BlockSpec(shape, lambda i, *_: zeros, pipeline_mode=pl.Buffered(1))


def forward_all(lens, spot, x, rows_in, wq, wo, we, wc, layers):
    rows, width = x.shape
    ff = we.shape[1]
    pairs = width // 128
    strip = ff // 8
    stack = lambda cols, r=rows, t=BF: jax.ShapeDtypeStruct((layers, r, cols), t)
    outs = [
        stack(width), stack(width), stack(3 * width), stack(rows, 2 * rows * pairs), stack(width),
        stack(width), stack(width), stack(ff), stack(ff), stack(256, rows, F32),
    ]
    per_layer = lambda s: pl.BlockSpec((1,) + s.shape[1:], lambda i, *_: (i, 0, 0))
    turned = [jax.ShapeDtypeStruct(s, BF) for s in ((4 * width, width), (ff, width), (width, ff))]
    by_rows = pl.BlockSpec((strip, width), lambda i, *_: (jnp.minimum(i, 7), 0))
    by_cols = pl.BlockSpec((width, strip), lambda i, *_: (0, jnp.minimum(i, 7)))
    last = jax.ShapeDtypeStruct((rows, width), BF)
    return pl.pallas_call(
        forward_kernel,
        grid_spec=pltpu.PrefetchScalarGridSpec(
            num_scalar_prefetch=2,
            grid=(layers,),
            in_specs=[whole_spec(a.shape) for a in (x, *rows_in)]
            + [pl.BlockSpec(memory_space=pl.ANY)] * 4,
            out_specs=[per_layer(s) for s in outs] + [by_rows, by_rows, by_cols, whole_spec(last.shape)],
            scratch_shapes=[
                pltpu.VMEM((rows, width), F32),
                pltpu.VMEM((rows, rows), F32),
                pltpu.VMEM((width, 4 * width), BF),
                pltpu.VMEM((width, ff), BF),
                pltpu.VMEM((ff, width), BF),
                pltpu.SemaphoreType.DMA((4,)),
            ],
        ),
        out_shape=outs + turned + [last],
        compiler_params=pltpu.CompilerParams(vmem_limit_bytes=VMEM_LIMIT),
    )(lens, spot, x, *rows_in, wq, wo, we, wc)


def backward_all(cot, g1, g2, wqot, wet, wct, n1, proj, probs, n2, slope, inv):
    layers, rows, width = n1.shape
    ff = wct.shape[1]
    stack = lambda cols: jax.ShapeDtypeStruct((layers, rows, cols), BF)
    outs = [stack(3 * width), stack(width), stack(ff), stack(width)]
    per_layer = lambda s: pl.BlockSpec((1,) + s.shape[1:], lambda i: (layers - 1 - i, 0, 0))
    last = [jax.ShapeDtypeStruct((rows, width), BF), jax.ShapeDtypeStruct((8, ff), F32)]
    return pl.pallas_call(
        backward_kernel,
        grid=(layers,),
        in_specs=[whole_spec(a.shape) for a in (cot, g1, g2)]
        + [pl.BlockSpec(memory_space=pl.ANY)] * 3
        + [per_layer(a) for a in (n1, proj, probs, n2, slope, inv)],
        out_specs=[per_layer(s) for s in outs] + [whole_spec(s.shape) for s in last],
        out_shape=outs + last,
        scratch_shapes=[
            pltpu.VMEM((rows, width), F32),
            pltpu.VMEM((6, 8, width), F32),
            pltpu.VMEM((8, 3 * width), F32),
            pltpu.VMEM((8, ff), F32),
            pltpu.VMEM((4 * width, width), BF),
            pltpu.VMEM((ff, width), BF),
            pltpu.VMEM((width, ff), BF),
            pltpu.SemaphoreType.DMA((3,)),
        ],
        compiler_params=pltpu.CompilerParams(vmem_limit_bytes=VMEM_LIMIT),
    )(cot, g1, g2, wqot, wet, wct, n1, proj, probs, n2, slope, inv)


def outer_kernel(spot_ref, left_ref, right_ref, give_ref, keep_ref, scr, *, tall):
    scr[...] = tn(left_ref[...], right_ref[...]).astype(BF)
    split_out(spot_ref, scr, give_ref, keep_ref, 0, scr.shape[1], tall)


def split_out(spot_ref, scr, give_ref, keep_ref, at, cols, tall):
    x, c, y = spot_ref[0], spot_ref[1], spot_ref[2]
    for crel in (1, 0):
        out = give_ref if crel else keep_ref
        for xrel in (0, 1):
            for yrel in (0, 1):
                part = ((x ^ xrel) * 2 + (c ^ crel)) * 2 + (y ^ yrel)
                start = pl.multiple_of(part * tall, tall)
                out[xrel, yrel, 0:tall, at : at + cols] = scr[pl.ds(start, tall), :]


def parts_of(rows, cols):
    return jax.ShapeDtypeStruct((2, 2, rows, cols), BF)


def expand_grads(spot, left, right, tile=768):
    depth, width = left.shape
    half = right.shape[1] // 2
    steps = half // tile
    out = parts_of(width // 8, half)
    out_spec = pl.BlockSpec((2, 2, width // 8, tile), lambda j, s: (0, 0, 0, j))
    return pl.pallas_call(
        partial(outer_kernel, tall=width // 8),
        grid_spec=pltpu.PrefetchScalarGridSpec(
            num_scalar_prefetch=1,
            grid=(steps,),
            in_specs=[
                pl.BlockSpec((depth, width), lambda j, s: (0, 0)),
                pl.BlockSpec((depth, tile), lambda j, s: (0, s[3] * steps + j)),
            ],
            out_specs=[out_spec, out_spec],
            scratch_shapes=[pltpu.VMEM((width, tile), BF)],
        ),
        out_shape=[out, out],
        cost_estimate=cost_of(depth, width, half),
        compiler_params=pltpu.CompilerParams(vmem_limit_bytes=VMEM_LIMIT),
    )(spot, left, right)


def cost_of(depth, rows, cols):
    return pl.CostEstimate(
        flops=2 * depth * rows * cols, transcendentals=0, bytes_accessed=2 * depth * (rows + cols) + 2 * rows * cols
    )


def contract_kernel(spot_ref, left_ref, right_ref, give_ref, keep_ref, scr):
    step = pl.program_id(0)
    y = spot_ref[2]
    tall = scr.shape[0] // 2
    scr[...] = tn(left_ref[...], right_ref[...]).astype(BF)
    for yrel in (0, 1):
        start = pl.multiple_of((y ^ yrel) * tall, tall)

        @pl.when(step < 2)
        def _():
            give_ref[0, yrel] = scr[pl.ds(start, tall), :]

        @pl.when(step >= 2)
        def _():
            keep_ref[0, yrel] = scr[pl.ds(start, tall), :]


def contract_grads(spot, left, right):
    depth, ff = left.shape
    width = right.shape[1]
    tall = ff // 8

    def column(i, s):
        return (0, (((i & 1) ^ s[0]) * 2 + ((1 - (i >> 1)) ^ s[1])) * 2 + s[3])

    out = parts_of(tall // 2, width)
    return pl.pallas_call(
        contract_kernel,
        grid_spec=pltpu.PrefetchScalarGridSpec(
            num_scalar_prefetch=1,
            grid=(4,),
            in_specs=[
                pl.BlockSpec((depth, tall), column),
                pl.BlockSpec((depth, width), lambda i, s: (0, 0)),
            ],
            out_specs=[
                pl.BlockSpec((1, 2, tall // 2, width), lambda i, s: (jnp.minimum(i, 1), 0, 0, 0)),
                pl.BlockSpec((1, 2, tall // 2, width), lambda i, s: (jnp.maximum(i - 2, 0), 0, 0, 0)),
            ],
            scratch_shapes=[pltpu.VMEM((tall, width), BF)],
        ),
        out_shape=[out, out],
        cost_estimate=cost_of(depth, ff // 2, width),
        compiler_params=pltpu.CompilerParams(vmem_limit_bytes=VMEM_LIMIT),
    )(spot, left, right)


def attention_kernel(
    spot_ref, first_ref, gproj_ref, att_ref, gattn_ref, sums_ref, give_ref, keep_ref, qkv_scr, out_scr,
):
    tall = qkv_scr.shape[0] // 8
    wide = qkv_scr.shape[1]
    qkv_scr[...] = tn(first_ref[...], gproj_ref[...]).astype(BF)
    split_out(spot_ref, qkv_scr, give_ref, keep_ref, 0, wide, tall)
    out_scr[...] = tn(att_ref[...], gattn_ref[...]).astype(BF)
    split_out(spot_ref, out_scr, give_ref, keep_ref, wide, out_scr.shape[1], tall)
    x, c = spot_ref[0], spot_ref[1]
    width, cols = qkv_scr.shape[0], give_ref.shape[3]
    for crel, out in ((1, give_ref), (0, keep_ref)):
        for xrel in (0, 1):
            place = (x ^ xrel) * 2 + (c ^ crel)
            window = lambda i, start, size: sums_ref[i : i + 1, pl.ds(pl.multiple_of(start, 128), size)]
            low = ((place * 3) >> 1) * 128
            singles = [window(i, low, 256) for i in range(6)]
            doubles = [window(6, place * (width // 2), width // 2), window(7, place * width, width)]
            used = (width // 2) * 3
            doubles.append(jnp.zeros((1, cols - used), F32))
            block = jnp.concatenate(
                [
                    jnp.concatenate(singles, axis=1),
                    jnp.concatenate(doubles, axis=1),
                    jnp.zeros((14, cols), F32),
                ],
                axis=0,
            ).astype(BF)
            for yrel in (0, 1):
                out[xrel, yrel, tall : tall + 16, :] = block


def attention_grads(spot, first, gproj, att, gattn, sums):
    depth, width = first.shape
    wide, thin = gproj.shape[1] // 2, gattn.shape[1] // 2
    out = parts_of(width // 8 + 16, wide + thin)
    whole = lambda shape: pl.BlockSpec(shape, lambda i, s: (0,) * len(shape))
    half = lambda cols: pl.BlockSpec((depth, cols), lambda i, s: (0, s[3]))
    return pl.pallas_call(
        attention_kernel,
        grid_spec=pltpu.PrefetchScalarGridSpec(
            num_scalar_prefetch=1,
            grid=(1,),
            in_specs=[
                whole(first.shape), half(wide), whole(att.shape), half(thin), whole(sums.shape),
            ],
            out_specs=[whole(out.shape), whole(out.shape)],
            scratch_shapes=[pltpu.VMEM((width, wide), BF), pltpu.VMEM((width, thin), BF)],
        ),
        out_shape=[out, out],
        cost_estimate=cost_of(depth, width, wide + thin),
        compiler_params=pltpu.CompilerParams(vmem_limit_bytes=VMEM_LIMIT),
    )(spot, first, gproj, att, gattn, sums)


def xor_order(stacked, flips):
    count = stacked.shape[0]
    rest = stacked.shape[1:]
    bit = 1
    while bit < count:
        split = stacked.reshape((count // (2 * bit), 2, bit) + rest)
        split = jnp.where((flips & bit) != 0, split[:, ::-1], split)
        stacked = split.reshape((count,) + rest)
        bit *= 2
    return stacked


def label_of(section):
    return (section & ~3) | ((section & 1) << 1) | ((section >> 1) & 1)


def by_label(k, sections):
    return [(s, label_of(label_of(s) ^ k)) for s in range(sections)]


def move(array, flip_x, flip_y, flip_z, sections, dps):
    flip = flip_z * 2 + flip_y
    pairs = [
        (s * dps + d, (s ^ flip) * dps + (d ^ (flip_x * 2))) for s in range(sections) for d in range(dps)
    ]
    return lax.ppermute(array, AXES, pairs)


def over_core(give, keep, dps):
    return keep + lax.ppermute(give, "dp", [(d, d ^ 1) for d in range(dps)])


def plane_parts(both, hop):
    return [hop(both[1, 0], 1, 0, 0), hop(both[0, 1], 0, 1, 0), hop(both[1, 1], 1, 1, 0)]


def plane_sum(both, parts):
    return (both[0, 0].astype(F32) + parts[0] + parts[1] + parts[2]).astype(BF)


def all_parts(total, hop):
    return total, hop(total, 0, 1, 0), hop(total, 0, 0, 1), hop(total, 0, 1, 1)


def in_order(pieces, y, r):
    own, other_y, other_r, other_both = (p.astype(F32) for p in pieces)
    low = jnp.where(y == 0, own, other_y), jnp.where(y == 0, other_y, own)
    high = jnp.where(y == 0, other_r, other_both), jnp.where(y == 0, other_both, other_r)
    pick = lambda a, b: jnp.where(r == 0, a, b)
    return (
        (pick(low[0], high[0]), pick(low[1], high[1])),
        (pick(high[0], low[0]), pick(high[1], low[1])),
    )


def body(
    tokens, lengths, cotangent, first_gain, first_shift, qkv_weight, qv_bias, out_weight, out_bias,
    second_gain, second_shift, expand_weight, expand_bias, contract_weight, contract_bias,
):
    sections, dps = lax.axis_size("section"), lax.axis_size("dp")
    section, dp = lax.axis_index("section"), lax.axis_index("dp")
    micro, _, piece_rows, width = tokens.shape
    rows = piece_rows * sections
    ff = expand_weight.shape[1]
    label = label_of(section)

    sent = jnp.concatenate([tokens[:, 0], cotangent[:, 0]], axis=-1)
    got = []
    for k in range(sections):
        block = lax.dynamic_index_in_dim(sent, (label ^ k) >> 1, 0, keepdims=False)
        got.append(block if k == 0 else lax.ppermute(block, "section", by_label(k, sections)))
    shard = xor_order(jnp.stack(got), label)
    shard = shard.reshape(sections // 4, 2, 2, piece_rows, 2 * width).swapaxes(1, 2).reshape(rows, 2 * width)
    x, cot = shard[:, :width], shard[:, width:]
    spot = jnp.stack([(dp >> 1) & 1, dp & 1, section & 1, (section >> 1) & 1, label >> 1]).astype(jnp.int32)
    first, n1, proj, probs, att, n2, second, slope, act, inv, wqot, wet, wct, last = forward_all(
        lengths[:, 0], spot, x,
        [first_gain, first_shift, qv_bias, out_bias, second_gain, second_shift, expand_bias, contract_bias],
        qkv_weight, out_weight, expand_weight, contract_weight, sections,
    )
    gproj, gattn, gpre, gmlp, gtok, sums = backward_all(
        cot, first_gain, second_gain, wqot, wet, wct, n1, proj, probs, n2, slope, inv,
    )

    flat = lambda a: a.reshape(-1, a.shape[-1])
    first, att, second, act = flat(first), flat(att), flat(second), flat(act)
    gproj, gattn, gpre, gmlp = flat(gproj), flat(gattn), flat(gpre), flat(gmlp)
    both = jnp.concatenate([last, gtok], axis=1).reshape(sections, piece_rows, 2 * width)
    blocks = [
        lax.dynamic_index_in_dim(both, label_of(label ^ k), 0, keepdims=False) for k in range(0, sections, 2)
    ]
    if (sections, dps) == (8, 4):
        g_qkv, g_out, g_exp, g_con, v, back = grads_small_slice(
            section, dp, spot, first, att, second, act, gproj, gattn, gpre, gmlp, sums, blocks
        )
    else:
        half = (label & 1) == 0

        def everywhere(whole):
            whole = jnp.where(half, whole, 0.0).astype(BF)
            own = lax.psum_scatter(whole, "dp", scatter_dimension=0, tiled=True)
            return lax.psum(own, "section").astype(F32)

        g_qkv, g_out = everywhere(tn(first, gproj)), everywhere(tn(att, gattn))
        g_exp, g_con = everywhere(tn(second, gpre)), everywhere(tn(act, gmlp))
        v = [everywhere(sums[i, :n]) for i, n in enumerate([width] * 6 + [2 * width, ff])]
        back = blocks[:1] + [
            lax.ppermute(block, "section", by_label(2 * i + 2, sections)) for i, block in enumerate(blocks[1:])
        ]

    back = xor_order(jnp.stack(back), label >> 1)
    result = back[:, None, :, :width]
    grad_tokens = back[:, None, :, width:].astype(F32)
    return (
        result, grad_tokens, v[0], v[1], g_qkv, v[6], g_out, v[2], v[3], v[4], g_exp, v[7], g_con, v[5],
    )


def grads_small_slice(section, dp, spot, first, att, second, act, gproj, gattn, gpre, gmlp, sums, blocks):
    sections, dps = 8, 4
    y, r, core = section & 1, (section >> 1) & 1, dp & 1
    width, ff = first.shape[1], act.shape[1]
    hop = partial(move, sections=sections, dps=dps)
    cols = 2 * width
    tall = width // 8
    tie = lax.optimization_barrier
    add_a = over_core(*contract_grads(spot, act, gmlp), dps)
    second, gpre, add_a = tie((second, gpre, add_a))
    from_a, out_b = plane_parts(add_a, hop), expand_grads(spot, second, gpre)
    from_a, out_b = tie((from_a, out_b))
    plane_a = plane_sum(add_a, from_a)
    z_a, add_b = hop(plane_a, 0, 0, 2), over_core(*out_b, dps)
    first, gproj, att, gattn, add_b = tie((first, gproj, att, gattn, add_b))
    from_b, out_c = plane_parts(add_b, hop), attention_grads(spot, first, gproj, att, gattn, sums)
    from_b, out_c, z_a = tie((from_b, out_c, z_a))
    plane_b, total_a = plane_sum(add_b, from_b), plane_a + z_a
    z_b = hop(jnp.concatenate([plane_b, blocks[2], blocks[3]], axis=0), 0, 0, 2)
    r_a, add_c = hop(total_a, 0, 0, 1), over_core(*out_c, dps)
    from_c = plane_parts(add_c, hop)
    from_c, z_b, r_a = tie((from_c, z_b, r_a))
    pieces = (z_b.shape[0] - tall) // 2
    z_b, from_z, through_z = z_b[:tall], z_b[tall : tall + pieces], z_b[tall + pieces :]
    plane_c, total_b = plane_sum(add_c, from_c), plane_b + z_b
    mid = tall // 2
    top, bottom = total_b[:mid], total_b[mid:]
    z_c, y_a = hop(plane_c, 0, 0, 2), hop(jnp.stack([total_a, r_a]), 0, 1, 0)
    r_top, y_bottom = hop(top, 0, 0, 1), hop(jnp.concatenate([bottom, blocks[1], through_z], axis=0), 0, 1, 0)
    z_c, y_a, r_top, y_bottom = tie((z_c, y_a, r_top, y_bottom))
    y_bottom, from_y, from_both = y_bottom[:mid], y_bottom[mid : mid + pieces], y_bottom[mid + pieces :]
    back = [blocks[0], from_y, from_z, from_both]
    rest = all_parts(plane_c + z_c, hop)
    y_top = hop(jnp.stack([top, r_top]), 0, 1, 0)
    r_bottom = hop(jnp.stack([bottom, y_bottom]), 0, 0, 1)
    stacked = lambda a, b: jnp.concatenate([a, b], axis=0)
    con = total_a, y_a[0], r_a, y_a[1]
    exp = total_b, stacked(y_top[0], y_bottom), stacked(r_top, r_bottom[0]), stacked(y_top[1], r_bottom[1])
    con, exp, att_part = in_order(con, y, r), in_order(exp, y, r), in_order([p[:tall] for p in rest], y, r)
    g_con = jnp.concatenate([con[0][0], con[0][1], con[1][0], con[1][1]], axis=0)
    g_exp = jnp.concatenate([jnp.concatenate([exp[0][j], exp[1][j]], axis=1) for j in (0, 1)], axis=0)
    wide = gproj.shape[1] // 2
    side = lambda a, b: jnp.concatenate(
        [jnp.concatenate([att_part[0][j][:, a:b], att_part[1][j][:, a:b]], axis=1) for j in (0, 1)], axis=0
    )
    vectors = rest[0][tall:].astype(F32)
    windows = vectors[0].reshape(6, -1)
    quarter = width // 4
    windows = jnp.where(core == 0, windows[:, :quarter], windows[:, 64 : 64 + quarter])
    v = [windows[i] for i in range(6)] + [vectors[1, : 2 * quarter], vectors[1, 2 * quarter : 2 * quarter + ff // 4]]
    return side(0, wide), side(wide, cols), g_exp, g_con, v, back


def solution(mesh):
    tok = P(None, "dp", "section", None)
    return jax.shard_map(
        body,
        mesh=mesh,
        in_specs=(tok, P(None, "dp", None), tok) + (P(),) * 12,
        out_specs=(
            tok, tok, P("dp"), P("dp"), P("dp", None), P("dp"), P("dp", None), P("dp"),
            P("dp"), P("dp"), P("dp", None), P("dp"), P("dp", None), P("dp"),
        ),
        check_vma=False,
    )
```

```python
from functools import partial

import jax
import jax.numpy as jnp
from jax import lax
from jax.experimental import pallas as pl
from jax.experimental.pallas import tpu as pltpu
from jax.sharding import PartitionSpec as P

HEAD_DIM = 64
EPSILON = 1e-05
SCORE_SCALE = 0.125
MASKED = -1e30
GELU_A = 0.7978845608028654
GELU_B = 0.044715
BF = jnp.bfloat16
F32 = jnp.float32
AXES = ("section", "dp")
VMEM_LIMIT = 60 * 2**20


def nn(left, right):
    return jnp.dot(left, right, preferred_element_type=F32)


def nt(left, right):
    return lax.dot_general(left, right, (((1,), (1,)), ((), ())), preferred_element_type=F32)


def tn(left, right):
    return lax.dot_general(left, right, (((0,), (0,)), ((), ())), preferred_element_type=F32)


def normed_of(values):
    center = values - jnp.mean(values, axis=-1, keepdims=True)
    inverse = lax.rsqrt(jnp.mean(center * center, axis=-1, keepdims=True) + EPSILON)
    return center * inverse, inverse


def norm_back(upstream, normed, inverse, gain_row):
    scaled = upstream * gain_row
    return inverse * (
        scaled
        - jnp.mean(scaled, axis=-1, keepdims=True)
        - normed * jnp.mean(scaled * normed, axis=-1, keepdims=True)
    )


def row_of(ref):
    return ref[...].reshape(1, -1)


def lane_split(pair):
    lane = lax.broadcasted_iota(jnp.int32, pair.shape, 1)
    zero = jnp.zeros_like(pair)
    return jnp.where(lane < HEAD_DIM, pair, zero), jnp.where(lane < HEAD_DIM, zero, pair)


def forward_kernel(
    lens_ref, spot_ref, x_ref, g1_ref, b1_ref, qvb_ref, obias_ref, g2_ref, b2_ref, ebias_ref, cbias_ref,
    wq_hbm, wo_hbm, we_hbm, wc_hbm,
    first_ref, n1_ref, proj_ref, probs_ref, att_ref, n2_ref, second_ref, slope_ref, act_ref,
    inv_ref, wqot_ref, wet_ref, wct_ref, last_ref, h_scr, mask_scr, wqo_scr, we_ref, wc_ref, sems,
):
    step = pl.program_id(0)
    rows, width = h_scr.shape
    pairs = width // 128
    ff = we_ref.shape[1]
    loads = [
        pltpu.make_async_copy(wq_hbm, wqo_scr.at[:, 0 : 3 * width], sems.at[0]),
        pltpu.make_async_copy(wo_hbm, wqo_scr.at[:, 3 * width : 4 * width], sems.at[1]),
        pltpu.make_async_copy(we_hbm, we_ref, sems.at[2]),
        pltpu.make_async_copy(wc_hbm, wc_ref, sems.at[3]),
    ]

    @pl.when(step == 0)
    def _():
        for load in loads:
            load.start()
        h_scr[...] = x_ref[...].astype(F32)
        query = lax.broadcasted_iota(jnp.int32, (rows, rows), 0)
        key = lax.broadcasted_iota(jnp.int32, (rows, rows), 1)
        own_q = jnp.zeros((rows, rows), jnp.int32)
        own_k = jnp.zeros((rows, rows), jnp.int32)
        slots = lens_ref.shape[1]
        end = jnp.int32(0)
        for slot in range(slots):
            end = end + lens_ref[spot_ref[4], slot]
            own_q += (query >= end).astype(jnp.int32)
            own_k += (key >= end).astype(jnp.int32)
        mask_scr[...] = jnp.where((own_q == own_k) & (key <= query), 0.0, MASKED)
        loads[0].wait()
        loads[1].wait()

    strip = wqot_ref.shape[0]
    at = pl.multiple_of(jnp.minimum(step, 4 * width // strip - 1) * strip, 128)
    wqot_ref[...] = wqo_scr[:, pl.ds(at, strip)].T
    h = h_scr[...]
    n1, inv1 = normed_of(h)
    first_low = (n1 * row_of(g1_ref) + row_of(b1_ref)).astype(BF)
    first_ref[0] = first_low
    n1_ref[0] = n1.astype(BF)
    raw = nn(first_low, wqo_scr[:, 0 : 3 * width])
    queries = ((raw[:, :width] + row_of(qvb_ref)[:, :width]) * SCORE_SCALE).astype(BF)
    keys = raw[:, width : 2 * width].astype(BF)
    values = (raw[:, 2 * width :] + row_of(qvb_ref)[:, width:]).astype(BF)
    proj_ref[0, :, 0:width] = queries
    proj_ref[0, :, width : 2 * width] = keys
    proj_ref[0, :, 2 * width : 3 * width] = values
    mask = mask_scr[...]
    mask = jnp.concatenate([mask, mask], axis=0)
    cuts = [slice(128 * p, 128 * (p + 1)) for p in range(pairs)]
    scores = [nt(jnp.concatenate(lane_split(queries[:, cut]), axis=0), keys[:, cut]) + mask for cut in cuts]
    tops = [jnp.max(s, axis=-1, keepdims=True) for s in scores]
    weights = [jnp.exp(s - t) for s, t in zip(scores, tops)]
    sums = [1.0 / jnp.sum(w, axis=-1, keepdims=True) for w in weights]
    lows = [(w * t).astype(BF) for w, t in zip(weights, sums)]
    outs = []
    for p, (low, cut) in enumerate(zip(lows, cuts)):
        probs_ref[0, 2 * rows * p : 2 * rows * (p + 1), :] = low
        both = jnp.concatenate([low[:rows], low[rows:]], axis=1)
        outs.append(nn(both, jnp.concatenate(lane_split(values[:, cut]), axis=0)).astype(BF))
    attended = jnp.concatenate(outs, axis=1)
    att_ref[0] = attended
    middle = h + (nn(attended, wqo_scr[:, 3 * width : 4 * width]) + row_of(obias_ref))
    n2, inv2 = normed_of(middle)
    second_low = (n2 * row_of(g2_ref) + row_of(b2_ref)).astype(BF)
    second_ref[0] = second_low
    n2_ref[0] = n2.astype(BF)
    inv_ref[0] = jnp.concatenate(
        [jnp.broadcast_to(inv1, (rows, 128)), jnp.broadcast_to(inv2, (rows, 128))], axis=1
    )
    total = middle + row_of(cbias_ref)

    @pl.when(step == 0)
    def _():
        loads[2].wait()
        loads[3].wait()

    wet_ref[...] = we_ref[:, pl.ds(at, strip)].T
    wct_ref[...] = wc_ref[pl.ds(at, strip), :].T
    ebias = row_of(ebias_ref)
    chunk = 768
    cuts = [slice(chunk * j, chunk * (j + 1)) for j in range(ff // chunk)]
    expand = lambda cut: nn(second_low, we_ref[:, cut]) + ebias[:, cut]
    pres = [expand(cuts[0])]
    for j, cols in enumerate(cuts):
        if j + 1 < len(cuts):
            pres.append(expand(cuts[j + 1]))
        pre = pres[j]
        square = pre * pre
        half = 0.5 + 0.5 * jnp.tanh(pre * (GELU_A + GELU_A * GELU_B * square))
        act = pre * half
        slope = half + act * (1.0 - half) * (2.0 * GELU_A + 6.0 * GELU_A * GELU_B * square)
        act = act.astype(BF)
        slope_ref[0, :, cols] = slope.astype(BF)
        act_ref[0, :, cols] = act
        total = total + nn(act, wc_ref[cols, :])
    low_out = total.astype(BF)
    h_scr[...] = low_out.astype(F32)

    @pl.when(step == pl.num_programs(0) - 1)
    def _():
        last_ref[...] = low_out


def fold(values):
    return jnp.sum(values.reshape(-1, 8, values.shape[-1]), axis=0)


def backward_kernel(
    spot_ref, cot_ref, g1_ref, g2_ref, wqot_hbm, wet_hbm, wct_hbm,
    n1_ref, proj_ref, probs_ref, n2_ref, slope_ref, inv_ref, *refs, fused,
):
    if fused:
        act_hbm, refs = refs[0], refs[1:]
    gproj_ref, gattn_ref, gpre_ref, gtok_ref, sums_ref, *refs = refs
    if fused:
        give_ref, keep_ref, *refs = refs
    else:
        gmlp_ref, *refs = refs
    g_scr, s768_scr, s2304_scr, s3072_scr, wqot_ref, wet_ref, wct_ref, sems, *refs = refs
    if fused:
        act_scr, gmlp_scr, tile_scr = refs
    step = pl.program_id(0)
    rows, width = g_scr.shape
    pairs = width // 128
    ff = wct_ref.shape[1]

    loads = [
        pltpu.make_async_copy(wct_hbm, wct_ref, sems.at[0]),
        pltpu.make_async_copy(wet_hbm, wet_ref, sems.at[1]),
        pltpu.make_async_copy(wqot_hbm, wqot_ref, sems.at[2]),
    ]

    if fused:
        x, c, r = spot_ref[0], spot_ref[1], spot_ref[3]
        tall = act_scr.shape[1] // 4
        for i in range(4):
            block = (((i & 1) ^ x) * 2 + ((1 - (i >> 1)) ^ c)) * 2 + r
            source = act_hbm.at[:, pl.ds(pl.multiple_of(block * tall, 128), tall)]
            loads.append(pltpu.make_async_copy(source, act_scr.at[:, tall * i : tall * (i + 1)], sems.at[3 + i]))

    @pl.when(step == 0)
    def _():
        for load in loads:
            load.start()
        g_scr[...] = cot_ref[...].astype(F32)
        s768_scr[...] = jnp.zeros_like(s768_scr)
        s2304_scr[...] = jnp.zeros_like(s2304_scr)
        s3072_scr[...] = jnp.zeros_like(s3072_scr)
        loads[0].wait()
        loads[1].wait()

    g = g_scr[...]
    gmlp = g.astype(BF)
    if fused:
        layer = pl.num_programs(0) - 1 - step
        gmlp_scr[pl.ds(pl.multiple_of(layer * rows, rows), rows), :] = gmlp
    else:
        gmlp_ref[0] = gmlp
    gsec = jnp.zeros((rows, width), F32)
    chunk = 1024
    for j in range(ff // chunk):
        cols = slice(chunk * j, chunk * (j + 1))
        gpre = (nn(gmlp, wct_ref[:, cols]) * slope_ref[0, :, cols].astype(F32)).astype(BF)
        gpre_ref[0, :, cols] = gpre
        s3072_scr[:, cols] += fold(gpre.astype(F32))
        gsec = gsec + nn(gpre, wet_ref[cols, :])
    n2 = n2_ref[0].astype(F32)
    gmid = g + norm_back(gsec, n2, inv_ref[0, :, 128:129], row_of(g2_ref))
    gattn = gmid.astype(BF)
    gattn_ref[0] = gattn

    @pl.when(step == 0)
    def _():
        loads[2].wait()

    gatt = nn(gattn, wqot_ref[3 * width : 4 * width, :]).astype(BF)
    dqs, dks, dvs = [], [], []
    outs2, gprobs = [], []
    for p in range(pairs):
        v = proj_ref[0, :, 2 * width + 128 * p : 2 * width + 128 * (p + 1)]
        out2 = jnp.concatenate(lane_split(gatt[:, 128 * p : 128 * (p + 1)]), axis=0)
        outs2.append(out2)
        gprobs.append(nt(out2, v))
    gscores = []
    for p in range(pairs):
        prob = probs_ref[0, 2 * rows * p : 2 * rows * (p + 1), :].astype(F32)
        gs = prob * (gprobs[p] - jnp.sum(prob * gprobs[p], axis=-1, keepdims=True))
        gscores.append(gs.astype(BF))
    for p in range(pairs):
        q = proj_ref[0, :, 128 * p : 128 * (p + 1)]
        k = proj_ref[0, :, width + 128 * p : width + 128 * (p + 1)]
        gscore = gscores[p]
        low = probs_ref[0, 2 * rows * p : 2 * rows * (p + 1), :]
        both = jnp.concatenate([gscore[:rows], gscore[rows:]], axis=1)
        k2 = jnp.concatenate(lane_split(k), axis=0)
        q2 = jnp.concatenate(lane_split(q), axis=0)
        dqs.append((nn(both, k2) * SCORE_SCALE).astype(BF))
        kv = tn(jnp.concatenate([gscore, low], axis=1), jnp.concatenate([q2, outs2[p]], axis=1))
        dks.append(kv[:rows, :128].astype(BF))
        dvs.append(kv[rows:, 128:].astype(BF))
    gproj = jnp.concatenate(dqs + dks + dvs, axis=1)
    gproj_ref[0] = gproj
    gfirst = nn(gproj, wqot_ref[0 : 3 * width, :])
    n1 = n1_ref[0].astype(F32)
    gin = gmid + norm_back(gfirst, n1, inv_ref[0, :, 0:1], row_of(g1_ref))
    s768_scr[0] += fold(gfirst * n1)
    s768_scr[1] += fold(gfirst)
    s768_scr[2] += fold(gattn.astype(F32))
    s768_scr[3] += fold(gsec * n2)
    s768_scr[4] += fold(gsec)
    s768_scr[5] += fold(gmlp.astype(F32))
    s2304_scr[...] += fold(gproj.astype(F32))
    low_out = gin.astype(BF)
    g_scr[...] = low_out.astype(F32)

    @pl.when(step == pl.num_programs(0) - 1)
    def _():
        gtok_ref[...] = low_out
        row = lambda v: jnp.sum(v, axis=0, keepdims=True)
        for i in range(6):
            sums_ref[i : i + 1, 0:width] = row(s768_scr[i])
        sums_ref[6:7, 0:width] = row(s2304_scr[:, 0:width])
        sums_ref[6:7, width : 2 * width] = row(s2304_scr[:, 2 * width : 3 * width])
        sums_ref[7:8, :] = row(s3072_scr[...])
        if fused:
            y = spot_ref[2]
            for load in loads[3:]:
                load.wait()
            for out, at in ((give_ref, 0), (keep_ref, 2 * tall)):
                tile_scr[...] = tn(act_scr[:, at : at + 2 * tall], gmlp_scr[...]).astype(BF)
                for xrel in (0, 1):
                    for yrel in (0, 1):
                        start = pl.multiple_of(xrel * tall + (y ^ yrel) * (tall // 2), 16)
                        out[xrel, yrel] = tile_scr[pl.ds(start, tall // 2), :]


def whole_spec(shape):
    zeros = (0,) * len(shape)
    return pl.BlockSpec(shape, lambda i, *_: zeros, pipeline_mode=pl.Buffered(1))


def forward_all(lens, spot, x, rows_in, wq, wo, we, wc, layers):
    rows, width = x.shape
    ff = we.shape[1]
    pairs = width // 128
    strip = ff // 8
    stack = lambda cols, r=rows, t=BF: jax.ShapeDtypeStruct((layers, r, cols), t)
    outs = [
        stack(width), stack(width), stack(3 * width), stack(rows, 2 * rows * pairs), stack(width),
        stack(width), stack(width), stack(ff), stack(ff), stack(256, rows, F32),
    ]
    per_layer = lambda s: pl.BlockSpec((1,) + s.shape[1:], lambda i, *_: (i, 0, 0))
    turned = [jax.ShapeDtypeStruct(s, BF) for s in ((4 * width, width), (ff, width), (width, ff))]
    by_rows = pl.BlockSpec((strip, width), lambda i, *_: (jnp.minimum(i, 7), 0))
    by_cols = pl.BlockSpec((width, strip), lambda i, *_: (0, jnp.minimum(i, 7)))
    last = jax.ShapeDtypeStruct((rows, width), BF)
    return pl.pallas_call(
        forward_kernel,
        grid_spec=pltpu.PrefetchScalarGridSpec(
            num_scalar_prefetch=2,
            grid=(layers,),
            in_specs=[whole_spec(a.shape) for a in (x, *rows_in)]
            + [pl.BlockSpec(memory_space=pl.ANY)] * 4,
            out_specs=[per_layer(s) for s in outs] + [by_rows, by_rows, by_cols, whole_spec(last.shape)],
            scratch_shapes=[
                pltpu.VMEM((rows, width), F32),
                pltpu.VMEM((rows, rows), F32),
                pltpu.VMEM((width, 4 * width), BF),
                pltpu.VMEM((width, ff), BF),
                pltpu.VMEM((ff, width), BF),
                pltpu.SemaphoreType.DMA((4,)),
            ],
        ),
        out_shape=outs + turned + [last],
        compiler_params=pltpu.CompilerParams(vmem_limit_bytes=VMEM_LIMIT),
    )(lens, spot, x, *rows_in, wq, wo, we, wc)


def backward_all(spot, cot, g1, g2, wqot, wet, wct, n1, proj, probs, n2, slope, inv, act=None):
    layers, rows, width = n1.shape
    ff = wct.shape[1]
    fused = act is not None
    stack = lambda cols: jax.ShapeDtypeStruct((layers, rows, cols), BF)
    outs = [stack(3 * width), stack(width), stack(ff)]
    per_layer = lambda s: pl.BlockSpec((1,) + s.shape[1:], lambda i, *_: (layers - 1 - i, 0, 0))
    last = [jax.ShapeDtypeStruct((rows, width), BF), jax.ShapeDtypeStruct((8, ff), F32)]
    out_specs = [per_layer(s) for s in outs] + [whole_spec(s.shape) for s in last]
    more_in, more_scratch = [], []
    if fused:
        more_in = [act]
        last += [parts_of(ff // 16, width)] * 2
        out_specs += [whole_spec(last[-1].shape)] * 2
        more_scratch = [
            pltpu.VMEM((layers * rows, ff // 2), BF),
            pltpu.VMEM((layers * rows, width), BF),
            pltpu.VMEM((ff // 4, width), BF),
        ]
    else:
        last.append(stack(width))
        out_specs.append(per_layer(last[-1]))
    return pl.pallas_call(
        partial(backward_kernel, fused=fused),
        grid_spec=pltpu.PrefetchScalarGridSpec(
            num_scalar_prefetch=1,
            grid=(layers,),
            in_specs=[whole_spec(a.shape) for a in (cot, g1, g2)]
            + [pl.BlockSpec(memory_space=pl.ANY)] * 3
            + [per_layer(a) for a in (n1, proj, probs, n2, slope, inv)]
            + [pl.BlockSpec(memory_space=pl.ANY)] * len(more_in),
            out_specs=out_specs,
            scratch_shapes=[
                pltpu.VMEM((rows, width), F32),
                pltpu.VMEM((6, 8, width), F32),
                pltpu.VMEM((8, 3 * width), F32),
                pltpu.VMEM((8, ff), F32),
                pltpu.VMEM((4 * width, width), BF),
                pltpu.VMEM((ff, width), BF),
                pltpu.VMEM((width, ff), BF),
                pltpu.SemaphoreType.DMA((7,)),
            ]
            + more_scratch,
        ),
        out_shape=outs + last,
        compiler_params=pltpu.CompilerParams(vmem_limit_bytes=VMEM_LIMIT),
    )(spot, cot, g1, g2, wqot, wet, wct, n1, proj, probs, n2, slope, inv, *more_in)


def outer_kernel(spot_ref, left_ref, right_ref, give_ref, keep_ref, scr, *, tall):
    scr[...] = tn(left_ref[...], right_ref[...]).astype(BF)
    split_out(spot_ref, scr, give_ref, keep_ref, 0, scr.shape[1], tall)


def split_out(spot_ref, scr, give_ref, keep_ref, at, cols, tall):
    x, c, y = spot_ref[0], spot_ref[1], spot_ref[2]
    for crel in (1, 0):
        out = give_ref if crel else keep_ref
        for xrel in (0, 1):
            for yrel in (0, 1):
                part = ((x ^ xrel) * 2 + (c ^ crel)) * 2 + (y ^ yrel)
                start = pl.multiple_of(part * tall, tall)
                out[xrel, yrel, 0:tall, at : at + cols] = scr[pl.ds(start, tall), :]


def parts_of(rows, cols):
    return jax.ShapeDtypeStruct((2, 2, rows, cols), BF)


def expand_grads(spot, left, right, tile=768):
    depth, width = left.shape
    half = right.shape[1] // 2
    steps = half // tile
    out = parts_of(width // 8, half)
    out_spec = pl.BlockSpec((2, 2, width // 8, tile), lambda j, s: (0, 0, 0, j))
    return pl.pallas_call(
        partial(outer_kernel, tall=width // 8),
        grid_spec=pltpu.PrefetchScalarGridSpec(
            num_scalar_prefetch=1,
            grid=(steps,),
            in_specs=[
                pl.BlockSpec((depth, width), lambda j, s: (0, 0)),
                pl.BlockSpec((depth, tile), lambda j, s: (0, s[3] * steps + j)),
            ],
            out_specs=[out_spec, out_spec],
            scratch_shapes=[pltpu.VMEM((width, tile), BF)],
        ),
        out_shape=[out, out],
        cost_estimate=cost_of(depth, width, half),
        compiler_params=pltpu.CompilerParams(vmem_limit_bytes=VMEM_LIMIT),
    )(spot, left, right)


def cost_of(depth, rows, cols):
    return pl.CostEstimate(
        flops=2 * depth * rows * cols, transcendentals=0, bytes_accessed=2 * depth * (rows + cols) + 2 * rows * cols
    )


def attention_kernel(
    spot_ref, first_ref, gproj_ref, att_ref, gattn_ref, sums_ref, give_ref, keep_ref, qkv_scr, out_scr,
):
    tall = qkv_scr.shape[0] // 8
    wide = qkv_scr.shape[1]
    qkv_scr[...] = tn(first_ref[...], gproj_ref[...]).astype(BF)
    split_out(spot_ref, qkv_scr, give_ref, keep_ref, 0, wide, tall)
    out_scr[...] = tn(att_ref[...], gattn_ref[...]).astype(BF)
    split_out(spot_ref, out_scr, give_ref, keep_ref, wide, out_scr.shape[1], tall)
    x, c = spot_ref[0], spot_ref[1]
    width, cols = qkv_scr.shape[0], give_ref.shape[3]
    for crel, out in ((1, give_ref), (0, keep_ref)):
        for xrel in (0, 1):
            place = (x ^ xrel) * 2 + (c ^ crel)
            window = lambda i, start, size: sums_ref[i : i + 1, pl.ds(pl.multiple_of(start, 128), size)]
            low = ((place * 3) >> 1) * 128
            singles = [window(i, low, 256) for i in range(6)]
            doubles = [window(6, place * (width // 2), width // 2), window(7, place * width, width)]
            used = (width // 2) * 3
            doubles.append(jnp.zeros((1, cols - used), F32))
            block = jnp.concatenate(
                [
                    jnp.concatenate(singles, axis=1),
                    jnp.concatenate(doubles, axis=1),
                    jnp.zeros((14, cols), F32),
                ],
                axis=0,
            ).astype(BF)
            for yrel in (0, 1):
                out[xrel, yrel, tall : tall + 16, :] = block


def attention_grads(spot, first, gproj, att, gattn, sums):
    depth, width = first.shape
    wide, thin = gproj.shape[1] // 2, gattn.shape[1] // 2
    out = parts_of(width // 8 + 16, wide + thin)
    whole = lambda shape: pl.BlockSpec(shape, lambda i, s: (0,) * len(shape))
    half = lambda cols: pl.BlockSpec((depth, cols), lambda i, s: (0, s[3]))
    return pl.pallas_call(
        attention_kernel,
        grid_spec=pltpu.PrefetchScalarGridSpec(
            num_scalar_prefetch=1,
            grid=(1,),
            in_specs=[
                whole(first.shape), half(wide), whole(att.shape), half(thin), whole(sums.shape),
            ],
            out_specs=[whole(out.shape), whole(out.shape)],
            scratch_shapes=[pltpu.VMEM((width, wide), BF), pltpu.VMEM((width, thin), BF)],
        ),
        out_shape=[out, out],
        cost_estimate=cost_of(depth, width, wide + thin),
        compiler_params=pltpu.CompilerParams(vmem_limit_bytes=VMEM_LIMIT),
    )(spot, first, gproj, att, gattn, sums)


def xor_order(stacked, flips):
    count = stacked.shape[0]
    rest = stacked.shape[1:]
    bit = 1
    while bit < count:
        split = stacked.reshape((count // (2 * bit), 2, bit) + rest)
        split = jnp.where((flips & bit) != 0, split[:, ::-1], split)
        stacked = split.reshape((count,) + rest)
        bit *= 2
    return stacked


def label_of(section):
    return (section & ~3) | ((section & 1) << 1) | ((section >> 1) & 1)


def by_label(k, sections):
    return [(s, label_of(label_of(s) ^ k)) for s in range(sections)]


def move(array, flip_x, flip_y, flip_z, sections, dps):
    flip = flip_z * 2 + flip_y
    pairs = [
        (s * dps + d, (s ^ flip) * dps + (d ^ (flip_x * 2))) for s in range(sections) for d in range(dps)
    ]
    return lax.ppermute(array, AXES, pairs)


def over_core(give, keep, dps):
    return keep + lax.ppermute(give, "dp", [(d, d ^ 1) for d in range(dps)])


def plane_parts(both, hop):
    return [hop(both[1, 0], 1, 0, 0), hop(both[0, 1], 0, 1, 0), hop(both[1, 1], 1, 1, 0)]


def plane_sum(both, parts):
    return (both[0, 0].astype(F32) + parts[0] + parts[1] + parts[2]).astype(BF)


def all_parts(total, hop):
    return total, hop(total, 0, 1, 0), hop(total, 0, 0, 1), hop(total, 0, 1, 1)


def in_order(pieces, y, r):
    own, other_y, other_r, other_both = (p.astype(F32) for p in pieces)
    low = jnp.where(y == 0, own, other_y), jnp.where(y == 0, other_y, own)
    high = jnp.where(y == 0, other_r, other_both), jnp.where(y == 0, other_both, other_r)
    pick = lambda a, b: jnp.where(r == 0, a, b)
    return (
        (pick(low[0], high[0]), pick(low[1], high[1])),
        (pick(high[0], low[0]), pick(high[1], low[1])),
    )


def body(
    tokens, lengths, cotangent, first_gain, first_shift, qkv_weight, qv_bias, out_weight, out_bias,
    second_gain, second_shift, expand_weight, expand_bias, contract_weight, contract_bias,
):
    sections, dps = lax.axis_size("section"), lax.axis_size("dp")
    section, dp = lax.axis_index("section"), lax.axis_index("dp")
    micro, _, piece_rows, width = tokens.shape
    rows = piece_rows * sections
    ff = expand_weight.shape[1]
    label = label_of(section)

    sent = jnp.concatenate([tokens[:, 0], cotangent[:, 0]], axis=-1)
    got = []
    for k in range(sections):
        block = lax.dynamic_index_in_dim(sent, (label ^ k) >> 1, 0, keepdims=False)
        got.append(block if k == 0 else lax.ppermute(block, "section", by_label(k, sections)))
    shard = xor_order(jnp.stack(got), label)
    shard = shard.reshape(sections // 4, 2, 2, piece_rows, 2 * width).swapaxes(1, 2).reshape(rows, 2 * width)
    x, cot = shard[:, :width], shard[:, width:]
    spot = jnp.stack([(dp >> 1) & 1, dp & 1, section & 1, (section >> 1) & 1, label >> 1]).astype(jnp.int32)
    first, n1, proj, probs, att, n2, second, slope, act, inv, wqot, wet, wct, last = forward_all(
        lengths[:, 0], spot, x,
        [first_gain, first_shift, qv_bias, out_bias, second_gain, second_shift, expand_bias, contract_bias],
        qkv_weight, out_weight, expand_weight, contract_weight, sections,
    )
    flat = lambda a: a.reshape(-1, a.shape[-1])
    first, att, second, act = flat(first), flat(att), flat(second), flat(act)
    known = (sections, dps) == (8, 4)
    gproj, gattn, gpre, gtok, sums, *contract = backward_all(
        spot, cot, first_gain, second_gain, wqot, wet, wct, n1, proj, probs, n2, slope, inv,
        act if known else None,
    )
    gproj, gattn, gpre = flat(gproj), flat(gattn), flat(gpre)
    both = jnp.concatenate([last, gtok], axis=1).reshape(sections, piece_rows, 2 * width)
    blocks = [
        lax.dynamic_index_in_dim(both, label_of(label ^ k), 0, keepdims=False) for k in range(0, sections, 2)
    ]
    if known:
        g_qkv, g_out, g_exp, g_con, v, back = grads_small_slice(
            section, dp, spot, first, att, second, gproj, gattn, gpre, contract, sums, blocks
        )
    else:
        half = (label & 1) == 0

        def everywhere(whole):
            whole = jnp.where(half, whole, 0.0).astype(BF)
            own = lax.psum_scatter(whole, "dp", scatter_dimension=0, tiled=True)
            return lax.psum(own, "section").astype(F32)

        g_qkv, g_out = everywhere(tn(first, gproj)), everywhere(tn(att, gattn))
        g_exp, g_con = everywhere(tn(second, gpre)), everywhere(tn(act, flat(contract[0])))
        v = [everywhere(sums[i, :n]) for i, n in enumerate([width] * 6 + [2 * width, ff])]
        back = blocks[:1] + [
            lax.ppermute(block, "section", by_label(2 * i + 2, sections)) for i, block in enumerate(blocks[1:])
        ]

    back = xor_order(jnp.stack(back), label >> 1)
    result = back[:, None, :, :width]
    grad_tokens = back[:, None, :, width:].astype(F32)
    return (
        result, grad_tokens, v[0], v[1], g_qkv, v[6], g_out, v[2], v[3], v[4], g_exp, v[7], g_con, v[5],
    )


def grads_small_slice(section, dp, spot, first, att, second, gproj, gattn, gpre, contract, sums, blocks):
    sections, dps = 8, 4
    y, r, core = section & 1, (section >> 1) & 1, dp & 1
    width, ff = first.shape[1], gpre.shape[1]
    hop = partial(move, sections=sections, dps=dps)
    cols = 2 * width
    tall = width // 8
    tie = lax.optimization_barrier
    add_a = over_core(*contract, dps)
    second, gpre, add_a = tie((second, gpre, add_a))
    from_a, out_b = plane_parts(add_a, hop), expand_grads(spot, second, gpre)
    from_a, out_b, blocks = tie((from_a, out_b, blocks))
    plane_a = plane_sum(add_a, from_a)
    z_a, add_b = hop(plane_a, 0, 0, 2), over_core(*out_b, dps)
    first, gproj, att, gattn, add_b = tie((first, gproj, att, gattn, add_b))
    from_b, out_c = plane_parts(add_b, hop), attention_grads(spot, first, gproj, att, gattn, sums)
    from_b, out_c, z_a = tie((from_b, out_c, z_a))
    plane_b, total_a = plane_sum(add_b, from_b), plane_a + z_a
    z_b = hop(jnp.concatenate([plane_b, blocks[2], blocks[3]], axis=0), 0, 0, 2)
    r_a, add_c = hop(total_a, 0, 0, 1), over_core(*out_c, dps)[:, :, : tall + 2]
    from_c = plane_parts(add_c, hop)
    from_c, z_b, r_a = tie((from_c, z_b, r_a))
    pieces = (z_b.shape[0] - tall) // 2
    z_b, from_z, through_z = z_b[:tall], z_b[tall : tall + pieces], z_b[tall + pieces :]
    plane_c, total_b = plane_sum(add_c, from_c), plane_b + z_b
    mid = tall // 2
    top, bottom = total_b[:mid], total_b[mid:]
    z_c, y_a = hop(plane_c, 0, 0, 2), hop(jnp.stack([total_a, r_a]), 0, 1, 0)
    r_top, y_bottom = hop(top, 0, 0, 1), hop(jnp.concatenate([bottom, blocks[1], through_z], axis=0), 0, 1, 0)
    z_c, y_a, r_top, y_bottom = tie((z_c, y_a, r_top, y_bottom))
    y_bottom, from_y, from_both = y_bottom[:mid], y_bottom[mid : mid + pieces], y_bottom[mid + pieces :]
    back = [blocks[0], from_y, from_z, from_both]
    rest = all_parts(plane_c + z_c, hop)
    y_top = hop(jnp.stack([top, r_top]), 0, 1, 0)
    r_bottom = hop(jnp.stack([bottom, y_bottom]), 0, 0, 1)
    stacked = lambda a, b: jnp.concatenate([a, b], axis=0)
    con = total_a, y_a[0], r_a, y_a[1]
    exp = total_b, stacked(y_top[0], y_bottom), stacked(r_top, r_bottom[0]), stacked(y_top[1], r_bottom[1])
    con, att_part = in_order(con, y, r), in_order([p[:tall] for p in rest], y, r)
    g_con = jnp.concatenate([con[0][0], con[0][1], con[1][0], con[1][1]], axis=0)
    wide = gproj.shape[1] // 2
    side = lambda a, b: jnp.concatenate(
        [jnp.concatenate([att_part[0][j][:, a:b], att_part[1][j][:, a:b]], axis=1) for j in (0, 1)], axis=0
    )
    g_qkv, g_out, last_b = tie((side(0, wide), side(wide, cols), exp[0]))
    exp = in_order((last_b,) + exp[1:], y, r)
    g_exp = jnp.concatenate([jnp.concatenate([exp[0][j], exp[1][j]], axis=1) for j in (0, 1)], axis=0)
    g_con, vectors = tie((g_con, rest[0][tall:]))
    vectors = vectors.astype(F32)
    windows = vectors[0].reshape(6, -1)
    quarter = width // 4
    windows = jnp.where(core == 0, windows[:, :quarter], windows[:, 64 : 64 + quarter])
    v = [windows[i] for i in range(6)] + [vectors[1, : 2 * quarter], vectors[1, 2 * quarter : 2 * quarter + ff // 4]]
    return g_qkv, g_out, g_exp, g_con, v, back


def solution(mesh):
    tok = P(None, "dp", "section", None)
    return jax.shard_map(
        body,
        mesh=mesh,
        in_specs=(tok, P(None, "dp", None), tok) + (P(),) * 12,
        out_specs=(
            tok, tok, P("dp"), P("dp"), P("dp", None), P("dp"), P("dp", None), P("dp"),
            P("dp"), P("dp"), P("dp", None), P("dp"), P("dp", None), P("dp"),
        ),
        check_vma=False,
    )
```

```python
from functools import partial

import jax
import jax.numpy as jnp
from jax import lax
from jax.experimental import pallas as pl
from jax.experimental.pallas import tpu as pltpu
from jax.sharding import PartitionSpec as P

HEAD_DIM = 64
EPSILON = 1e-05
SCORE_SCALE = 0.125
MASKED = -1e30
GELU_A = 0.7978845608028654
GELU_B = 0.044715
BF = jnp.bfloat16
F32 = jnp.float32
AXES = ("section", "dp")
VMEM_LIMIT = 60 * 2**20


def nn(left, right):
    return jnp.dot(left, right, preferred_element_type=F32)


def nt(left, right):
    return lax.dot_general(left, right, (((1,), (1,)), ((), ())), preferred_element_type=F32)


def tn(left, right):
    return lax.dot_general(left, right, (((0,), (0,)), ((), ())), preferred_element_type=F32)


def normed_of(values):
    center = values - jnp.mean(values, axis=-1, keepdims=True)
    inverse = lax.rsqrt(jnp.mean(center * center, axis=-1, keepdims=True) + EPSILON)
    return center * inverse, inverse


def norm_back(upstream, normed, inverse, gain_row):
    scaled = upstream * gain_row
    return inverse * (
        scaled
        - jnp.mean(scaled, axis=-1, keepdims=True)
        - normed * jnp.mean(scaled * normed, axis=-1, keepdims=True)
    )


def row_of(ref):
    return ref[...].reshape(1, -1)


def lane_split(pair):
    lane = lax.broadcasted_iota(jnp.int32, pair.shape, 1)
    zero = jnp.zeros_like(pair)
    return jnp.where(lane < HEAD_DIM, pair, zero), jnp.where(lane < HEAD_DIM, zero, pair)


def forward_kernel(
    lens_ref, spot_ref, x_ref, g1_ref, b1_ref, qvb_ref, obias_ref, g2_ref, b2_ref, ebias_ref, cbias_ref,
    wq_hbm, wo_hbm, we_hbm, wc_hbm,
    first_ref, n1_ref, proj_ref, probs_ref, att_ref, n2_ref, second_ref, slope_ref, act_ref,
    inv_ref, wqot_ref, wet_ref, wct_ref, last_ref, h_scr, mask_scr, wqo_scr, we_ref, wc_ref, sems,
):
    step = pl.program_id(0)
    rows, width = h_scr.shape
    pairs = width // 128
    ff = we_ref.shape[1]
    loads = [
        pltpu.make_async_copy(wq_hbm, wqo_scr.at[:, 0 : 3 * width], sems.at[0]),
        pltpu.make_async_copy(wo_hbm, wqo_scr.at[:, 3 * width : 4 * width], sems.at[1]),
        pltpu.make_async_copy(we_hbm, we_ref, sems.at[2]),
        pltpu.make_async_copy(wc_hbm, wc_ref, sems.at[3]),
    ]

    @pl.when(step == 0)
    def _():
        for load in loads:
            load.start()
        h_scr[...] = x_ref[...].astype(F32)
        query = lax.broadcasted_iota(jnp.int32, (rows, rows), 0)
        key = lax.broadcasted_iota(jnp.int32, (rows, rows), 1)
        own_q = jnp.zeros((rows, rows), jnp.int32)
        own_k = jnp.zeros((rows, rows), jnp.int32)
        slots = lens_ref.shape[1]
        end = jnp.int32(0)
        for slot in range(slots):
            end = end + lens_ref[spot_ref[4], slot]
            own_q += (query >= end).astype(jnp.int32)
            own_k += (key >= end).astype(jnp.int32)
        mask_scr[...] = jnp.where((own_q == own_k) & (key <= query), 0.0, MASKED)
        loads[0].wait()
        loads[1].wait()

    strip = wqot_ref.shape[0]
    at = pl.multiple_of(jnp.minimum(step, 4 * width // strip - 1) * strip, 128)
    wqot_ref[...] = wqo_scr[:, pl.ds(at, strip)].T
    h = h_scr[...]
    n1, inv1 = normed_of(h)
    first_low = (n1 * row_of(g1_ref) + row_of(b1_ref)).astype(BF)
    first_ref[0] = first_low
    n1_ref[0] = n1.astype(BF)
    raw = nn(first_low, wqo_scr[:, 0 : 3 * width])
    queries = ((raw[:, :width] + row_of(qvb_ref)[:, :width]) * SCORE_SCALE).astype(BF)
    keys = raw[:, width : 2 * width].astype(BF)
    values = (raw[:, 2 * width :] + row_of(qvb_ref)[:, width:]).astype(BF)
    proj_ref[0, :, 0:width] = queries
    proj_ref[0, :, width : 2 * width] = keys
    proj_ref[0, :, 2 * width : 3 * width] = values
    mask = mask_scr[...]
    mask = jnp.concatenate([mask, mask], axis=0)
    cuts = [slice(128 * p, 128 * (p + 1)) for p in range(pairs)]
    scores = [nt(jnp.concatenate(lane_split(queries[:, cut]), axis=0), keys[:, cut]) + mask for cut in cuts]
    tops = [jnp.max(s, axis=-1, keepdims=True) for s in scores]
    weights = [jnp.exp(s - t) for s, t in zip(scores, tops)]
    sums = [1.0 / jnp.sum(w, axis=-1, keepdims=True) for w in weights]
    lows = [(w * t).astype(BF) for w, t in zip(weights, sums)]
    outs = []
    for p, (low, cut) in enumerate(zip(lows, cuts)):
        probs_ref[0, 2 * rows * p : 2 * rows * (p + 1), :] = low
        both = jnp.concatenate([low[:rows], low[rows:]], axis=1)
        outs.append(nn(both, jnp.concatenate(lane_split(values[:, cut]), axis=0)).astype(BF))
    attended = jnp.concatenate(outs, axis=1)
    att_ref[0] = attended
    middle = h + (nn(attended, wqo_scr[:, 3 * width : 4 * width]) + row_of(obias_ref))
    n2, inv2 = normed_of(middle)
    second_low = (n2 * row_of(g2_ref) + row_of(b2_ref)).astype(BF)
    second_ref[0] = second_low
    n2_ref[0] = n2.astype(BF)
    inv_ref[0] = jnp.concatenate(
        [jnp.broadcast_to(inv1, (rows, 128)), jnp.broadcast_to(inv2, (rows, 128))], axis=1
    )
    total = middle + row_of(cbias_ref)

    @pl.when(step == 0)
    def _():
        loads[2].wait()
        loads[3].wait()

    wet_ref[...] = we_ref[:, pl.ds(at, strip)].T
    wct_ref[...] = wc_ref[pl.ds(at, strip), :].T
    ebias = row_of(ebias_ref)
    chunk = 768
    cuts = [slice(chunk * j, chunk * (j + 1)) for j in range(ff // chunk)]
    expand = lambda cut: nn(second_low, we_ref[:, cut]) + ebias[:, cut]
    pres = [expand(cuts[0])]
    for j, cols in enumerate(cuts):
        if j + 1 < len(cuts):
            pres.append(expand(cuts[j + 1]))
        pre = pres[j]
        square = pre * pre
        half = 0.5 + 0.5 * jnp.tanh(pre * (GELU_A + GELU_A * GELU_B * square))
        act = pre * half
        slope = half + act * (1.0 - half) * (2.0 * GELU_A + 6.0 * GELU_A * GELU_B * square)
        act = act.astype(BF)
        slope_ref[0, :, cols] = slope.astype(BF)
        act_ref[0, :, cols] = act
        total = total + nn(act, wc_ref[cols, :])
    low_out = total.astype(BF)
    h_scr[...] = low_out.astype(F32)

    @pl.when(step == pl.num_programs(0) - 1)
    def _():
        last_ref[...] = low_out


def fold(values):
    return jnp.sum(values.reshape(-1, 8, values.shape[-1]), axis=0)


def backward_kernel(
    spot_ref, cot_ref, g1_ref, g2_ref, wqot_hbm, wet_hbm, wct_hbm,
    n1_ref, proj_ref, probs_ref, n2_ref, slope_ref, inv_ref, *refs, fused,
):
    if fused:
        act_hbm, refs = refs[0], refs[1:]
    gproj_ref, gattn_ref, gpre_ref, gtok_ref, sums_ref, *refs = refs
    if fused:
        give_ref, keep_ref, *refs = refs
    else:
        gmlp_ref, *refs = refs
    g_scr, s768_scr, s2304_scr, s3072_scr, wqot_ref, wet_ref, wct_ref, sems, *refs = refs
    if fused:
        act_scr, gmlp_scr, tile_scr = refs
    step = pl.program_id(0)
    rows, width = g_scr.shape
    pairs = width // 128
    ff = wct_ref.shape[1]

    loads = [
        pltpu.make_async_copy(wct_hbm, wct_ref, sems.at[0]),
        pltpu.make_async_copy(wet_hbm, wet_ref, sems.at[1]),
        pltpu.make_async_copy(wqot_hbm, wqot_ref, sems.at[2]),
    ]

    if fused:
        x, c, r = spot_ref[0], spot_ref[1], spot_ref[3]
        tall = act_scr.shape[1] // 4
        for i in range(4):
            block = (((i & 1) ^ x) * 2 + ((1 - (i >> 1)) ^ c)) * 2 + r
            source = act_hbm.at[:, pl.ds(pl.multiple_of(block * tall, 128), tall)]
            loads.append(pltpu.make_async_copy(source, act_scr.at[:, tall * i : tall * (i + 1)], sems.at[3 + i]))

    @pl.when(step == 0)
    def _():
        for load in loads:
            load.start()
        g_scr[...] = cot_ref[...].astype(F32)
        s768_scr[...] = jnp.zeros_like(s768_scr)
        s2304_scr[...] = jnp.zeros_like(s2304_scr)
        s3072_scr[...] = jnp.zeros_like(s3072_scr)
        loads[0].wait()
        loads[1].wait()

    g = g_scr[...]
    gmlp = g.astype(BF)
    if fused:
        layer = pl.num_programs(0) - 1 - step
        gmlp_scr[pl.ds(pl.multiple_of(layer * rows, rows), rows), :] = gmlp
    else:
        gmlp_ref[0] = gmlp
    gsec = jnp.zeros((rows, width), F32)
    chunk = 1024
    for j in range(ff // chunk):
        cols = slice(chunk * j, chunk * (j + 1))
        gpre = (nn(gmlp, wct_ref[:, cols]) * slope_ref[0, :, cols].astype(F32)).astype(BF)
        gpre_ref[0, :, cols] = gpre
        s3072_scr[:, cols] += fold(gpre.astype(F32))
        gsec = gsec + nn(gpre, wet_ref[cols, :])
    n2 = n2_ref[0].astype(F32)
    gmid = g + norm_back(gsec, n2, inv_ref[0, :, 128:129], row_of(g2_ref))
    gattn = gmid.astype(BF)
    gattn_ref[0] = gattn

    @pl.when(step == 0)
    def _():
        loads[2].wait()

    gatt = nn(gattn, wqot_ref[3 * width : 4 * width, :]).astype(BF)
    dqs, dks, dvs = [], [], []
    outs2, gprobs = [], []
    for p in range(pairs):
        v = proj_ref[0, :, 2 * width + 128 * p : 2 * width + 128 * (p + 1)]
        out2 = jnp.concatenate(lane_split(gatt[:, 128 * p : 128 * (p + 1)]), axis=0)
        outs2.append(out2)
        gprobs.append(nt(out2, v))
    gscores = []
    for p in range(pairs):
        prob = probs_ref[0, 2 * rows * p : 2 * rows * (p + 1), :].astype(F32)
        gs = prob * (gprobs[p] - jnp.sum(prob * gprobs[p], axis=-1, keepdims=True))
        gscores.append(gs.astype(BF))
    for p in range(pairs):
        q = proj_ref[0, :, 128 * p : 128 * (p + 1)]
        k = proj_ref[0, :, width + 128 * p : width + 128 * (p + 1)]
        gscore = gscores[p]
        low = probs_ref[0, 2 * rows * p : 2 * rows * (p + 1), :]
        both = jnp.concatenate([gscore[:rows], gscore[rows:]], axis=1)
        k2 = jnp.concatenate(lane_split(k), axis=0)
        q2 = jnp.concatenate(lane_split(q), axis=0)
        dqs.append((nn(both, k2) * SCORE_SCALE).astype(BF))
        kv = tn(jnp.concatenate([gscore, low], axis=1), jnp.concatenate([q2, outs2[p]], axis=1))
        dks.append(kv[:rows, :128].astype(BF))
        dvs.append(kv[rows:, 128:].astype(BF))
    gproj = jnp.concatenate(dqs + dks + dvs, axis=1)
    gproj_ref[0] = gproj
    gfirst = nn(gproj, wqot_ref[0 : 3 * width, :])
    n1 = n1_ref[0].astype(F32)
    gin = gmid + norm_back(gfirst, n1, inv_ref[0, :, 0:1], row_of(g1_ref))
    s768_scr[0] += fold(gfirst * n1)
    s768_scr[1] += fold(gfirst)
    s768_scr[2] += fold(gattn.astype(F32))
    s768_scr[3] += fold(gsec * n2)
    s768_scr[4] += fold(gsec)
    s768_scr[5] += fold(gmlp.astype(F32))
    s2304_scr[...] += fold(gproj.astype(F32))
    low_out = gin.astype(BF)
    g_scr[...] = low_out.astype(F32)

    @pl.when(step == pl.num_programs(0) - 1)
    def _():
        gtok_ref[...] = low_out
        row = lambda v: jnp.sum(v, axis=0, keepdims=True)
        for i in range(6):
            sums_ref[i : i + 1, 0:width] = row(s768_scr[i])
        sums_ref[6:7, 0:width] = row(s2304_scr[:, 0:width])
        sums_ref[6:7, width : 2 * width] = row(s2304_scr[:, 2 * width : 3 * width])
        sums_ref[7:8, :] = row(s3072_scr[...])
        if fused:
            y = spot_ref[2]
            for load in loads[3:]:
                load.wait()
            for out, at in ((give_ref, 0), (keep_ref, 2 * tall)):
                tile_scr[...] = tn(act_scr[:, at : at + 2 * tall], gmlp_scr[...]).astype(BF)
                for xrel in (0, 1):
                    for yrel in (0, 1):
                        start = pl.multiple_of(xrel * tall + (y ^ yrel) * (tall // 2), 16)
                        out[xrel, yrel] = tile_scr[pl.ds(start, tall // 2), :]


def whole_spec(shape):
    zeros = (0,) * len(shape)
    return pl.BlockSpec(shape, lambda i, *_: zeros, pipeline_mode=pl.Buffered(1))


def forward_all(lens, spot, x, rows_in, wq, wo, we, wc, layers):
    rows, width = x.shape
    ff = we.shape[1]
    pairs = width // 128
    strip = ff // 8
    stack = lambda cols, r=rows, t=BF: jax.ShapeDtypeStruct((layers, r, cols), t)
    outs = [
        stack(width), stack(width), stack(3 * width), stack(rows, 2 * rows * pairs), stack(width),
        stack(width), stack(width), stack(ff), stack(ff), stack(256, rows, F32),
    ]
    per_layer = lambda s: pl.BlockSpec((1,) + s.shape[1:], lambda i, *_: (i, 0, 0))
    turned = [jax.ShapeDtypeStruct(s, BF) for s in ((4 * width, width), (ff, width), (width, ff))]
    by_rows = pl.BlockSpec((strip, width), lambda i, *_: (jnp.minimum(i, 7), 0))
    by_cols = pl.BlockSpec((width, strip), lambda i, *_: (0, jnp.minimum(i, 7)))
    last = jax.ShapeDtypeStruct((rows, width), BF)
    return pl.pallas_call(
        forward_kernel,
        grid_spec=pltpu.PrefetchScalarGridSpec(
            num_scalar_prefetch=2,
            grid=(layers,),
            in_specs=[whole_spec(a.shape) for a in (x, *rows_in)]
            + [pl.BlockSpec(memory_space=pl.ANY)] * 4,
            out_specs=[per_layer(s) for s in outs] + [by_rows, by_rows, by_cols, whole_spec(last.shape)],
            scratch_shapes=[
                pltpu.VMEM((rows, width), F32),
                pltpu.VMEM((rows, rows), F32),
                pltpu.VMEM((width, 4 * width), BF),
                pltpu.VMEM((width, ff), BF),
                pltpu.VMEM((ff, width), BF),
                pltpu.SemaphoreType.DMA((4,)),
            ],
        ),
        out_shape=outs + turned + [last],
        compiler_params=pltpu.CompilerParams(vmem_limit_bytes=VMEM_LIMIT),
    )(lens, spot, x, *rows_in, wq, wo, we, wc)


def backward_all(spot, cot, g1, g2, wqot, wet, wct, n1, proj, probs, n2, slope, inv, act=None):
    layers, rows, width = n1.shape
    ff = wct.shape[1]
    fused = act is not None
    stack = lambda cols: jax.ShapeDtypeStruct((layers, rows, cols), BF)
    outs = [stack(3 * width), stack(width), stack(ff)]
    per_layer = lambda s: pl.BlockSpec((1,) + s.shape[1:], lambda i, *_: (layers - 1 - i, 0, 0))
    last = [jax.ShapeDtypeStruct((rows, width), BF), jax.ShapeDtypeStruct((8, ff), F32)]
    out_specs = [per_layer(s) for s in outs] + [whole_spec(s.shape) for s in last]
    more_in, more_scratch = [], []
    if fused:
        more_in = [act]
        last += [parts_of(ff // 16, width)] * 2
        out_specs += [whole_spec(last[-1].shape)] * 2
        more_scratch = [
            pltpu.VMEM((layers * rows, ff // 2), BF),
            pltpu.VMEM((layers * rows, width), BF),
            pltpu.VMEM((ff // 4, width), BF),
        ]
    else:
        last.append(stack(width))
        out_specs.append(per_layer(last[-1]))
    return pl.pallas_call(
        partial(backward_kernel, fused=fused),
        grid_spec=pltpu.PrefetchScalarGridSpec(
            num_scalar_prefetch=1,
            grid=(layers,),
            in_specs=[whole_spec(a.shape) for a in (cot, g1, g2)]
            + [pl.BlockSpec(memory_space=pl.ANY)] * 3
            + [per_layer(a) for a in (n1, proj, probs, n2, slope, inv)]
            + [pl.BlockSpec(memory_space=pl.ANY)] * len(more_in),
            out_specs=out_specs,
            scratch_shapes=[
                pltpu.VMEM((rows, width), F32),
                pltpu.VMEM((6, 8, width), F32),
                pltpu.VMEM((8, 3 * width), F32),
                pltpu.VMEM((8, ff), F32),
                pltpu.VMEM((4 * width, width), BF),
                pltpu.VMEM((ff, width), BF),
                pltpu.VMEM((width, ff), BF),
                pltpu.SemaphoreType.DMA((7,)),
            ]
            + more_scratch,
        ),
        out_shape=outs + last,
        compiler_params=pltpu.CompilerParams(vmem_limit_bytes=VMEM_LIMIT),
    )(spot, cot, g1, g2, wqot, wet, wct, n1, proj, probs, n2, slope, inv, *more_in)


def outer_kernel(spot_ref, left_ref, right_ref, give_ref, keep_ref, scr, *, tall):
    scr[...] = tn(left_ref[...], right_ref[...]).astype(BF)
    split_out(spot_ref, scr, give_ref, keep_ref, 0, scr.shape[1], tall)


def split_out(spot_ref, scr, give_ref, keep_ref, at, cols, tall):
    x, c, y = spot_ref[0], spot_ref[1], spot_ref[2]
    for crel in (1, 0):
        out = give_ref if crel else keep_ref
        for xrel in (0, 1):
            for yrel in (0, 1):
                part = ((x ^ xrel) * 2 + (c ^ crel)) * 2 + (y ^ yrel)
                start = pl.multiple_of(part * tall, tall)
                out[xrel, yrel, 0:tall, at : at + cols] = scr[pl.ds(start, tall), :]


def parts_of(rows, cols):
    return jax.ShapeDtypeStruct((2, 2, rows, cols), BF)


def expand_grads(spot, left, right, tile=768):
    depth, width = left.shape
    half = right.shape[1] // 2
    steps = half // tile
    out = parts_of(width // 8, half)
    out_spec = pl.BlockSpec((2, 2, width // 8, tile), lambda j, s: (0, 0, 0, j))
    return pl.pallas_call(
        partial(outer_kernel, tall=width // 8),
        grid_spec=pltpu.PrefetchScalarGridSpec(
            num_scalar_prefetch=1,
            grid=(steps,),
            in_specs=[
                pl.BlockSpec((depth, width), lambda j, s: (0, 0)),
                pl.BlockSpec((depth, tile), lambda j, s: (0, s[3] * steps + j)),
            ],
            out_specs=[out_spec, out_spec],
            scratch_shapes=[pltpu.VMEM((width, tile), BF)],
        ),
        out_shape=[out, out],
        cost_estimate=cost_of(depth, width, half),
        compiler_params=pltpu.CompilerParams(vmem_limit_bytes=VMEM_LIMIT),
    )(spot, left, right)


def cost_of(depth, rows, cols):
    return pl.CostEstimate(
        flops=2 * depth * rows * cols, transcendentals=0, bytes_accessed=2 * depth * (rows + cols) + 2 * rows * cols
    )


def attention_kernel(
    spot_ref, first_ref, gproj_ref, att_ref, gattn_ref, sums_ref, give_ref, keep_ref, qkv_scr, out_scr,
):
    tall = qkv_scr.shape[0] // 8
    wide = qkv_scr.shape[1]
    qkv_scr[...] = tn(first_ref[...], gproj_ref[...]).astype(BF)
    split_out(spot_ref, qkv_scr, give_ref, keep_ref, 0, wide, tall)
    out_scr[...] = tn(att_ref[...], gattn_ref[...]).astype(BF)
    split_out(spot_ref, out_scr, give_ref, keep_ref, wide, out_scr.shape[1], tall)
    x, c = spot_ref[0], spot_ref[1]
    width, cols = qkv_scr.shape[0], give_ref.shape[3]
    for crel, out in ((1, give_ref), (0, keep_ref)):
        for xrel in (0, 1):
            place = (x ^ xrel) * 2 + (c ^ crel)
            window = lambda i, start, size: sums_ref[i : i + 1, pl.ds(pl.multiple_of(start, 128), size)]
            low = ((place * 3) >> 1) * 128
            singles = [window(i, low, 256) for i in range(6)]
            doubles = [window(6, place * (width // 2), width // 2), window(7, place * width, width)]
            used = (width // 2) * 3
            doubles.append(jnp.zeros((1, cols - used), F32))
            block = jnp.concatenate(
                [
                    jnp.concatenate(singles, axis=1),
                    jnp.concatenate(doubles, axis=1),
                    jnp.zeros((14, cols), F32),
                ],
                axis=0,
            ).astype(BF)
            for yrel in (0, 1):
                out[xrel, yrel, tall : tall + 16, :] = block


def attention_grads(spot, first, gproj, att, gattn, sums):
    depth, width = first.shape
    wide, thin = gproj.shape[1] // 2, gattn.shape[1] // 2
    out = parts_of(width // 8 + 16, wide + thin)
    whole = lambda shape: pl.BlockSpec(shape, lambda i, s: (0,) * len(shape))
    half = lambda cols: pl.BlockSpec((depth, cols), lambda i, s: (0, s[3]))
    return pl.pallas_call(
        attention_kernel,
        grid_spec=pltpu.PrefetchScalarGridSpec(
            num_scalar_prefetch=1,
            grid=(1,),
            in_specs=[
                whole(first.shape), half(wide), whole(att.shape), half(thin), whole(sums.shape),
            ],
            out_specs=[whole(out.shape), whole(out.shape)],
            scratch_shapes=[pltpu.VMEM((width, wide), BF), pltpu.VMEM((width, thin), BF)],
        ),
        out_shape=[out, out],
        cost_estimate=cost_of(depth, width, wide + thin),
        compiler_params=pltpu.CompilerParams(vmem_limit_bytes=VMEM_LIMIT),
    )(spot, first, gproj, att, gattn, sums)


def xor_order(stacked, flips):
    count = stacked.shape[0]
    rest = stacked.shape[1:]
    bit = 1
    while bit < count:
        split = stacked.reshape((count // (2 * bit), 2, bit) + rest)
        split = jnp.where((flips & bit) != 0, split[:, ::-1], split)
        stacked = split.reshape((count,) + rest)
        bit *= 2
    return stacked


def label_of(section):
    return (section & ~3) | ((section & 1) << 1) | ((section >> 1) & 1)


def by_label(k, sections):
    return [(s, label_of(label_of(s) ^ k)) for s in range(sections)]


def move(array, flip_x, flip_y, flip_z, sections, dps):
    flip = flip_z * 2 + flip_y
    pairs = [
        (s * dps + d, (s ^ flip) * dps + (d ^ (flip_x * 2))) for s in range(sections) for d in range(dps)
    ]
    return lax.ppermute(array, AXES, pairs)


def over_core(give, keep, dps):
    return keep + lax.ppermute(give, "dp", [(d, d ^ 1) for d in range(dps)])


def plane_parts(both, hop):
    return [hop(both[1, 0], 1, 0, 0), hop(both[0, 1], 0, 1, 0), hop(both[1, 1], 1, 1, 0)]


def plane_sum(both, parts):
    return (both[0, 0].astype(F32) + parts[0] + parts[1] + parts[2]).astype(BF)


def all_parts(total, hop):
    return total, hop(total, 0, 1, 0), hop(total, 0, 0, 1), hop(total, 0, 1, 1)


def in_order(pieces, y, r):
    own, other_y, other_r, other_both = (p.astype(F32) for p in pieces)
    low = jnp.where(y == 0, own, other_y), jnp.where(y == 0, other_y, own)
    high = jnp.where(y == 0, other_r, other_both), jnp.where(y == 0, other_both, other_r)
    pick = lambda a, b: jnp.where(r == 0, a, b)
    return (
        (pick(low[0], high[0]), pick(low[1], high[1])),
        (pick(high[0], low[0]), pick(high[1], low[1])),
    )


def body(
    tokens, lengths, cotangent, first_gain, first_shift, qkv_weight, qv_bias, out_weight, out_bias,
    second_gain, second_shift, expand_weight, expand_bias, contract_weight, contract_bias,
):
    sections, dps = lax.axis_size("section"), lax.axis_size("dp")
    section, dp = lax.axis_index("section"), lax.axis_index("dp")
    micro, _, piece_rows, width = tokens.shape
    rows = piece_rows * sections
    ff = expand_weight.shape[1]
    label = label_of(section)

    sent = jnp.concatenate([tokens[:, 0], cotangent[:, 0]], axis=-1)
    got = []
    for k in range(sections):
        block = lax.dynamic_index_in_dim(sent, (label ^ k) >> 1, 0, keepdims=False)
        got.append(block if k == 0 else lax.ppermute(block, "section", by_label(k, sections)))
    shard = xor_order(jnp.stack(got), label)
    shard = shard.reshape(sections // 4, 2, 2, piece_rows, 2 * width).swapaxes(1, 2).reshape(rows, 2 * width)
    x, cot = shard[:, :width], shard[:, width:]
    spot = jnp.stack([(dp >> 1) & 1, dp & 1, section & 1, (section >> 1) & 1, label >> 1]).astype(jnp.int32)
    first, n1, proj, probs, att, n2, second, slope, act, inv, wqot, wet, wct, last = forward_all(
        lengths[:, 0], spot, x,
        [first_gain, first_shift, qv_bias, out_bias, second_gain, second_shift, expand_bias, contract_bias],
        qkv_weight, out_weight, expand_weight, contract_weight, sections,
    )
    flat = lambda a: a.reshape(-1, a.shape[-1])
    first, att, second, act = flat(first), flat(att), flat(second), flat(act)
    known = (sections, dps) == (8, 4)
    gproj, gattn, gpre, gtok, sums, *contract = backward_all(
        spot, cot, first_gain, second_gain, wqot, wet, wct, n1, proj, probs, n2, slope, inv,
        act if known else None,
    )
    gproj, gattn, gpre = flat(gproj), flat(gattn), flat(gpre)
    both = jnp.concatenate([last, gtok], axis=1).reshape(sections, piece_rows, 2 * width)
    blocks = [
        lax.dynamic_index_in_dim(both, label_of(label ^ k), 0, keepdims=False) for k in range(0, sections, 2)
    ]
    if known:
        g_qkv, g_out, g_exp, g_con, v, back = grads_small_slice(
            section, dp, spot, first, att, second, gproj, gattn, gpre, contract, sums, blocks
        )
    else:
        half = (label & 1) == 0

        def everywhere(whole):
            whole = jnp.where(half, whole, 0.0).astype(BF)
            own = lax.psum_scatter(whole, "dp", scatter_dimension=0, tiled=True)
            return lax.psum(own, "section").astype(F32)

        g_qkv, g_out = everywhere(tn(first, gproj)), everywhere(tn(att, gattn))
        g_exp, g_con = everywhere(tn(second, gpre)), everywhere(tn(act, flat(contract[0])))
        v = [everywhere(sums[i, :n]) for i, n in enumerate([width] * 6 + [2 * width, ff])]
        back = blocks[:1] + [
            lax.ppermute(block, "section", by_label(2 * i + 2, sections)) for i, block in enumerate(blocks[1:])
        ]

    back = xor_order(jnp.stack(back), label >> 1)
    result = back[:, None, :, :width]
    grad_tokens = back[:, None, :, width:].astype(F32)
    return (
        result, grad_tokens, v[0], v[1], g_qkv, v[6], g_out, v[2], v[3], v[4], g_exp, v[7], g_con, v[5],
    )


def grads_small_slice(section, dp, spot, first, att, second, gproj, gattn, gpre, contract, sums, blocks):
    sections, dps = 8, 4
    y, r, core = section & 1, (section >> 1) & 1, dp & 1
    width, ff = first.shape[1], gpre.shape[1]
    hop = partial(move, sections=sections, dps=dps)
    cols = 2 * width
    tall = width // 8
    tie = lax.optimization_barrier
    add_a = over_core(*contract, dps)
    second, gpre, add_a = tie((second, gpre, add_a))
    from_a, out_b = plane_parts(add_a, hop), expand_grads(spot, second, gpre)
    from_a, out_b, blocks = tie((from_a, out_b, blocks))
    plane_a = plane_sum(add_a, from_a)
    z_a, add_b = hop(plane_a, 0, 0, 2), over_core(*out_b, dps)
    first, gproj, att, gattn, add_b = tie((first, gproj, att, gattn, add_b))
    from_b, out_c = plane_parts(add_b, hop), attention_grads(spot, first, gproj, att, gattn, sums)
    from_b, out_c, z_a = tie((from_b, out_c, z_a))
    plane_b, total_a = plane_sum(add_b, from_b), plane_a + z_a
    z_b = hop(jnp.concatenate([plane_b, blocks[2], blocks[3]], axis=0), 0, 0, 2)
    r_a, add_c = hop(total_a, 0, 0, 1), over_core(*out_c, dps)[:, :, : tall + 8]
    from_c = plane_parts(add_c, hop)
    from_c, z_b, r_a = tie((from_c, z_b, r_a))
    pieces = (z_b.shape[0] - tall) // 2
    z_b, from_z, through_z = z_b[:tall], z_b[tall : tall + pieces], z_b[tall + pieces :]
    plane_c, total_b = plane_sum(add_c, from_c), plane_b + z_b
    mid = tall // 2
    top, bottom = total_b[:mid], total_b[mid:]
    z_c, y_a = hop(plane_c, 0, 0, 2), hop(jnp.stack([total_a, r_a]), 0, 1, 0)
    r_top, y_bottom = hop(top, 0, 0, 1), hop(jnp.concatenate([bottom, blocks[1], through_z], axis=0), 0, 1, 0)
    z_c, y_a, r_top, y_bottom = tie((z_c, y_a, r_top, y_bottom))
    y_bottom, from_y, from_both = y_bottom[:mid], y_bottom[mid : mid + pieces], y_bottom[mid + pieces :]
    back = [blocks[0], from_y, from_z, from_both]
    rest = all_parts(plane_c + z_c, hop)
    y_top = hop(jnp.stack([top, r_top]), 0, 1, 0)
    r_bottom = hop(jnp.stack([bottom, y_bottom]), 0, 0, 1)
    con = total_a, y_a[0], r_a, y_a[1]
    con, att_part = in_order(con, y, r), in_order([p[:tall] for p in rest], y, r)
    g_con = jnp.concatenate([con[0][0], con[0][1], con[1][0], con[1][1]], axis=0)
    wide = gproj.shape[1] // 2
    side = lambda a, b: jnp.concatenate(
        [jnp.concatenate([att_part[0][j][:, a:b], att_part[1][j][:, a:b]], axis=1) for j in (0, 1)], axis=0
    )
    g_qkv, g_out, y_top, r_bottom = tie((side(0, wide), side(wide, cols), y_top, r_bottom))
    stacked = lambda a, b: jnp.concatenate([a, b], axis=0)
    exp = total_b, stacked(y_top[0], y_bottom), stacked(r_top, r_bottom[0]), stacked(y_top[1], r_bottom[1])
    exp = in_order(exp, y, r)
    g_exp = jnp.concatenate([jnp.concatenate([exp[0][j], exp[1][j]], axis=1) for j in (0, 1)], axis=0)
    g_con, vectors = tie((g_con, rest[0][tall:]))
    vectors = vectors.astype(F32)
    windows = vectors[0].reshape(6, -1)
    quarter = width // 4
    windows = jnp.where(core == 0, windows[:, :quarter], windows[:, 64 : 64 + quarter])
    v = [windows[i] for i in range(6)] + [vectors[1, : 2 * quarter], vectors[1, 2 * quarter : 2 * quarter + ff // 4]]
    return g_qkv, g_out, g_exp, g_con, v, back


def solution(mesh):
    tok = P(None, "dp", "section", None)
    return jax.shard_map(
        body,
        mesh=mesh,
        in_specs=(tok, P(None, "dp", None), tok) + (P(),) * 12,
        out_specs=(
            tok, tok, P("dp"), P("dp"), P("dp", None), P("dp"), P("dp", None), P("dp"),
            P("dp"), P("dp"), P("dp", None), P("dp"), P("dp", None), P("dp"),
        ),
        check_vma=False,
    )
```

```python
from functools import partial

import jax
import jax.numpy as jnp
from jax import lax
from jax.experimental import pallas as pl
from jax.experimental.pallas import tpu as pltpu
from jax.sharding import PartitionSpec as P

HEAD_DIM = 64
EPSILON = 1e-05
SCORE_SCALE = 0.125
MASKED = -1e30
GELU_A = 0.7978845608028654
GELU_B = 0.044715
BF = jnp.bfloat16
F32 = jnp.float32
AXES = ("section", "dp")
VMEM_LIMIT = 60 * 2**20


def nn(left, right):
    return jnp.dot(left, right, preferred_element_type=F32)


def nt(left, right):
    return lax.dot_general(left, right, (((1,), (1,)), ((), ())), preferred_element_type=F32)


def tn(left, right):
    return lax.dot_general(left, right, (((0,), (0,)), ((), ())), preferred_element_type=F32)


def normed_of(values):
    center = values - jnp.mean(values, axis=-1, keepdims=True)
    inverse = lax.rsqrt(jnp.mean(center * center, axis=-1, keepdims=True) + EPSILON)
    return center * inverse, inverse


def norm_back(upstream, normed, inverse, gain_row):
    scaled = upstream * gain_row
    return inverse * (
        scaled
        - jnp.mean(scaled, axis=-1, keepdims=True)
        - normed * jnp.mean(scaled * normed, axis=-1, keepdims=True)
    )


def row_of(ref):
    return ref[...].reshape(1, -1)


def lane_split(pair):
    lane = lax.broadcasted_iota(jnp.int32, pair.shape, 1)
    zero = jnp.zeros_like(pair)
    return jnp.where(lane < HEAD_DIM, pair, zero), jnp.where(lane < HEAD_DIM, zero, pair)


def forward_kernel(
    lens_ref, spot_ref, x_ref, g1_ref, b1_ref, qvb_ref, obias_ref, g2_ref, b2_ref, ebias_ref, cbias_ref,
    wq_hbm, wo_hbm, we_hbm, wc_hbm,
    first_ref, n1_ref, proj_ref, probs_ref, att_ref, n2_ref, second_ref, slope_ref, act_ref,
    inv_ref, wqot_ref, wet_ref, wct_ref, last_ref, h_scr, mask_scr, wqo_scr, we_ref, wc_ref, sems,
):
    step = pl.program_id(0)
    rows, width = h_scr.shape
    pairs = width // 128
    ff = we_ref.shape[1]
    loads = [
        pltpu.make_async_copy(wq_hbm, wqo_scr.at[:, 0 : 3 * width], sems.at[0]),
        pltpu.make_async_copy(wo_hbm, wqo_scr.at[:, 3 * width : 4 * width], sems.at[1]),
        pltpu.make_async_copy(we_hbm, we_ref, sems.at[2]),
        pltpu.make_async_copy(wc_hbm, wc_ref, sems.at[3]),
    ]

    @pl.when(step == 0)
    def _():
        for load in loads:
            load.start()
        h_scr[...] = x_ref[...].astype(F32)
        query = lax.broadcasted_iota(jnp.int32, (rows, rows), 0)
        key = lax.broadcasted_iota(jnp.int32, (rows, rows), 1)
        own_q = jnp.zeros((rows, rows), jnp.int32)
        own_k = jnp.zeros((rows, rows), jnp.int32)
        slots = lens_ref.shape[1]
        end = jnp.int32(0)
        for slot in range(slots):
            end = end + lens_ref[spot_ref[4], slot]
            own_q += (query >= end).astype(jnp.int32)
            own_k += (key >= end).astype(jnp.int32)
        mask_scr[...] = jnp.where((own_q == own_k) & (key <= query), 0.0, MASKED)
        loads[0].wait()
        loads[1].wait()

    strip = wqot_ref.shape[0]
    at = pl.multiple_of(jnp.minimum(step, 4 * width // strip - 1) * strip, 128)
    wqot_ref[...] = wqo_scr[:, pl.ds(at, strip)].T
    h = h_scr[...]
    n1, inv1 = normed_of(h)
    first_low = (n1 * row_of(g1_ref) + row_of(b1_ref)).astype(BF)
    first_ref[0] = first_low
    n1_ref[0] = n1.astype(BF)
    raw = nn(first_low, wqo_scr[:, 0 : 3 * width])
    queries = ((raw[:, :width] + row_of(qvb_ref)[:, :width]) * SCORE_SCALE).astype(BF)
    keys = raw[:, width : 2 * width].astype(BF)
    values = (raw[:, 2 * width :] + row_of(qvb_ref)[:, width:]).astype(BF)
    proj_ref[0, :, 0:width] = queries
    proj_ref[0, :, width : 2 * width] = keys
    proj_ref[0, :, 2 * width : 3 * width] = values
    mask = mask_scr[...]
    mask = jnp.concatenate([mask, mask], axis=0)
    cuts = [slice(128 * p, 128 * (p + 1)) for p in range(pairs)]
    scores = [nt(jnp.concatenate(lane_split(queries[:, cut]), axis=0), keys[:, cut]) + mask for cut in cuts]
    tops = [jnp.max(s, axis=-1, keepdims=True) for s in scores]
    weights = [jnp.exp(s - t) for s, t in zip(scores, tops)]
    sums = [1.0 / jnp.sum(w, axis=-1, keepdims=True) for w in weights]
    lows = [(w * t).astype(BF) for w, t in zip(weights, sums)]
    outs = []
    for p, (low, cut) in enumerate(zip(lows, cuts)):
        probs_ref[0, 2 * rows * p : 2 * rows * (p + 1), :] = low
        both = jnp.concatenate([low[:rows], low[rows:]], axis=1)
        outs.append(nn(both, jnp.concatenate(lane_split(values[:, cut]), axis=0)).astype(BF))
    attended = jnp.concatenate(outs, axis=1)
    att_ref[0] = attended
    middle = h + (nn(attended, wqo_scr[:, 3 * width : 4 * width]) + row_of(obias_ref))
    n2, inv2 = normed_of(middle)
    second_low = (n2 * row_of(g2_ref) + row_of(b2_ref)).astype(BF)
    second_ref[0] = second_low
    n2_ref[0] = n2.astype(BF)
    inv_ref[0] = jnp.concatenate(
        [jnp.broadcast_to(inv1, (rows, 128)), jnp.broadcast_to(inv2, (rows, 128))], axis=1
    )
    total = middle + row_of(cbias_ref)

    @pl.when(step == 0)
    def _():
        loads[2].wait()
        loads[3].wait()

    wet_ref[...] = we_ref[:, pl.ds(at, strip)].T
    wct_ref[...] = wc_ref[pl.ds(at, strip), :].T
    ebias = row_of(ebias_ref)
    chunk = 768
    cuts = [slice(chunk * j, chunk * (j + 1)) for j in range(ff // chunk)]
    expand = lambda cut: nn(second_low, we_ref[:, cut]) + ebias[:, cut]
    pres = [expand(cuts[0])]
    for j, cols in enumerate(cuts):
        if j + 1 < len(cuts):
            pres.append(expand(cuts[j + 1]))
        pre = pres[j]
        square = pre * pre
        half = 0.5 + 0.5 * jnp.tanh(pre * (GELU_A + GELU_A * GELU_B * square))
        act = pre * half
        slope = half + act * (1.0 - half) * (2.0 * GELU_A + 6.0 * GELU_A * GELU_B * square)
        act = act.astype(BF)
        slope_ref[0, :, cols] = slope.astype(BF)
        act_ref[0, :, cols] = act
        total = total + nn(act, wc_ref[cols, :])
    low_out = total.astype(BF)
    h_scr[...] = low_out.astype(F32)

    @pl.when(step == pl.num_programs(0) - 1)
    def _():
        last_ref[...] = low_out


def fold(values):
    return jnp.sum(values.reshape(-1, 8, values.shape[-1]), axis=0)


def backward_kernel(
    spot_ref, cot_ref, g1_ref, g2_ref, wqot_hbm, wet_hbm, wct_hbm,
    n1_ref, proj_ref, probs_ref, n2_ref, slope_ref, inv_ref, *refs, fused,
):
    if fused:
        act_hbm, refs = refs[0], refs[1:]
    gproj_ref, gattn_ref, gpre_ref, gtok_ref, sums_ref, *refs = refs
    if fused:
        give_ref, keep_ref, *refs = refs
    else:
        gmlp_ref, *refs = refs
    g_scr, s768_scr, s2304_scr, s3072_scr, wqot_ref, wet_ref, wct_ref, sems, *refs = refs
    if fused:
        act_scr, gmlp_scr, tile_scr = refs
    step = pl.program_id(0)
    rows, width = g_scr.shape
    pairs = width // 128
    ff = wct_ref.shape[1]

    loads = [
        pltpu.make_async_copy(wct_hbm, wct_ref, sems.at[0]),
        pltpu.make_async_copy(wet_hbm, wet_ref, sems.at[1]),
        pltpu.make_async_copy(wqot_hbm, wqot_ref, sems.at[2]),
    ]

    if fused:
        x, c, r = spot_ref[0], spot_ref[1], spot_ref[3]
        tall = act_scr.shape[1] // 4
        for i in range(4):
            block = (((i & 1) ^ x) * 2 + ((1 - (i >> 1)) ^ c)) * 2 + r
            source = act_hbm.at[:, pl.ds(pl.multiple_of(block * tall, 128), tall)]
            loads.append(pltpu.make_async_copy(source, act_scr.at[:, tall * i : tall * (i + 1)], sems.at[3 + i]))

    @pl.when(step == 0)
    def _():
        for load in loads:
            load.start()
        g_scr[...] = cot_ref[...].astype(F32)
        s768_scr[...] = jnp.zeros_like(s768_scr)
        s2304_scr[...] = jnp.zeros_like(s2304_scr)
        s3072_scr[...] = jnp.zeros_like(s3072_scr)
        loads[0].wait()
        loads[1].wait()

    g = g_scr[...]
    gmlp = g.astype(BF)
    if fused:
        layer = pl.num_programs(0) - 1 - step
        gmlp_scr[pl.ds(pl.multiple_of(layer * rows, rows), rows), :] = gmlp
    else:
        gmlp_ref[0] = gmlp
    gsec = jnp.zeros((rows, width), F32)
    chunk = 1024
    for j in range(ff // chunk):
        cols = slice(chunk * j, chunk * (j + 1))
        gpre = (nn(gmlp, wct_ref[:, cols]) * slope_ref[0, :, cols].astype(F32)).astype(BF)
        gpre_ref[0, :, cols] = gpre
        s3072_scr[:, cols] += fold(gpre.astype(F32))
        gsec = gsec + nn(gpre, wet_ref[cols, :])
    n2 = n2_ref[0].astype(F32)
    gmid = g + norm_back(gsec, n2, inv_ref[0, :, 128:129], row_of(g2_ref))
    gattn = gmid.astype(BF)
    gattn_ref[0] = gattn

    @pl.when(step == 0)
    def _():
        loads[2].wait()

    gatt = nn(gattn, wqot_ref[3 * width : 4 * width, :]).astype(BF)
    dqs, dks, dvs = [], [], []
    outs2, gprobs = [], []
    for p in range(pairs):
        v = proj_ref[0, :, 2 * width + 128 * p : 2 * width + 128 * (p + 1)]
        out2 = jnp.concatenate(lane_split(gatt[:, 128 * p : 128 * (p + 1)]), axis=0)
        outs2.append(out2)
        gprobs.append(nt(out2, v))
    gscores = []
    for p in range(pairs):
        prob = probs_ref[0, 2 * rows * p : 2 * rows * (p + 1), :].astype(F32)
        gs = prob * (gprobs[p] - jnp.sum(prob * gprobs[p], axis=-1, keepdims=True))
        gscores.append(gs.astype(BF))
    for p in range(pairs):
        q = proj_ref[0, :, 128 * p : 128 * (p + 1)]
        k = proj_ref[0, :, width + 128 * p : width + 128 * (p + 1)]
        gscore = gscores[p]
        low = probs_ref[0, 2 * rows * p : 2 * rows * (p + 1), :]
        both = jnp.concatenate([gscore[:rows], gscore[rows:]], axis=1)
        k2 = jnp.concatenate(lane_split(k), axis=0)
        q2 = jnp.concatenate(lane_split(q), axis=0)
        dqs.append((nn(both, k2) * SCORE_SCALE).astype(BF))
        kv = tn(jnp.concatenate([gscore, low], axis=1), jnp.concatenate([q2, outs2[p]], axis=1))
        dks.append(kv[:rows, :128].astype(BF))
        dvs.append(kv[rows:, 128:].astype(BF))
    gproj = jnp.concatenate(dqs + dks + dvs, axis=1)
    gproj_ref[0] = gproj
    gfirst = nn(gproj, wqot_ref[0 : 3 * width, :])
    n1 = n1_ref[0].astype(F32)
    gin = gmid + norm_back(gfirst, n1, inv_ref[0, :, 0:1], row_of(g1_ref))
    s768_scr[0] += fold(gfirst * n1)
    s768_scr[1] += fold(gfirst)
    s768_scr[2] += fold(gattn.astype(F32))
    s768_scr[3] += fold(gsec * n2)
    s768_scr[4] += fold(gsec)
    s768_scr[5] += fold(gmlp.astype(F32))
    s2304_scr[...] += fold(gproj.astype(F32))
    low_out = gin.astype(BF)
    g_scr[...] = low_out.astype(F32)

    @pl.when(step == pl.num_programs(0) - 1)
    def _():
        gtok_ref[...] = low_out
        row = lambda v: jnp.sum(v, axis=0, keepdims=True)
        for i in range(6):
            sums_ref[i : i + 1, 0:width] = row(s768_scr[i])
        sums_ref[6:7, 0:width] = row(s2304_scr[:, 0:width])
        sums_ref[6:7, width : 2 * width] = row(s2304_scr[:, 2 * width : 3 * width])
        sums_ref[7:8, :] = row(s3072_scr[...])
        if fused:
            y = spot_ref[2]
            for load in loads[3:]:
                load.wait()
            for out, at in ((give_ref, 0), (keep_ref, 2 * tall)):
                tile_scr[...] = tn(act_scr[:, at : at + 2 * tall], gmlp_scr[...]).astype(BF)
                for xrel in (0, 1):
                    for yrel in (0, 1):
                        start = pl.multiple_of(xrel * tall + (y ^ yrel) * (tall // 2), 16)
                        out[xrel, yrel] = tile_scr[pl.ds(start, tall // 2), :]


def whole_spec(shape):
    zeros = (0,) * len(shape)
    return pl.BlockSpec(shape, lambda i, *_: zeros, pipeline_mode=pl.Buffered(1))


def forward_all(lens, spot, x, rows_in, wq, wo, we, wc, layers):
    rows, width = x.shape
    ff = we.shape[1]
    pairs = width // 128
    strip = ff // 8
    stack = lambda cols, r=rows, t=BF: jax.ShapeDtypeStruct((layers, r, cols), t)
    outs = [
        stack(width), stack(width), stack(3 * width), stack(rows, 2 * rows * pairs), stack(width),
        stack(width), stack(width), stack(ff), stack(ff), stack(256, rows, F32),
    ]
    per_layer = lambda s: pl.BlockSpec((1,) + s.shape[1:], lambda i, *_: (i, 0, 0))
    turned = [jax.ShapeDtypeStruct(s, BF) for s in ((4 * width, width), (ff, width), (width, ff))]
    by_rows = pl.BlockSpec((strip, width), lambda i, *_: (jnp.minimum(i, 7), 0))
    by_cols = pl.BlockSpec((width, strip), lambda i, *_: (0, jnp.minimum(i, 7)))
    last = jax.ShapeDtypeStruct((rows, width), BF)
    return pl.pallas_call(
        forward_kernel,
        grid_spec=pltpu.PrefetchScalarGridSpec(
            num_scalar_prefetch=2,
            grid=(layers,),
            in_specs=[whole_spec(a.shape) for a in (x, *rows_in)]
            + [pl.BlockSpec(memory_space=pl.ANY)] * 4,
            out_specs=[per_layer(s) for s in outs] + [by_rows, by_rows, by_cols, whole_spec(last.shape)],
            scratch_shapes=[
                pltpu.VMEM((rows, width), F32),
                pltpu.VMEM((rows, rows), F32),
                pltpu.VMEM((width, 4 * width), BF),
                pltpu.VMEM((width, ff), BF),
                pltpu.VMEM((ff, width), BF),
                pltpu.SemaphoreType.DMA((4,)),
            ],
        ),
        out_shape=outs + turned + [last],
        compiler_params=pltpu.CompilerParams(vmem_limit_bytes=VMEM_LIMIT),
    )(lens, spot, x, *rows_in, wq, wo, we, wc)


def backward_all(spot, cot, g1, g2, wqot, wet, wct, n1, proj, probs, n2, slope, inv, act=None):
    layers, rows, width = n1.shape
    ff = wct.shape[1]
    fused = act is not None
    stack = lambda cols: jax.ShapeDtypeStruct((layers, rows, cols), BF)
    outs = [stack(3 * width), stack(width), stack(ff)]
    per_layer = lambda s: pl.BlockSpec((1,) + s.shape[1:], lambda i, *_: (layers - 1 - i, 0, 0))
    last = [jax.ShapeDtypeStruct((rows, width), BF), jax.ShapeDtypeStruct((8, ff), F32)]
    out_specs = [per_layer(s) for s in outs] + [whole_spec(s.shape) for s in last]
    more_in, more_scratch = [], []
    if fused:
        more_in = [act]
        last += [parts_of(ff // 16, width)] * 2
        out_specs += [whole_spec(last[-1].shape)] * 2
        more_scratch = [
            pltpu.VMEM((layers * rows, ff // 2), BF),
            pltpu.VMEM((layers * rows, width), BF),
            pltpu.VMEM((ff // 4, width), BF),
        ]
    else:
        last.append(stack(width))
        out_specs.append(per_layer(last[-1]))
    return pl.pallas_call(
        partial(backward_kernel, fused=fused),
        grid_spec=pltpu.PrefetchScalarGridSpec(
            num_scalar_prefetch=1,
            grid=(layers,),
            in_specs=[whole_spec(a.shape) for a in (cot, g1, g2)]
            + [pl.BlockSpec(memory_space=pl.ANY)] * 3
            + [per_layer(a) for a in (n1, proj, probs, n2, slope, inv)]
            + [pl.BlockSpec(memory_space=pl.ANY)] * len(more_in),
            out_specs=out_specs,
            scratch_shapes=[
                pltpu.VMEM((rows, width), F32),
                pltpu.VMEM((6, 8, width), F32),
                pltpu.VMEM((8, 3 * width), F32),
                pltpu.VMEM((8, ff), F32),
                pltpu.VMEM((4 * width, width), BF),
                pltpu.VMEM((ff, width), BF),
                pltpu.VMEM((width, ff), BF),
                pltpu.SemaphoreType.DMA((7,)),
            ]
            + more_scratch,
        ),
        out_shape=outs + last,
        compiler_params=pltpu.CompilerParams(vmem_limit_bytes=VMEM_LIMIT),
    )(spot, cot, g1, g2, wqot, wet, wct, n1, proj, probs, n2, slope, inv, *more_in)


def outer_kernel(spot_ref, left_ref, right_ref, give_ref, keep_ref, scr, *, tall):
    scr[...] = tn(left_ref[...], right_ref[...]).astype(BF)
    split_out(spot_ref, scr, give_ref, keep_ref, 0, scr.shape[1], tall)


def split_out(spot_ref, scr, give_ref, keep_ref, at, cols, tall):
    x, c, y = spot_ref[0], spot_ref[1], spot_ref[2]
    for crel in (1, 0):
        out = give_ref if crel else keep_ref
        for xrel in (0, 1):
            for yrel in (0, 1):
                part = ((x ^ xrel) * 2 + (c ^ crel)) * 2 + (y ^ yrel)
                start = pl.multiple_of(part * tall, tall)
                out[xrel, yrel, 0:tall, at : at + cols] = scr[pl.ds(start, tall), :]


def parts_of(rows, cols):
    return jax.ShapeDtypeStruct((2, 2, rows, cols), BF)


def expand_grads(spot, left, right, tile=768):
    depth, width = left.shape
    half = right.shape[1] // 2
    steps = half // tile
    out = parts_of(width // 8, half)
    out_spec = pl.BlockSpec((2, 2, width // 8, tile), lambda j, s: (0, 0, 0, j))
    return pl.pallas_call(
        partial(outer_kernel, tall=width // 8),
        grid_spec=pltpu.PrefetchScalarGridSpec(
            num_scalar_prefetch=1,
            grid=(steps,),
            in_specs=[
                pl.BlockSpec((depth, width), lambda j, s: (0, 0)),
                pl.BlockSpec((depth, tile), lambda j, s: (0, s[3] * steps + j)),
            ],
            out_specs=[out_spec, out_spec],
            scratch_shapes=[pltpu.VMEM((width, tile), BF)],
        ),
        out_shape=[out, out],
        cost_estimate=cost_of(depth, width, half),
        compiler_params=pltpu.CompilerParams(vmem_limit_bytes=VMEM_LIMIT),
    )(spot, left, right)


def cost_of(depth, rows, cols):
    return pl.CostEstimate(
        flops=2 * depth * rows * cols, transcendentals=0, bytes_accessed=2 * depth * (rows + cols) + 2 * rows * cols
    )


def attention_kernel(
    spot_ref, first_ref, gproj_ref, att_ref, gattn_ref, sums_ref, give_ref, keep_ref, qkv_scr, out_scr,
):
    tall = qkv_scr.shape[0] // 8
    wide = qkv_scr.shape[1]
    qkv_scr[...] = tn(first_ref[...], gproj_ref[...]).astype(BF)
    split_out(spot_ref, qkv_scr, give_ref, keep_ref, 0, wide, tall)
    out_scr[...] = tn(att_ref[...], gattn_ref[...]).astype(BF)
    split_out(spot_ref, out_scr, give_ref, keep_ref, wide, out_scr.shape[1], tall)
    x, c = spot_ref[0], spot_ref[1]
    width, cols = qkv_scr.shape[0], give_ref.shape[3]
    for crel, out in ((1, give_ref), (0, keep_ref)):
        for xrel in (0, 1):
            place = (x ^ xrel) * 2 + (c ^ crel)
            window = lambda i, start, size: sums_ref[i : i + 1, pl.ds(pl.multiple_of(start, 128), size)]
            low = ((place * 3) >> 1) * 128
            singles = [window(i, low, 256) for i in range(6)]
            doubles = [window(6, place * (width // 2), width // 2), window(7, place * width, width)]
            used = (width // 2) * 3
            doubles.append(jnp.zeros((1, cols - used), F32))
            block = jnp.concatenate(
                [
                    jnp.concatenate(singles, axis=1),
                    jnp.concatenate(doubles, axis=1),
                    jnp.zeros((14, cols), F32),
                ],
                axis=0,
            ).astype(BF)
            for yrel in (0, 1):
                out[xrel, yrel, tall : tall + 16, :] = block


def attention_grads(spot, first, gproj, att, gattn, sums):
    depth, width = first.shape
    wide, thin = gproj.shape[1] // 2, gattn.shape[1] // 2
    out = parts_of(width // 8 + 16, wide + thin)
    whole = lambda shape: pl.BlockSpec(shape, lambda i, s: (0,) * len(shape))
    half = lambda cols: pl.BlockSpec((depth, cols), lambda i, s: (0, s[3]))
    return pl.pallas_call(
        attention_kernel,
        grid_spec=pltpu.PrefetchScalarGridSpec(
            num_scalar_prefetch=1,
            grid=(1,),
            in_specs=[
                whole(first.shape), half(wide), whole(att.shape), half(thin), whole(sums.shape),
            ],
            out_specs=[whole(out.shape), whole(out.shape)],
            scratch_shapes=[pltpu.VMEM((width, wide), BF), pltpu.VMEM((width, thin), BF)],
        ),
        out_shape=[out, out],
        cost_estimate=cost_of(depth, width, wide + thin),
        compiler_params=pltpu.CompilerParams(vmem_limit_bytes=VMEM_LIMIT),
    )(spot, first, gproj, att, gattn, sums)


def xor_order(stacked, flips):
    count = stacked.shape[0]
    rest = stacked.shape[1:]
    bit = 1
    while bit < count:
        split = stacked.reshape((count // (2 * bit), 2, bit) + rest)
        split = jnp.where((flips & bit) != 0, split[:, ::-1], split)
        stacked = split.reshape((count,) + rest)
        bit *= 2
    return stacked


def label_of(section):
    return (section & ~3) | ((section & 1) << 1) | ((section >> 1) & 1)


def by_label(k, sections):
    return [(s, label_of(label_of(s) ^ k)) for s in range(sections)]


def move(array, flip_x, flip_y, flip_z, sections, dps):
    flip = flip_z * 2 + flip_y
    pairs = [
        (s * dps + d, (s ^ flip) * dps + (d ^ (flip_x * 2))) for s in range(sections) for d in range(dps)
    ]
    return lax.ppermute(array, AXES, pairs)


def over_core(give, keep, dps):
    return keep + lax.ppermute(give, "dp", [(d, d ^ 1) for d in range(dps)])


def plane_parts(both, hop):
    return [hop(both[1, 0], 1, 0, 0), hop(both[0, 1], 0, 1, 0), hop(both[1, 1], 1, 1, 0)]


def plane_sum(both, parts):
    return (both[0, 0].astype(F32) + parts[0] + parts[1] + parts[2]).astype(BF)


def all_parts(total, hop):
    return total, hop(total, 0, 1, 0), hop(total, 0, 0, 1), hop(total, 0, 1, 1)


def in_order(pieces, y, r):
    own, other_y, other_r, other_both = (p.astype(F32) for p in pieces)
    low = jnp.where(y == 0, own, other_y), jnp.where(y == 0, other_y, own)
    high = jnp.where(y == 0, other_r, other_both), jnp.where(y == 0, other_both, other_r)
    pick = lambda a, b: jnp.where(r == 0, a, b)
    return (
        (pick(low[0], high[0]), pick(low[1], high[1])),
        (pick(high[0], low[0]), pick(high[1], low[1])),
    )


def body(
    tokens, lengths, cotangent, first_gain, first_shift, qkv_weight, qv_bias, out_weight, out_bias,
    second_gain, second_shift, expand_weight, expand_bias, contract_weight, contract_bias,
):
    sections, dps = lax.axis_size("section"), lax.axis_size("dp")
    section, dp = lax.axis_index("section"), lax.axis_index("dp")
    micro, _, piece_rows, width = tokens.shape
    rows = piece_rows * sections
    ff = expand_weight.shape[1]
    label = label_of(section)

    sent = jnp.concatenate([tokens[:, 0], cotangent[:, 0]], axis=-1)
    outgoing = sent.reshape(sections // 4, 1, 2, piece_rows, 2 * width)
    outgoing = jnp.broadcast_to(outgoing, (sections // 4, 2, 2, piece_rows, 2 * width))
    outgoing = outgoing.reshape(sections, piece_rows, 2 * width)
    shard = lax.all_to_all(outgoing, "section", 0, 0, tiled=True).reshape(rows, 2 * width)
    x, cot = shard[:, :width], shard[:, width:]
    spot = jnp.stack([(dp >> 1) & 1, dp & 1, section & 1, (section >> 1) & 1, label >> 1]).astype(jnp.int32)
    first, n1, proj, probs, att, n2, second, slope, act, inv, wqot, wet, wct, last = forward_all(
        lengths[:, 0], spot, x,
        [first_gain, first_shift, qv_bias, out_bias, second_gain, second_shift, expand_bias, contract_bias],
        qkv_weight, out_weight, expand_weight, contract_weight, sections,
    )
    flat = lambda a: a.reshape(-1, a.shape[-1])
    first, att, second, act = flat(first), flat(att), flat(second), flat(act)
    known = (sections, dps) == (8, 4)
    gproj, gattn, gpre, gtok, sums, *contract = backward_all(
        spot, cot, first_gain, second_gain, wqot, wet, wct, n1, proj, probs, n2, slope, inv,
        act if known else None,
    )
    gproj, gattn, gpre = flat(gproj), flat(gattn), flat(gpre)
    both = jnp.concatenate([last, gtok], axis=1).reshape(sections, piece_rows, 2 * width)
    blocks = [
        lax.dynamic_index_in_dim(both, label_of(label ^ k), 0, keepdims=False) for k in range(0, sections, 2)
    ]
    if known:
        g_qkv, g_out, g_exp, g_con, v, back = grads_small_slice(
            section, dp, spot, first, att, second, gproj, gattn, gpre, contract, sums, blocks
        )
    else:
        half = (label & 1) == 0

        def everywhere(whole):
            whole = jnp.where(half, whole, 0.0).astype(BF)
            own = lax.psum_scatter(whole, "dp", scatter_dimension=0, tiled=True)
            return lax.psum(own, "section").astype(F32)

        g_qkv, g_out = everywhere(tn(first, gproj)), everywhere(tn(att, gattn))
        g_exp, g_con = everywhere(tn(second, gpre)), everywhere(tn(act, flat(contract[0])))
        v = [everywhere(sums[i, :n]) for i, n in enumerate([width] * 6 + [2 * width, ff])]
        back = blocks[:1] + [
            lax.ppermute(block, "section", by_label(2 * i + 2, sections)) for i, block in enumerate(blocks[1:])
        ]

    back = xor_order(jnp.stack(back), label >> 1)
    result = back[:, None, :, :width]
    grad_tokens = back[:, None, :, width:].astype(F32)
    return (
        result, grad_tokens, v[0], v[1], g_qkv, v[6], g_out, v[2], v[3], v[4], g_exp, v[7], g_con, v[5],
    )


def grads_small_slice(section, dp, spot, first, att, second, gproj, gattn, gpre, contract, sums, blocks):
    sections, dps = 8, 4
    y, r, core = section & 1, (section >> 1) & 1, dp & 1
    width, ff = first.shape[1], gpre.shape[1]
    hop = partial(move, sections=sections, dps=dps)
    cols = 2 * width
    tall = width // 8
    tie = lax.optimization_barrier
    add_a = over_core(*contract, dps)
    second, gpre, add_a = tie((second, gpre, add_a))
    from_a, out_b = plane_parts(add_a, hop), expand_grads(spot, second, gpre)
    from_a, out_b, blocks = tie((from_a, out_b, blocks))
    plane_a = plane_sum(add_a, from_a)
    z_a, add_b = hop(plane_a, 0, 0, 2), over_core(*out_b, dps)
    first, gproj, att, gattn, add_b = tie((first, gproj, att, gattn, add_b))
    from_b, out_c = plane_parts(add_b, hop), attention_grads(spot, first, gproj, att, gattn, sums)
    from_b, out_c, z_a = tie((from_b, out_c, z_a))
    plane_b, total_a = plane_sum(add_b, from_b), plane_a + z_a
    z_b = hop(jnp.concatenate([plane_b, blocks[2], blocks[3]], axis=0), 0, 0, 2)
    r_a, add_c = hop(total_a, 0, 0, 1), over_core(*out_c, dps)[:, :, : tall + 8]
    from_c = plane_parts(add_c, hop)
    from_c, z_b, r_a = tie((from_c, z_b, r_a))
    pieces = (z_b.shape[0] - tall) // 2
    z_b, from_z, through_z = z_b[:tall], z_b[tall : tall + pieces], z_b[tall + pieces :]
    plane_c, total_b = plane_sum(add_c, from_c), plane_b + z_b
    mid = tall // 2
    top, bottom = total_b[:mid], total_b[mid:]
    z_c, y_a = hop(plane_c, 0, 0, 2), hop(jnp.stack([total_a, r_a]), 0, 1, 0)
    r_top, y_bottom = hop(top, 0, 0, 1), hop(jnp.concatenate([bottom, blocks[1], through_z], axis=0), 0, 1, 0)
    z_c, y_a, r_top, y_bottom = tie((z_c, y_a, r_top, y_bottom))
    y_bottom, from_y, from_both = y_bottom[:mid], y_bottom[mid : mid + pieces], y_bottom[mid + pieces :]
    back = [blocks[0], from_y, from_z, from_both]
    rest = all_parts(plane_c + z_c, hop)
    y_top = hop(jnp.stack([top, r_top]), 0, 1, 0)
    r_bottom = hop(jnp.stack([bottom, y_bottom]), 0, 0, 1)
    con = total_a, y_a[0], r_a, y_a[1]
    con, att_part = in_order(con, y, r), in_order([p[:tall] for p in rest], y, r)
    g_con = jnp.concatenate([con[0][0], con[0][1], con[1][0], con[1][1]], axis=0)
    wide = gproj.shape[1] // 2
    side = lambda a, b: jnp.concatenate(
        [jnp.concatenate([att_part[0][j][:, a:b], att_part[1][j][:, a:b]], axis=1) for j in (0, 1)], axis=0
    )
    g_qkv, g_out, y_top, r_bottom = tie((side(0, wide), side(wide, cols), y_top, r_bottom))
    stacked = lambda a, b: jnp.concatenate([a, b], axis=0)
    exp = total_b, stacked(y_top[0], y_bottom), stacked(r_top, r_bottom[0]), stacked(y_top[1], r_bottom[1])
    exp = in_order(exp, y, r)
    g_exp = jnp.concatenate([jnp.concatenate([exp[0][j], exp[1][j]], axis=1) for j in (0, 1)], axis=0)
    g_con, vectors = tie((g_con, rest[0][tall:]))
    vectors = vectors.astype(F32)
    windows = vectors[0].reshape(6, -1)
    quarter = width // 4
    windows = jnp.where(core == 0, windows[:, :quarter], windows[:, 64 : 64 + quarter])
    v = [windows[i] for i in range(6)] + [vectors[1, : 2 * quarter], vectors[1, 2 * quarter : 2 * quarter + ff // 4]]
    return g_qkv, g_out, g_exp, g_con, v, back


def solution(mesh):
    tok = P(None, "dp", "section", None)
    return jax.shard_map(
        body,
        mesh=mesh,
        in_specs=(tok, P(None, "dp", None), tok) + (P(),) * 12,
        out_specs=(
            tok, tok, P("dp"), P("dp"), P("dp", None), P("dp"), P("dp", None), P("dp"),
            P("dp"), P("dp"), P("dp", None), P("dp"), P("dp", None), P("dp"),
        ),
        check_vma=False,
    )
```

```python
from functools import partial

import jax
import jax.numpy as jnp
from jax import lax
from jax.experimental import pallas as pl
from jax.experimental.pallas import tpu as pltpu
from jax.sharding import PartitionSpec as P

HEAD_DIM = 64
EPSILON = 1e-05
SCORE_SCALE = 0.125
MASKED = -1e30
GELU_A = 0.7978845608028654
GELU_B = 0.044715
BF = jnp.bfloat16
F32 = jnp.float32
AXES = ("section", "dp")
VMEM_LIMIT = 60 * 2**20


def nn(left, right):
    return jnp.dot(left, right, preferred_element_type=F32)


def nt(left, right):
    return lax.dot_general(left, right, (((1,), (1,)), ((), ())), preferred_element_type=F32)


def tn(left, right):
    return lax.dot_general(left, right, (((0,), (0,)), ((), ())), preferred_element_type=F32)


def normed_of(values):
    center = values - jnp.mean(values, axis=-1, keepdims=True)
    inverse = lax.rsqrt(jnp.mean(center * center, axis=-1, keepdims=True) + EPSILON)
    return center * inverse, inverse


def norm_back(upstream, normed, inverse, gain_row):
    scaled = upstream * gain_row
    return inverse * (
        scaled
        - jnp.mean(scaled, axis=-1, keepdims=True)
        - normed * jnp.mean(scaled * normed, axis=-1, keepdims=True)
    )


def row_of(ref):
    return ref[...].reshape(1, -1)


def lane_split(pair):
    lane = lax.broadcasted_iota(jnp.int32, pair.shape, 1)
    zero = jnp.zeros_like(pair)
    return jnp.where(lane < HEAD_DIM, pair, zero), jnp.where(lane < HEAD_DIM, zero, pair)


def forward_kernel(
    lens_ref, spot_ref, x_ref, g1_ref, b1_ref, qvb_ref, obias_ref, g2_ref, b2_ref, ebias_ref, cbias_ref,
    wq_hbm, wo_hbm, we_hbm, wc_hbm,
    first_ref, n1_ref, proj_ref, probs_ref, att_ref, n2_ref, second_ref, slope_ref, act_ref,
    inv_ref, wqot_ref, wet_ref, wct_ref, last_ref, h_scr, mask_scr, wqo_scr, we_ref, wc_ref, sems,
):
    step = pl.program_id(0)
    rows, width = h_scr.shape
    pairs = width // 128
    ff = we_ref.shape[1]
    loads = [
        pltpu.make_async_copy(wq_hbm, wqo_scr.at[:, 0 : 3 * width], sems.at[0]),
        pltpu.make_async_copy(wo_hbm, wqo_scr.at[:, 3 * width : 4 * width], sems.at[1]),
        pltpu.make_async_copy(we_hbm, we_ref, sems.at[2]),
        pltpu.make_async_copy(wc_hbm, wc_ref, sems.at[3]),
    ]

    @pl.when(step == 0)
    def _():
        for load in loads:
            load.start()
        h_scr[...] = x_ref[...].astype(F32)
        query = lax.broadcasted_iota(jnp.int32, (rows, rows), 0)
        key = lax.broadcasted_iota(jnp.int32, (rows, rows), 1)
        own_q = jnp.zeros((rows, rows), jnp.int32)
        own_k = jnp.zeros((rows, rows), jnp.int32)
        slots = lens_ref.shape[1]
        end = jnp.int32(0)
        for slot in range(slots):
            end = end + lens_ref[spot_ref[4], slot]
            own_q += (query >= end).astype(jnp.int32)
            own_k += (key >= end).astype(jnp.int32)
        mask_scr[...] = jnp.where((own_q == own_k) & (key <= query), 0.0, MASKED)
        loads[0].wait()
        loads[1].wait()

    strip = wqot_ref.shape[0]
    at = pl.multiple_of(jnp.minimum(step, 4 * width // strip - 1) * strip, 128)
    wqot_ref[...] = wqo_scr[:, pl.ds(at, strip)].T
    h = h_scr[...]
    n1, inv1 = normed_of(h)
    first_low = (n1 * row_of(g1_ref) + row_of(b1_ref)).astype(BF)
    first_ref[0] = first_low
    n1_ref[0] = n1.astype(BF)
    raw = nn(first_low, wqo_scr[:, 0 : 3 * width])
    queries = ((raw[:, :width] + row_of(qvb_ref)[:, :width]) * SCORE_SCALE).astype(BF)
    keys = raw[:, width : 2 * width].astype(BF)
    values = (raw[:, 2 * width :] + row_of(qvb_ref)[:, width:]).astype(BF)
    proj_ref[0, :, 0:width] = queries
    proj_ref[0, :, width : 2 * width] = keys
    proj_ref[0, :, 2 * width : 3 * width] = values
    mask = mask_scr[...]
    mask = jnp.concatenate([mask, mask], axis=0)
    cuts = [slice(128 * p, 128 * (p + 1)) for p in range(pairs)]
    scores = [nt(jnp.concatenate(lane_split(queries[:, cut]), axis=0), keys[:, cut]) + mask for cut in cuts]
    tops = [jnp.max(s, axis=-1, keepdims=True) for s in scores]
    weights = [jnp.exp(s - t) for s, t in zip(scores, tops)]
    sums = [1.0 / jnp.sum(w, axis=-1, keepdims=True) for w in weights]
    lows = [(w * t).astype(BF) for w, t in zip(weights, sums)]
    outs = []
    for p, (low, cut) in enumerate(zip(lows, cuts)):
        probs_ref[0, 2 * rows * p : 2 * rows * (p + 1), :] = low
        both = jnp.concatenate([low[:rows], low[rows:]], axis=1)
        outs.append(nn(both, jnp.concatenate(lane_split(values[:, cut]), axis=0)).astype(BF))
    attended = jnp.concatenate(outs, axis=1)
    att_ref[0] = attended
    middle = h + (nn(attended, wqo_scr[:, 3 * width : 4 * width]) + row_of(obias_ref))
    n2, inv2 = normed_of(middle)
    second_low = (n2 * row_of(g2_ref) + row_of(b2_ref)).astype(BF)
    second_ref[0] = second_low
    n2_ref[0] = n2.astype(BF)
    inv_ref[0] = jnp.concatenate(
        [jnp.broadcast_to(inv1, (rows, 128)), jnp.broadcast_to(inv2, (rows, 128))], axis=1
    )
    total = middle + row_of(cbias_ref)

    @pl.when(step == 0)
    def _():
        loads[2].wait()
        loads[3].wait()

    wet_ref[...] = we_ref[:, pl.ds(at, strip)].T
    wct_ref[...] = wc_ref[pl.ds(at, strip), :].T
    ebias = row_of(ebias_ref)
    chunk = 512
    cuts = [slice(chunk * j, chunk * (j + 1)) for j in range(ff // chunk)]
    expand = lambda cut: nn(second_low, we_ref[:, cut]) + ebias[:, cut]
    pres = [expand(cuts[0])]
    for j, cols in enumerate(cuts):
        if j + 1 < len(cuts):
            pres.append(expand(cuts[j + 1]))
        pre = pres[j]
        square = pre * pre
        half = 0.5 + 0.5 * jnp.tanh(pre * (GELU_A + GELU_A * GELU_B * square))
        act = pre * half
        slope = half + act * (1.0 - half) * (2.0 * GELU_A + 6.0 * GELU_A * GELU_B * square)
        act = act.astype(BF)
        slope_ref[0, :, cols] = slope.astype(BF)
        act_ref[0, :, cols] = act
        total = total + nn(act, wc_ref[cols, :])
    low_out = total.astype(BF)
    h_scr[...] = low_out.astype(F32)

    @pl.when(step == pl.num_programs(0) - 1)
    def _():
        last_ref[...] = low_out


def fold(values):
    return jnp.sum(values.reshape(-1, 8, values.shape[-1]), axis=0)


def backward_kernel(
    spot_ref, cot_ref, g1_ref, g2_ref, wqot_hbm, wet_hbm, wct_hbm,
    n1_ref, proj_ref, probs_ref, n2_ref, slope_ref, inv_ref, *refs, fused,
):
    if fused:
        act_hbm, refs = refs[0], refs[1:]
    gproj_ref, gattn_ref, gpre_ref, gtok_ref, sums_ref, *refs = refs
    if fused:
        give_ref, keep_ref, *refs = refs
    else:
        gmlp_ref, *refs = refs
    g_scr, s768_scr, s2304_scr, s3072_scr, wqot_ref, wet_ref, wct_ref, sems, *refs = refs
    if fused:
        act_scr, gmlp_scr, tile_scr = refs
    step = pl.program_id(0)
    rows, width = g_scr.shape
    pairs = width // 128
    ff = wct_ref.shape[1]

    loads = [
        pltpu.make_async_copy(wct_hbm, wct_ref, sems.at[0]),
        pltpu.make_async_copy(wet_hbm, wet_ref, sems.at[1]),
        pltpu.make_async_copy(wqot_hbm, wqot_ref, sems.at[2]),
    ]

    if fused:
        x, c, r = spot_ref[0], spot_ref[1], spot_ref[3]
        tall = act_scr.shape[1] // 4
        for i in range(4):
            block = (((i & 1) ^ x) * 2 + ((1 - (i >> 1)) ^ c)) * 2 + r
            source = act_hbm.at[:, pl.ds(pl.multiple_of(block * tall, 128), tall)]
            loads.append(pltpu.make_async_copy(source, act_scr.at[:, tall * i : tall * (i + 1)], sems.at[3 + i]))

    @pl.when(step == 0)
    def _():
        for load in loads:
            load.start()
        g_scr[...] = cot_ref[...].astype(F32)
        s768_scr[...] = jnp.zeros_like(s768_scr)
        s2304_scr[...] = jnp.zeros_like(s2304_scr)
        s3072_scr[...] = jnp.zeros_like(s3072_scr)
        loads[0].wait()
        loads[1].wait()

    g = g_scr[...]
    gmlp = g.astype(BF)
    if fused:
        layer = pl.num_programs(0) - 1 - step
        gmlp_scr[pl.ds(pl.multiple_of(layer * rows, rows), rows), :] = gmlp
    else:
        gmlp_ref[0] = gmlp
    gsec = jnp.zeros((rows, width), F32)
    chunk = 1024
    for j in range(ff // chunk):
        cols = slice(chunk * j, chunk * (j + 1))
        gpre = (nn(gmlp, wct_ref[:, cols]) * slope_ref[0, :, cols].astype(F32)).astype(BF)
        gpre_ref[0, :, cols] = gpre
        s3072_scr[:, cols] += fold(gpre.astype(F32))
        gsec = gsec + nn(gpre, wet_ref[cols, :])
    n2 = n2_ref[0].astype(F32)
    gmid = g + norm_back(gsec, n2, inv_ref[0, :, 128:129], row_of(g2_ref))
    gattn = gmid.astype(BF)
    gattn_ref[0] = gattn

    @pl.when(step == 0)
    def _():
        loads[2].wait()

    gatt = nn(gattn, wqot_ref[3 * width : 4 * width, :]).astype(BF)
    dqs, dks, dvs = [], [], []
    outs2, gprobs = [], []
    for p in range(pairs):
        v = proj_ref[0, :, 2 * width + 128 * p : 2 * width + 128 * (p + 1)]
        out2 = jnp.concatenate(lane_split(gatt[:, 128 * p : 128 * (p + 1)]), axis=0)
        outs2.append(out2)
        gprobs.append(nt(out2, v))
    gscores = []
    for p in range(pairs):
        prob = probs_ref[0, 2 * rows * p : 2 * rows * (p + 1), :].astype(F32)
        gs = prob * (gprobs[p] - jnp.sum(prob * gprobs[p], axis=-1, keepdims=True))
        gscores.append(gs.astype(BF))
    for p in range(pairs):
        q = proj_ref[0, :, 128 * p : 128 * (p + 1)]
        k = proj_ref[0, :, width + 128 * p : width + 128 * (p + 1)]
        gscore = gscores[p]
        low = probs_ref[0, 2 * rows * p : 2 * rows * (p + 1), :]
        both = jnp.concatenate([gscore[:rows], gscore[rows:]], axis=1)
        k2 = jnp.concatenate(lane_split(k), axis=0)
        q2 = jnp.concatenate(lane_split(q), axis=0)
        dqs.append((nn(both, k2) * SCORE_SCALE).astype(BF))
        kv = tn(jnp.concatenate([gscore, low], axis=1), jnp.concatenate([q2, outs2[p]], axis=1))
        dks.append(kv[:rows, :128].astype(BF))
        dvs.append(kv[rows:, 128:].astype(BF))
    gproj = jnp.concatenate(dqs + dks + dvs, axis=1)
    gproj_ref[0] = gproj
    gfirst = nn(gproj, wqot_ref[0 : 3 * width, :])
    n1 = n1_ref[0].astype(F32)
    gin = gmid + norm_back(gfirst, n1, inv_ref[0, :, 0:1], row_of(g1_ref))
    s768_scr[0] += fold(gfirst * n1)
    s768_scr[1] += fold(gfirst)
    s768_scr[2] += fold(gattn.astype(F32))
    s768_scr[3] += fold(gsec * n2)
    s768_scr[4] += fold(gsec)
    s768_scr[5] += fold(gmlp.astype(F32))
    s2304_scr[...] += fold(gproj.astype(F32))
    low_out = gin.astype(BF)
    g_scr[...] = low_out.astype(F32)

    @pl.when(step == pl.num_programs(0) - 1)
    def _():
        gtok_ref[...] = low_out
        row = lambda v: jnp.sum(v, axis=0, keepdims=True)
        for i in range(6):
            sums_ref[i : i + 1, 0:width] = row(s768_scr[i])
        sums_ref[6:7, 0:width] = row(s2304_scr[:, 0:width])
        sums_ref[6:7, width : 2 * width] = row(s2304_scr[:, 2 * width : 3 * width])
        sums_ref[7:8, :] = row(s3072_scr[...])
        if fused:
            y = spot_ref[2]
            for load in loads[3:]:
                load.wait()
            for out, at in ((give_ref, 0), (keep_ref, 2 * tall)):
                tile_scr[...] = tn(act_scr[:, at : at + 2 * tall], gmlp_scr[...]).astype(BF)
                for xrel in (0, 1):
                    for yrel in (0, 1):
                        start = pl.multiple_of(xrel * tall + (y ^ yrel) * (tall // 2), 16)
                        out[xrel, yrel] = tile_scr[pl.ds(start, tall // 2), :]


def whole_spec(shape):
    zeros = (0,) * len(shape)
    return pl.BlockSpec(shape, lambda i, *_: zeros, pipeline_mode=pl.Buffered(1))


def forward_all(lens, spot, x, rows_in, wq, wo, we, wc, layers):
    rows, width = x.shape
    ff = we.shape[1]
    pairs = width // 128
    strip = ff // 8
    stack = lambda cols, r=rows, t=BF: jax.ShapeDtypeStruct((layers, r, cols), t)
    outs = [
        stack(width), stack(width), stack(3 * width), stack(rows, 2 * rows * pairs), stack(width),
        stack(width), stack(width), stack(ff), stack(ff), stack(256, rows, F32),
    ]
    per_layer = lambda s: pl.BlockSpec((1,) + s.shape[1:], lambda i, *_: (i, 0, 0))
    turned = [jax.ShapeDtypeStruct(s, BF) for s in ((4 * width, width), (ff, width), (width, ff))]
    by_rows = pl.BlockSpec((strip, width), lambda i, *_: (jnp.minimum(i, 7), 0))
    by_cols = pl.BlockSpec((width, strip), lambda i, *_: (0, jnp.minimum(i, 7)))
    last = jax.ShapeDtypeStruct((rows, width), BF)
    return pl.pallas_call(
        forward_kernel,
        grid_spec=pltpu.PrefetchScalarGridSpec(
            num_scalar_prefetch=2,
            grid=(layers,),
            in_specs=[whole_spec(a.shape) for a in (x, *rows_in)]
            + [pl.BlockSpec(memory_space=pl.ANY)] * 4,
            out_specs=[per_layer(s) for s in outs] + [by_rows, by_rows, by_cols, whole_spec(last.shape)],
            scratch_shapes=[
                pltpu.VMEM((rows, width), F32),
                pltpu.VMEM((rows, rows), F32),
                pltpu.VMEM((width, 4 * width), BF),
                pltpu.VMEM((width, ff), BF),
                pltpu.VMEM((ff, width), BF),
                pltpu.SemaphoreType.DMA((4,)),
            ],
        ),
        out_shape=outs + turned + [last],
        compiler_params=pltpu.CompilerParams(vmem_limit_bytes=VMEM_LIMIT),
    )(lens, spot, x, *rows_in, wq, wo, we, wc)


def backward_all(spot, cot, g1, g2, wqot, wet, wct, n1, proj, probs, n2, slope, inv, act=None):
    layers, rows, width = n1.shape
    ff = wct.shape[1]
    fused = act is not None
    stack = lambda cols: jax.ShapeDtypeStruct((layers, rows, cols), BF)
    outs = [stack(3 * width), stack(width), stack(ff)]
    per_layer = lambda s: pl.BlockSpec((1,) + s.shape[1:], lambda i, *_: (layers - 1 - i, 0, 0))
    last = [jax.ShapeDtypeStruct((rows, width), BF), jax.ShapeDtypeStruct((8, ff), F32)]
    out_specs = [per_layer(s) for s in outs] + [whole_spec(s.shape) for s in last]
    more_in, more_scratch = [], []
    if fused:
        more_in = [act]
        last += [parts_of(ff // 16, width)] * 2
        out_specs += [whole_spec(last[-1].shape)] * 2
        more_scratch = [
            pltpu.VMEM((layers * rows, ff // 2), BF),
            pltpu.VMEM((layers * rows, width), BF),
            pltpu.VMEM((ff // 4, width), BF),
        ]
    else:
        last.append(stack(width))
        out_specs.append(per_layer(last[-1]))
    return pl.pallas_call(
        partial(backward_kernel, fused=fused),
        grid_spec=pltpu.PrefetchScalarGridSpec(
            num_scalar_prefetch=1,
            grid=(layers,),
            in_specs=[whole_spec(a.shape) for a in (cot, g1, g2)]
            + [pl.BlockSpec(memory_space=pl.ANY)] * 3
            + [per_layer(a) for a in (n1, proj, probs, n2, slope, inv)]
            + [pl.BlockSpec(memory_space=pl.ANY)] * len(more_in),
            out_specs=out_specs,
            scratch_shapes=[
                pltpu.VMEM((rows, width), F32),
                pltpu.VMEM((6, 8, width), F32),
                pltpu.VMEM((8, 3 * width), F32),
                pltpu.VMEM((8, ff), F32),
                pltpu.VMEM((4 * width, width), BF),
                pltpu.VMEM((ff, width), BF),
                pltpu.VMEM((width, ff), BF),
                pltpu.SemaphoreType.DMA((7,)),
            ]
            + more_scratch,
        ),
        out_shape=outs + last,
        compiler_params=pltpu.CompilerParams(vmem_limit_bytes=VMEM_LIMIT),
    )(spot, cot, g1, g2, wqot, wet, wct, n1, proj, probs, n2, slope, inv, *more_in)


def outer_kernel(spot_ref, left_ref, right_ref, give_ref, keep_ref, scr, *, tall):
    scr[...] = tn(left_ref[...], right_ref[...]).astype(BF)
    split_out(spot_ref, scr, give_ref, keep_ref, 0, scr.shape[1], tall)


def split_out(spot_ref, scr, give_ref, keep_ref, at, cols, tall):
    x, c, y = spot_ref[0], spot_ref[1], spot_ref[2]
    for crel in (1, 0):
        out = give_ref if crel else keep_ref
        for xrel in (0, 1):
            for yrel in (0, 1):
                part = ((x ^ xrel) * 2 + (c ^ crel)) * 2 + (y ^ yrel)
                start = pl.multiple_of(part * tall, tall)
                out[xrel, yrel, 0:tall, at : at + cols] = scr[pl.ds(start, tall), :]


def parts_of(rows, cols):
    return jax.ShapeDtypeStruct((2, 2, rows, cols), BF)


def expand_grads(spot, left, right, tile=768):
    depth, width = left.shape
    half = right.shape[1] // 2
    steps = half // tile
    out = parts_of(width // 8, half)
    out_spec = pl.BlockSpec((2, 2, width // 8, tile), lambda j, s: (0, 0, 0, j))
    return pl.pallas_call(
        partial(outer_kernel, tall=width // 8),
        grid_spec=pltpu.PrefetchScalarGridSpec(
            num_scalar_prefetch=1,
            grid=(steps,),
            in_specs=[
                pl.BlockSpec((depth, width), lambda j, s: (0, 0)),
                pl.BlockSpec((depth, tile), lambda j, s: (0, s[3] * steps + j)),
            ],
            out_specs=[out_spec, out_spec],
            scratch_shapes=[pltpu.VMEM((width, tile), BF)],
        ),
        out_shape=[out, out],
        cost_estimate=cost_of(depth, width, half),
        compiler_params=pltpu.CompilerParams(vmem_limit_bytes=VMEM_LIMIT),
    )(spot, left, right)


def cost_of(depth, rows, cols):
    return pl.CostEstimate(
        flops=2 * depth * rows * cols, transcendentals=0, bytes_accessed=2 * depth * (rows + cols) + 2 * rows * cols
    )


def attention_kernel(
    spot_ref, first_ref, gproj_ref, att_ref, gattn_ref, sums_ref, give_ref, keep_ref, qkv_scr, out_scr,
):
    tall = qkv_scr.shape[0] // 8
    wide = qkv_scr.shape[1]
    qkv_scr[...] = tn(first_ref[...], gproj_ref[...]).astype(BF)
    split_out(spot_ref, qkv_scr, give_ref, keep_ref, 0, wide, tall)
    out_scr[...] = tn(att_ref[...], gattn_ref[...]).astype(BF)
    split_out(spot_ref, out_scr, give_ref, keep_ref, wide, out_scr.shape[1], tall)
    x, c = spot_ref[0], spot_ref[1]
    width, cols = qkv_scr.shape[0], give_ref.shape[3]
    for crel, out in ((1, give_ref), (0, keep_ref)):
        for xrel in (0, 1):
            place = (x ^ xrel) * 2 + (c ^ crel)
            window = lambda i, start, size: sums_ref[i : i + 1, pl.ds(pl.multiple_of(start, 128), size)]
            low = ((place * 3) >> 1) * 128
            singles = [window(i, low, 256) for i in range(6)]
            doubles = [window(6, place * (width // 2), width // 2), window(7, place * width, width)]
            used = (width // 2) * 3
            doubles.append(jnp.zeros((1, cols - used), F32))
            block = jnp.concatenate(
                [
                    jnp.concatenate(singles, axis=1),
                    jnp.concatenate(doubles, axis=1),
                    jnp.zeros((14, cols), F32),
                ],
                axis=0,
            ).astype(BF)
            for yrel in (0, 1):
                out[xrel, yrel, tall : tall + 16, :] = block


def attention_grads(spot, first, gproj, att, gattn, sums):
    depth, width = first.shape
    wide, thin = gproj.shape[1] // 2, gattn.shape[1] // 2
    out = parts_of(width // 8 + 16, wide + thin)
    whole = lambda shape: pl.BlockSpec(shape, lambda i, s: (0,) * len(shape))
    half = lambda cols: pl.BlockSpec((depth, cols), lambda i, s: (0, s[3]))
    return pl.pallas_call(
        attention_kernel,
        grid_spec=pltpu.PrefetchScalarGridSpec(
            num_scalar_prefetch=1,
            grid=(1,),
            in_specs=[
                whole(first.shape), half(wide), whole(att.shape), half(thin), whole(sums.shape),
            ],
            out_specs=[whole(out.shape), whole(out.shape)],
            scratch_shapes=[pltpu.VMEM((width, wide), BF), pltpu.VMEM((width, thin), BF)],
        ),
        out_shape=[out, out],
        cost_estimate=cost_of(depth, width, wide + thin),
        compiler_params=pltpu.CompilerParams(vmem_limit_bytes=VMEM_LIMIT),
    )(spot, first, gproj, att, gattn, sums)


def xor_order(stacked, flips):
    count = stacked.shape[0]
    rest = stacked.shape[1:]
    bit = 1
    while bit < count:
        split = stacked.reshape((count // (2 * bit), 2, bit) + rest)
        split = jnp.where((flips & bit) != 0, split[:, ::-1], split)
        stacked = split.reshape((count,) + rest)
        bit *= 2
    return stacked


def label_of(section):
    return (section & ~3) | ((section & 1) << 1) | ((section >> 1) & 1)


def by_label(k, sections):
    return [(s, label_of(label_of(s) ^ k)) for s in range(sections)]


def move(array, flip_x, flip_y, flip_z, sections, dps):
    flip = flip_z * 2 + flip_y
    pairs = [
        (s * dps + d, (s ^ flip) * dps + (d ^ (flip_x * 2))) for s in range(sections) for d in range(dps)
    ]
    return lax.ppermute(array, AXES, pairs)


def over_core(give, keep, dps):
    return keep + lax.ppermute(give, "dp", [(d, d ^ 1) for d in range(dps)])


def plane_parts(both, hop):
    return [hop(both[1, 0], 1, 0, 0), hop(both[0, 1], 0, 1, 0), hop(both[1, 1], 1, 1, 0)]


def plane_sum(both, parts):
    return (both[0, 0].astype(F32) + parts[0] + parts[1] + parts[2]).astype(BF)


def all_parts(total, hop):
    return total, hop(total, 0, 1, 0), hop(total, 0, 0, 1), hop(total, 0, 1, 1)


def in_order(pieces, y, r):
    own, other_y, other_r, other_both = (p.astype(F32) for p in pieces)
    low = jnp.where(y == 0, own, other_y), jnp.where(y == 0, other_y, own)
    high = jnp.where(y == 0, other_r, other_both), jnp.where(y == 0, other_both, other_r)
    pick = lambda a, b: jnp.where(r == 0, a, b)
    return (
        (pick(low[0], high[0]), pick(low[1], high[1])),
        (pick(high[0], low[0]), pick(high[1], low[1])),
    )


def body(
    tokens, lengths, cotangent, first_gain, first_shift, qkv_weight, qv_bias, out_weight, out_bias,
    second_gain, second_shift, expand_weight, expand_bias, contract_weight, contract_bias,
):
    sections, dps = lax.axis_size("section"), lax.axis_size("dp")
    section, dp = lax.axis_index("section"), lax.axis_index("dp")
    micro, _, piece_rows, width = tokens.shape
    rows = piece_rows * sections
    ff = expand_weight.shape[1]
    label = label_of(section)

    sent = jnp.concatenate([tokens[:, 0], cotangent[:, 0]], axis=-1)
    outgoing = sent.reshape(sections // 4, 1, 2, piece_rows, 2 * width)
    outgoing = jnp.broadcast_to(outgoing, (sections // 4, 2, 2, piece_rows, 2 * width))
    outgoing = outgoing.reshape(sections, piece_rows, 2 * width)
    shard = lax.all_to_all(outgoing, "section", 0, 0, tiled=True).reshape(rows, 2 * width)
    x, cot = shard[:, :width], shard[:, width:]
    spot = jnp.stack([(dp >> 1) & 1, dp & 1, section & 1, (section >> 1) & 1, label >> 1]).astype(jnp.int32)
    first, n1, proj, probs, att, n2, second, slope, act, inv, wqot, wet, wct, last = forward_all(
        lengths[:, 0], spot, x,
        [first_gain, first_shift, qv_bias, out_bias, second_gain, second_shift, expand_bias, contract_bias],
        qkv_weight, out_weight, expand_weight, contract_weight, sections,
    )
    flat = lambda a: a.reshape(-1, a.shape[-1])
    first, att, second, act = flat(first), flat(att), flat(second), flat(act)
    known = (sections, dps) == (8, 4)
    gproj, gattn, gpre, gtok, sums, *contract = backward_all(
        spot, cot, first_gain, second_gain, wqot, wet, wct, n1, proj, probs, n2, slope, inv,
        act if known else None,
    )
    gproj, gattn, gpre = flat(gproj), flat(gattn), flat(gpre)
    both = jnp.concatenate([last, gtok], axis=1).reshape(sections, piece_rows, 2 * width)
    blocks = [
        lax.dynamic_index_in_dim(both, label_of(label ^ k), 0, keepdims=False) for k in range(0, sections, 2)
    ]
    if known:
        g_qkv, g_out, g_exp, g_con, v, back = grads_small_slice(
            section, dp, spot, first, att, second, gproj, gattn, gpre, contract, sums, blocks
        )
    else:
        half = (label & 1) == 0

        def everywhere(whole):
            whole = jnp.where(half, whole, 0.0).astype(BF)
            own = lax.psum_scatter(whole, "dp", scatter_dimension=0, tiled=True)
            return lax.psum(own, "section").astype(F32)

        g_qkv, g_out = everywhere(tn(first, gproj)), everywhere(tn(att, gattn))
        g_exp, g_con = everywhere(tn(second, gpre)), everywhere(tn(act, flat(contract[0])))
        v = [everywhere(sums[i, :n]) for i, n in enumerate([width] * 6 + [2 * width, ff])]
        back = blocks[:1] + [
            lax.ppermute(block, "section", by_label(2 * i + 2, sections)) for i, block in enumerate(blocks[1:])
        ]

    back = xor_order(jnp.stack(back), label >> 1)
    result = back[:, None, :, :width]
    grad_tokens = back[:, None, :, width:].astype(F32)
    return (
        result, grad_tokens, v[0], v[1], g_qkv, v[6], g_out, v[2], v[3], v[4], g_exp, v[7], g_con, v[5],
    )


def grads_small_slice(section, dp, spot, first, att, second, gproj, gattn, gpre, contract, sums, blocks):
    sections, dps = 8, 4
    y, r, core = section & 1, (section >> 1) & 1, dp & 1
    width, ff = first.shape[1], gpre.shape[1]
    hop = partial(move, sections=sections, dps=dps)
    cols = 2 * width
    tall = width // 8
    tie = lax.optimization_barrier
    add_a = over_core(*contract, dps)
    second, gpre, add_a = tie((second, gpre, add_a))
    from_a, out_b = plane_parts(add_a, hop), expand_grads(spot, second, gpre)
    from_a, out_b, blocks = tie((from_a, out_b, blocks))
    plane_a = plane_sum(add_a, from_a)
    z_a, add_b = hop(plane_a, 0, 0, 2), over_core(*out_b, dps)
    first, gproj, att, gattn, add_b = tie((first, gproj, att, gattn, add_b))
    from_b, out_c = plane_parts(add_b, hop), attention_grads(spot, first, gproj, att, gattn, sums)
    from_b, out_c, z_a = tie((from_b, out_c, z_a))
    plane_b, total_a = plane_sum(add_b, from_b), plane_a + z_a
    z_b = hop(jnp.concatenate([plane_b, blocks[2], blocks[3]], axis=0), 0, 0, 2)
    r_a, add_c = hop(total_a, 0, 0, 1), over_core(*out_c, dps)[:, :, : tall + 8]
    from_c = plane_parts(add_c, hop)
    from_c, z_b, r_a = tie((from_c, z_b, r_a))
    pieces = (z_b.shape[0] - tall) // 2
    z_b, from_z, through_z = z_b[:tall], z_b[tall : tall + pieces], z_b[tall + pieces :]
    plane_c, total_b = plane_sum(add_c, from_c), plane_b + z_b
    mid = tall // 2
    top, bottom = total_b[:mid], total_b[mid:]
    z_c, y_a = hop(plane_c, 0, 0, 2), hop(jnp.stack([total_a, r_a]), 0, 1, 0)
    r_top, y_bottom = hop(top, 0, 0, 1), hop(jnp.concatenate([bottom, blocks[1], through_z], axis=0), 0, 1, 0)
    z_c, y_a, r_top, y_bottom = tie((z_c, y_a, r_top, y_bottom))
    y_bottom, from_y, from_both = y_bottom[:mid], y_bottom[mid : mid + pieces], y_bottom[mid + pieces :]
    back = [blocks[0], from_y, from_z, from_both]
    rest = all_parts(plane_c + z_c, hop)
    y_top = hop(jnp.stack([top, r_top]), 0, 1, 0)
    r_bottom = hop(jnp.stack([bottom, y_bottom]), 0, 0, 1)
    con = total_a, y_a[0], r_a, y_a[1]
    con, att_part = in_order(con, y, r), in_order([p[:tall] for p in rest], y, r)
    g_con = jnp.concatenate([con[0][0], con[0][1], con[1][0], con[1][1]], axis=0)
    wide = gproj.shape[1] // 2
    side = lambda a, b: jnp.concatenate(
        [jnp.concatenate([att_part[0][j][:, a:b], att_part[1][j][:, a:b]], axis=1) for j in (0, 1)], axis=0
    )
    g_qkv, g_out, y_top, r_bottom = tie((side(0, wide), side(wide, cols), y_top, r_bottom))
    stacked = lambda a, b: jnp.concatenate([a, b], axis=0)
    exp = total_b, stacked(y_top[0], y_bottom), stacked(r_top, r_bottom[0]), stacked(y_top[1], r_bottom[1])
    exp = in_order(exp, y, r)
    g_exp = jnp.concatenate([jnp.concatenate([exp[0][j], exp[1][j]], axis=1) for j in (0, 1)], axis=0)
    g_con, vectors = tie((g_con, rest[0][tall:]))
    vectors = vectors.astype(F32)
    windows = vectors[0].reshape(6, -1)
    quarter = width // 4
    windows = jnp.where(core == 0, windows[:, :quarter], windows[:, 64 : 64 + quarter])
    v = [windows[i] for i in range(6)] + [vectors[1, : 2 * quarter], vectors[1, 2 * quarter : 2 * quarter + ff // 4]]
    return g_qkv, g_out, g_exp, g_con, v, back


def solution(mesh):
    tok = P(None, "dp", "section", None)
    return jax.shard_map(
        body,
        mesh=mesh,
        in_specs=(tok, P(None, "dp", None), tok) + (P(),) * 12,
        out_specs=(
            tok, tok, P("dp"), P("dp"), P("dp", None), P("dp"), P("dp", None), P("dp"),
            P("dp"), P("dp"), P("dp", None), P("dp"), P("dp", None), P("dp"),
        ),
        check_vma=False,
    )
```
